32 devices in a mesh: brick: 8 (over z, x), chan: 4 (over y, core).
Axes of the slice: x: 2, y: 2, z: 4, core: 2. Of those that a mesh axis runs over, the one named last changes fastest.
Arguments:
- features: bfloat16 [32, 128, 512], P('brick', 'chan'), may hold values from -6 to 6
- fine_links: int32 [32, 26], P('brick'), may hold values from -1 to 31, as said below
- coarse_links: int32 [16, 26], P('brick'), may hold values from -1 to 15, as said below
- parents: int32 [32], P('brick'), may hold values from 0 to 127, as said below
- down_weight: bfloat16 [8, 128, 128], P(None, None, 'chan'), may hold values from -0.1875 to 0.1875
- coarse_weight: bfloat16 [27, 128, 128], P(None, 'chan'), may hold values from -0.109375 to 0.109375
- up_weight: bfloat16 [8, 128, 128], P(None, 'chan'), may hold values from -0.5 to 0.5
- fine_weight: bfloat16 [27, 128, 128], P(None, 'chan'), may hold values from -0.109375 to 0.109375
- coarse_bias: float32 [128], P('chan'), may hold values from -3 to 3
- fine_bias: float32 [128], P('chan'), may hold values from -3 to 3
Outputs:
- refined: bfloat16 [32, 128, 512], P('brick', 'chan')
The draws below stay inside these ranges and needn't reach their ends.
Inputs may be any that keep to these rules, and one draw needn't show every extreme that they name: `fine_links`: A fine brick's index is its owner times 4 plus its place there; the owner of fine brick b is b // 4. Among the rows of one owner's bricks, at most 3 of the entries in columns 0 to 5 name bricks of any one owner, and at most 10 of the entries in columns 6 to 25 do. `coarse_links`: A coarse brick's index is its owner times 2 plus its place there. Among the rows of one owner's coarse bricks, at most 2 of the entries in columns 0 to 5 name coarse bricks of any one owner, and at most 5 of the entries in columns 6 to 25 do. parents[b] // 8 is a coarse brick; at most 1 of one owner's fine bricks have parents on any one owner.
All inputs are finite; a program needn't handle non-finite values.
Results may differ from the reference program's by a relative error of at most 0.0059.
Values may be sent and summed in bfloat16 or wider, within the bound.
No kernel may reach another device: no remote copies, remote signals or barrier semaphores. Data moves between devices by JAX's collectives and lax.ppermute only.
A program may use at most 64 MiB of HBM per device.

```python
import jax
import jax.numpy as jnp
from jax import lax

C = 128
EDGE = 8
BR_DEV = 4
CBR_DEV = 2
BRICKS = 32
N_BRICK = 8


def owner_table(seed_key, item_total, owner_total, sparse):
    capacity = -(-item_total // owner_total)
    hot_owner = jax.random.randint(jax.random.fold_in(seed_key, 7), (), 0, owner_total)

    def one_device(device):
        local_key = jax.random.fold_in(seed_key, 100 + device)
        ranking = jax.random.permutation(jax.random.fold_in(local_key, 1), item_total).astype(jnp.int32)
        groups = ranking // capacity
        shuffled = jax.random.permutation(jax.random.fold_in(local_key, 2), owner_total - 1).astype(jnp.int32)
        offsets = jnp.concatenate([jnp.zeros((1,), jnp.int32), 1 + shuffled])
        target = (hot_owner + offsets[groups]) % owner_total
        coin_flip = jax.random.randint(jax.random.fold_in(local_key, 3), (item_total,), 0, 8)
        return jnp.where((groups == 0) | (coin_flip < sparse), target, -1).astype(jnp.int32)
    return jax.vmap(one_device)(jnp.arange(owner_total, dtype=jnp.int32))


def linked(seed_key, per_owner):
    face_owner = owner_table(jax.random.fold_in(seed_key, 1), 6 * per_owner, N_BRICK, 7)
    rim_owner = owner_table(jax.random.fold_in(seed_key, 2), 20 * per_owner, N_BRICK, 7)
    face_slot = jax.random.randint(jax.random.fold_in(seed_key, 3), face_owner.shape, 0, per_owner)
    rim_slot = jax.random.randint(jax.random.fold_in(seed_key, 4), rim_owner.shape, 0, per_owner)
    face_ids = jnp.where(face_owner >= 0, face_owner * per_owner + face_slot, -1).reshape(N_BRICK, per_owner, 6)
    rim_ids = jnp.where(rim_owner >= 0, rim_owner * per_owner + rim_slot, -1).reshape(N_BRICK, per_owner, 20)
    return jnp.concatenate([face_ids, rim_ids], axis=2).reshape(N_BRICK * per_owner, 26).astype(jnp.int32)


def draw_fine_links(key, part):
    return linked(jax.random.fold_in(key, 11), BR_DEV)


def draw_coarse_links(key, part):
    return linked(jax.random.fold_in(key, 12), CBR_DEV)


def draw_parents(key, part):
    seed_key = jax.random.fold_in(key, 13)
    owners = owner_table(jax.random.fold_in(seed_key, 1), BR_DEV, N_BRICK, 8)
    slot_draw = jax.random.randint(jax.random.fold_in(seed_key, 2), owners.shape, 0, CBR_DEV)
    octant = jax.random.randint(jax.random.fold_in(seed_key, 3), owners.shape, 0, 8)
    return ((owners * CBR_DEV + slot_draw) * 8 + octant).reshape(-1).astype(jnp.int32)


def level_of(stream_key, dims, cuts, least, high):
    def one(position, blocks):
        heights = jax.random.uniform(jax.random.fold_in(jax.random.fold_in(stream_key, 6), position), (blocks,), jnp.float32, least / len(cuts), high / len(cuts))
        return jnp.repeat(jnp.exp(heights), dims[position] // blocks).reshape((-1,) + (1,) * (len(dims) - position - 1))

    level = one(*cuts[0])
    for cut in cuts[1:]:
        level = level * one(*cut)
    return level


def scatter_about(rng, shape, spread, limit, shards=(), kind=jnp.bfloat16):
    level = level_of(rng, shape, shards, -0.22, 0.18) if shards else 1.0
    drawn = jax.random.normal(rng, shape, jnp.float32) * spread * level
    return jnp.minimum(jnp.maximum(drawn, -limit), limit).astype(kind)


def setup_inputs(seed: int = 0) -> dict:
    keys = jax.random.split(jax.random.key(seed), 11)
    features = scatter_about(keys[0], (BRICKS, C, EDGE ** 3), 1.0, 6.0, ((0, 8), (1, 4)))
    fine_links = draw_fine_links(jax.random.fold_in(keys[10], 71), 0)
    coarse_links = draw_coarse_links(jax.random.fold_in(keys[10], 71), 0)
    parents = draw_parents(jax.random.fold_in(keys[10], 71), 0)
    down_weight = scatter_about(keys[4], (8, C, C), (8 * C) ** -0.5, 0.1875, ((2, 4),))
    coarse_weight = scatter_about(keys[5], (27, C, C), (27 * C) ** -0.5, 0.109375, ((1, 4),))
    up_weight = scatter_about(keys[6], (8, C, C), C ** -0.5, 0.5, ((1, 4),))
    fine_weight = scatter_about(keys[7], (27, C, C), (27 * C) ** -0.5, 0.109375, ((1, 4),))
    coarse_bias = scatter_about(keys[8], (C,), 0.5, 3.0, ((0, 4),), jnp.float32)
    fine_bias = scatter_about(keys[9], (C,), 0.5, 3.0, ((0, 4),), jnp.float32)
    return dict(features=features, fine_links=fine_links, coarse_links=coarse_links, parents=parents, down_weight=down_weight, coarse_weight=coarse_weight, up_weight=up_weight, fine_weight=fine_weight, coarse_bias=coarse_bias, fine_bias=fine_bias)


def headings():
    face_steps = [(1, 0, 0), (-1, 0, 0), (0, 1, 0), (0, -1, 0), (0, 0, 1), (0, 0, -1)]
    others = []
    for step_x in (-1, 0, 1):
        for step_y in (-1, 0, 1):
            for step_z in (-1, 0, 1):
                if abs(step_x) + abs(step_y) + abs(step_z) >= 2:
                    others.append((step_x, step_y, step_z))
    return face_steps + others


def source_span(edge_cells, heading):
    return [(0, 1) if along == 1 else ((edge_cells - 1, edge_cells) if along == -1 else (0, edge_cells)) for along in heading]


def target_span(edge_cells, heading):
    return [(edge_cells + 1, edge_cells + 2) if along == 1 else ((0, 1) if along == -1 else (1, edge_cells + 1)) for along in heading]


def outer_pieces(blocks):
    edge_cells = blocks.shape[-1]
    face_list = []
    rim_list = []
    for number, heading in enumerate(headings()):
        bounds = source_span(edge_cells, heading)
        section = blocks[:, :, bounds[0][0]:bounds[0][1], bounds[1][0]:bounds[1][1], bounds[2][0]:bounds[2][1]]
        section = section.reshape(blocks.shape[0], blocks.shape[1], -1)
        if number < 6:
            face_list.append(section)
        else:
            rim_list.append(jnp.pad(section, ((0, 0), (0, 0), (0, edge_cells - section.shape[2]))))
    return jnp.stack(face_list, 1), jnp.stack(rim_list, 1)


def framed(centre, face_rows, rim_rows):
    edge_cells = centre.shape[-1]
    padded = jnp.pad(centre, ((0, 0), (0, 0), (1, 1), (1, 1), (1, 1)))
    for number, heading in enumerate(headings()):
        bounds = target_span(edge_cells, heading)
        extent = [limits[1] - limits[0] for limits in bounds]
        volume = extent[0] * extent[1] * extent[2]
        section = face_rows[:, number] if number < 6 else rim_rows[:, number - 6]
        section = section[:, :, :volume].reshape((centre.shape[0], centre.shape[1], extent[0], extent[1], extent[2]))
        padded = padded.at[:, :, bounds[0][0]:bounds[0][1], bounds[1][0]:bounds[1][1], bounds[2][0]:bounds[2][1]].set(section)
    return padded


def level_conv(field_rows, neighbours, weight, biases, group_size):
    brick_total, channels = field_rows.shape[0], field_rows.shape[1]
    blocks = field_rows.reshape(brick_total, channels, EDGE, EDGE, EDGE)
    face_all, rim_all = outer_pieces(blocks)
    kernel = jnp.transpose(weight, (1, 2, 0)).reshape(channels, channels, 3, 3, 3).astype(jnp.float32)

    def one_group(packed):
        centre, links_here = packed
        clipped = jnp.maximum(links_here, 0)
        present = links_here >= 0
        face_rows = face_all[clipped[:, :6], jnp.arange(6, dtype=jnp.int32)[None, :]]
        face_rows = jnp.where(present[:, :6, None, None], face_rows, jnp.zeros_like(face_rows))
        rim_rows = rim_all[clipped[:, 6:], jnp.arange(20, dtype=jnp.int32)[None, :]]
        rim_rows = jnp.where(present[:, 6:, None, None], rim_rows, jnp.zeros_like(rim_rows))
        padded = framed(centre, face_rows, rim_rows).astype(jnp.float32)
        result = lax.conv_general_dilated(padded, kernel, (1, 1, 1), "VALID", dimension_numbers=("NCDHW", "OIDHW", "NCDHW"), precision=lax.Precision.HIGHEST)
        return jnp.maximum(result + biases[None, :, None, None, None], 0.0).astype(jnp.bfloat16)

    grouped = (blocks.reshape(brick_total // group_size, group_size, channels, EDGE, EDGE, EDGE), neighbours.reshape(brick_total // group_size, group_size, 26))
    return lax.map(one_group, grouped).reshape(brick_total, channels, EDGE ** 3)


def reference(features, fine_links, coarse_links, parents, down_weight, coarse_weight, up_weight, fine_weight, coarse_bias, fine_bias):
    half_edge = EDGE // 2
    octant_size = half_edge ** 3
    brick_total, channels = features.shape[0], features.shape[1]
    coarse_total = coarse_links.shape[0]
    down_float = down_weight.astype(jnp.float32)
    up_float = up_weight.astype(jnp.float32)

    def project(block_rows):
        split_rows = block_rows.reshape(BR_DEV, channels, half_edge, 2, half_edge, 2, half_edge, 2)
        split_rows = jnp.transpose(split_rows, (0, 3, 5, 7, 1, 2, 4, 6)).reshape(BR_DEV, 8, channels, octant_size)
        summed = jnp.einsum("oed,bodu->beu", down_float, split_rows.astype(jnp.float32), precision=lax.Precision.HIGHEST)
        return summed.astype(jnp.bfloat16)

    projected = lax.map(project, features.reshape(brick_total // BR_DEV, BR_DEV, channels, EDGE ** 3))
    projected = projected.reshape(brick_total, channels, octant_size)
    summed = jax.ops.segment_sum(projected.astype(jnp.float32), parents, num_segments=8 * coarse_total)
    summed = summed.reshape(coarse_total, 2, 2, 2, channels, half_edge, half_edge, half_edge)
    coarse_in = jnp.transpose(summed, (0, 4, 1, 5, 2, 6, 3, 7)).reshape(coarse_total, channels, EDGE ** 3).astype(jnp.bfloat16)
    coarse_out = level_conv(coarse_in, coarse_links, coarse_weight, coarse_bias, CBR_DEV)
    octant_rows = coarse_out.reshape(coarse_total, channels, 2, half_edge, 2, half_edge, 2, half_edge)
    octant_rows = jnp.transpose(octant_rows, (0, 2, 4, 6, 1, 3, 5, 7)).reshape(8 * coarse_total, channels, octant_size)

    def lift(packed):
        rows_here, codes_here = packed
        octants = octant_rows[codes_here].astype(jnp.float32)
        upsampled = jnp.einsum("oec,bcu->boeu", up_float, octants, precision=lax.Precision.HIGHEST)
        upsampled = upsampled.reshape(BR_DEV, 2, 2, 2, channels, half_edge, half_edge, half_edge)
        upsampled = jnp.transpose(upsampled, (0, 4, 5, 1, 6, 2, 7, 3)).reshape(BR_DEV, channels, EDGE ** 3)
        return (rows_here.astype(jnp.float32) + upsampled).astype(jnp.bfloat16)

    merged = lax.map(lift, (features.reshape(brick_total // BR_DEV, BR_DEV, channels, EDGE ** 3), parents.reshape(brick_total // BR_DEV, BR_DEV)))
    merged = merged.reshape(brick_total, channels, EDGE ** 3)
    return level_conv(merged, fine_links, fine_weight, fine_bias, BR_DEV)
```

```python
import numpy as np
import jax
import jax.numpy as jnp
from jax import lax
from jax.experimental import pallas as pl
from jax.experimental.pallas import tpu as pltpu
from jax.sharding import PartitionSpec as P

EDGE = 8
HALF = EDGE // 2
CUBE = HALF**3
FRAME = EDGE + 2
NBLK = 32
F32 = jnp.float32
BF16 = jnp.bfloat16
VMEM_LIMIT = 56 * 1024 * 1024


def headings():
    face_steps = [(1, 0, 0), (-1, 0, 0), (0, 1, 0), (0, -1, 0), (0, 0, 1), (0, 0, -1)]
    others = []
    for step_x in (-1, 0, 1):
        for step_y in (-1, 0, 1):
            for step_z in (-1, 0, 1):
                if abs(step_x) + abs(step_y) + abs(step_z) >= 2:
                    others.append((step_x, step_y, step_z))
    return face_steps + others


HEADINGS = headings()
HEADING_INDEX = {d: k for k, d in enumerate(HEADINGS)}
HEADING_INDEX[(0, 0, 0)] = len(HEADINGS)


def piece_lanes():
    starts, at = [], 0
    order = sorted(
        range(len(HEADINGS)), key=lambda k: (sum(1 for e in HEADINGS[k] if e), k)
    )
    starts = [0] * len(HEADINGS)
    voxels = [None] * len(HEADINGS)
    for k in order:
        spans = [
            [0] if e == 1 else [EDGE - 1] if e == -1 else list(range(EDGE))
            for e in HEADINGS[k]
        ]
        voxels[k] = [
            (x * EDGE + y) * EDGE + z
            for x in spans[0]
            for y in spans[1]
            for z in spans[2]
        ]
        starts[k] = at
        at += len(voxels[k])
    return starts, voxels


STARTS, VOXELS = piece_lanes()


def octant_selector():
    sel = np.zeros((EDGE**3, EDGE**3), np.float32)
    for x in range(EDGE):
        for y in range(EDGE):
            for z in range(EDGE):
                o = (x % 2) * 4 + (y % 2) * 2 + z % 2
                u = ((x // 2) * HALF + y // 2) * HALF + z // 2
                sel[(x * EDGE + y) * EDGE + z, o * CUBE + u] = 1
    return sel


def outer_selector():
    sel = np.zeros((EDGE**3, EDGE**3), np.float32)
    for k in range(len(HEADINGS)):
        for i, v in enumerate(VOXELS[k]):
            sel[v, STARTS[k] + i] = 1
    return sel


def pair_selector():
    sel = np.zeros((256, 256), np.float32)
    for x in range(2):
        for y in range(8):
            for b in range(2):
                for z in range(8):
                    sel[((x * 8 + y) * 2 + b) * 8 + z, ((b * 2 + x) * 8 + y) * 8 + z] = 1
    return sel


def dot(a, b):
    return lax.dot_general(a, b, (((1,), (0,)), ((), ())), preferred_element_type=F32)


def dot_t(a, b):
    return lax.dot_general(a, b, (((1,), (1,)), ((), ())), preferred_element_type=F32)


def params():
    return pltpu.CompilerParams(vmem_limit_bytes=VMEM_LIMIT)


def cost(flops, moved):
    return pl.CostEstimate(flops=flops, bytes_accessed=moved, transcendentals=0)


VM = pltpu.VMEM
SM = pltpu.SMEM


def project_kernel(chans, me_ref, f_ref, oct_ref, outer_ref, w_ref, *rest):
    outs, hs_ref, part = rest[:chans], rest[chans], rest[chans + 1]
    q = w_ref.shape[2]
    fine = f_ref.shape[0] // q
    x = f_ref[...]
    picked = dot(x, oct_ref[...]).astype(BF16)
    acc = None
    for o in range(8):
        z = jnp.concatenate(
            [picked[b * q : (b + 1) * q, o * CUBE : (o + 1) * CUBE] for b in range(fine)],
            axis=1,
        )
        term = dot(w_ref[o], z)
        acc = term if acc is None else acc + term
    part[...] = acc
    me = me_ref[0]
    for s in range(chans):
        outs[s][...] = part[pl.ds(pl.multiple_of((me ^ s) * q, q), q), :].astype(BF16)
    hs_ref[...] = dot(x, outer_ref[...]).astype(BF16)


def project(me, features, down_weight, chans):
    fine, q, vox = features.shape
    c_out = down_weight.shape[1]
    lanes = fine * CUBE
    res = pl.pallas_call(
        lambda *refs: project_kernel(chans, *refs),
        out_shape=[jax.ShapeDtypeStruct((q, lanes), BF16)] * chans
        + [jax.ShapeDtypeStruct((fine * q, vox), BF16)],
        in_specs=[pl.BlockSpec(memory_space=SM)] + [pl.BlockSpec(memory_space=VM)] * 4,
        out_specs=[pl.BlockSpec(memory_space=VM)] * (chans + 1),
        scratch_shapes=[pltpu.VMEM((c_out, lanes), F32)],
        compiler_params=params(),
        cost_estimate=cost(2 * c_out * 8 * q * lanes, 2 * 1024 * 1024),
        name="project",
    )(
        me,
        features.reshape(fine * q, vox),
        jnp.asarray(octant_selector(), BF16),
        jnp.asarray(outer_selector(), BF16),
        down_weight,
    )
    return res[:chans], res[chans]


def assemble_kernel(chans, *refs):
    slots, hs_ref, meta_ref, out_ref = refs[:chans], refs[chans], refs[chans + 1], refs[chans + 2]
    total = slots[0][...].astype(F32)
    for s in slots[1:]:
        total = total + s[...].astype(F32)
    q, lanes = slots[0].shape
    rows = hs_ref.shape[0]
    out_ref[0, 0:q, :] = total.astype(BF16)
    at = q
    for h in range(hs_ref.shape[1] // lanes):
        out_ref[0, at : at + rows, :] = hs_ref[:, h * lanes : (h + 1) * lanes]
        at += rows
    out_ref[0, at : at + meta_ref.shape[0], :] = meta_ref[...]


def assemble(slots, outer, meta, owners):
    q, lanes = slots[0].shape
    rows = q + outer.shape[0] * outer.shape[1] // lanes + meta.shape[0]
    whole = lambda a: pl.BlockSpec(a.shape, lambda i: (0,) * a.ndim)
    ins = list(slots) + [outer, meta]
    return pl.pallas_call(
        lambda *refs: assemble_kernel(len(slots), *refs),
        out_shape=jax.ShapeDtypeStruct((owners, rows, lanes), BF16),
        grid=(owners,),
        in_specs=[whole(a) for a in ins],
        out_specs=pl.BlockSpec((1, rows, lanes), lambda i: (i, 0, 0)),
        compiler_params=params(),
        name="assemble",
    )(*ins)


def halo_kernel(q, links_ref, recv_ref, out_ref):
    fine = out_ref.shape[0]
    lanes = recv_ref.shape[2]
    lane = lax.broadcasted_iota(jnp.int32, (q, 128), 1)
    for b in range(fine):
        for chunk in range(out_ref.shape[2] // 128):
            here = jnp.zeros((q, 128), F32)
            base = q + (chunk * 128 // lanes) * fine * q
            col = chunk * 128 % lanes
            for k in range(len(HEADINGS)):
                if STARTS[k] // 128 != chunk:
                    continue
                first = STARTS[k] % 128
                last = first + len(VOXELS[k])
                m = links_ref[b, k]
                safe = jnp.maximum(m, 0)
                row = pl.multiple_of(base + lax.rem(safe, fine) * q, 16)
                got = recv_ref[lax.div(safe, fine), pl.ds(row, q), col : col + 128].astype(F32)
                got = jnp.where(m >= 0, got, 0.0)
                here = jnp.where((lane >= first) & (lane < last), got, here)
            out_ref[b, :, chunk * 128 : (chunk + 1) * 128] = here.astype(BF16)


def halo(links, recv, fine, q, vox):
    return pl.pallas_call(
        lambda *refs: halo_kernel(q, *refs),
        out_shape=jax.ShapeDtypeStruct((fine, q, vox), BF16),
        in_specs=[pl.BlockSpec(memory_space=SM), pl.BlockSpec(memory_space=VM)],
        out_specs=pl.BlockSpec(memory_space=VM),
        compiler_params=params(),
        name="halo",
    )(links, recv)


def axis_places(u):
    found = [(0, 1 + u)]
    if u == 0:
        found.append((1, HALF + 1))
    if u == HALF - 1:
        found.append((-1, 0))
    return found


def coarse_kernel(proj_ref, target_ref, parents_ref, w_ref, bias_ref, out_ref, rows_ref, sel_ref, nb_ref):
    chans, owners, q, lanes = proj_ref.shape
    fine = lanes // CUBE
    total = owners * fine

    def spread(w, _):
        block = jnp.concatenate([proj_ref[c, w] for c in range(chans)], axis=0)
        turned = block.astype(F32).T
        for b in range(fine):
            rows_ref[pl.ds(w * fine + b, CUBE, stride=total), :] = turned[b * CUBE : (b + 1) * CUBE]
        return 0

    @pl.when(pl.program_id(0) == 0)
    def _():
        if owners <= 8:
            for w in range(owners):
                spread(w, 0)
        else:
            lax.fori_loop(0, owners, spread, 0)

    for d in range(27):
        sel_ref[d * NBLK : (d + 1) * NBLK, :] = (
            (target_ref[:, d : d + 1] == parents_ref[0:1, :]).astype(F32).astype(BF16)
        )
    for ux in range(HALF):
        for uy in range(HALF):
            for uz in range(HALF):
                places = [
                    (9 * (a[0] + 1) + 3 * (b[0] + 1) + c[0] + 1, a[1], b[1], c[1])
                    for a in axis_places(ux)
                    for b in axis_places(uy)
                    for c in axis_places(uz)
                ]
                u = (ux * HALF + uy) * HALF + uz
                source = rows_ref[u * total : (u + 1) * total, :].astype(BF16)
                picker = jnp.concatenate(
                    [sel_ref[d * NBLK : (d + 1) * NBLK, :] for d, _, _, _ in places], axis=0
                )
                got = dot(picker, source).astype(BF16)
                for i, (_, x, y, z) in enumerate(places):
                    nb_ref[x, y, z] = got[i * NBLK : (i + 1) * NBLK]
    span = HALF + 2
    size = span * HALF * HALF * NBLK
    acc = conv_rows(
        w_ref,
        lambda a2, a3: nb_ref[:, a2 : a2 + HALF, a3 : a3 + HALF].reshape(size, nb_ref.shape[4]),
    )
    step = HALF * HALF * NBLK
    n = HALF * step
    res = acc[0:q, 0:n] + acc[q : 2 * q, step : step + n] + acc[2 * q : 3 * q, 2 * step : 2 * step + n]
    out_ref[0] = jnp.maximum(res + bias_ref[...], 0.0).astype(BF16)


def conv_rows(w_ref, rows_of):
    taps = [(a2, a3) for a2 in range(3) for a3 in range(3)]
    acc = None
    for i in range(0, 9, 2):
        some = taps[i : i + 2]
        lhs = jnp.concatenate(
            [
                jnp.concatenate([w_ref[9 * a1 + 3 * a2 + a3] for a1 in range(3)], axis=0)
                for a2, a3 in some
            ],
            axis=1,
        )
        rhs = jnp.concatenate([rows_of(a2, a3) for a2, a3 in some], axis=1)
        term = dot_t(lhs, rhs)
        acc = term if acc is None else acc + term
    return acc


def coarse(proj, target, parents, weight, bias):
    chans, owners, q, lanes = proj.shape
    total = owners * lanes // CUBE
    blocks = total // NBLK
    c_in = weight.shape[2]
    whole = lambda a: pl.BlockSpec(a.shape, lambda i: (0,) * a.ndim)
    return pl.pallas_call(
        coarse_kernel,
        out_shape=jax.ShapeDtypeStruct((blocks, q, CUBE * NBLK), BF16),
        grid=(blocks,),
        in_specs=[
            whole(proj),
            pl.BlockSpec((NBLK, target.shape[1]), lambda i: (i, 0)),
            whole(parents),
            whole(weight),
            whole(bias),
        ],
        out_specs=pl.BlockSpec((1, q, CUBE * NBLK), lambda i: (i, 0, 0)),
        scratch_shapes=[
            pltpu.VMEM((CUBE * total, c_in), F32),
            pltpu.VMEM((27 * NBLK, total), BF16),
            pltpu.VMEM((HALF + 2, HALF + 2, HALF + 2, NBLK, c_in), BF16),
        ],
        compiler_params=params(),
        cost_estimate=cost(2 * 27 * c_in * q * CUBE * total, 2 * 1024 * 1024),
        name="coarse",
    )(proj, target, parents, weight, bias)


def frame_axis(f):
    if f == 0:
        return -1, EDGE - 1
    if f == FRAME - 1:
        return 1, 0
    return 0, f - 1


def frame_kernel(owner_ref, links_ref, fi_ref, fh_ref, ff_ref, sel_ref, inner, outer, plane):
    chans, fine, q, vox = fi_ref.shape
    span = 8 * fine
    owner = owner_ref[0]
    for b in range(fine):
        inner[b] = jnp.concatenate([fi_ref[c, b] for c in range(chans)], axis=0).astype(F32).T
        outer[b] = jnp.concatenate([fh_ref[c, b] for c in range(chans)], axis=0).astype(F32).T
    for b in range(fine):
        for s in range(2):
            dz = 2 * s - 1
            row = 2 * b + s
            for fx in range(FRAME):
                dx, vx = frame_axis(fx)
                start = STARTS[HEADING_INDEX[(dx, 0, dz)]] + (0 if dx else vx * EDGE)
                plane[pl.ds((fx * FRAME + 1) * 8 + row, EDGE, stride=8), :] = outer[b, start : start + EDGE, :]
            for fy in (0, FRAME - 1):
                dy = frame_axis(fy)[0]
                start = STARTS[HEADING_INDEX[(0, dy, dz)]]
                plane[pl.ds((FRAME + fy) * 8 + row, EDGE, stride=8 * FRAME), :] = outer[b, start : start + EDGE, :]
                for fx in (0, FRAME - 1):
                    start = STARTS[HEADING_INDEX[(frame_axis(fx)[0], dy, dz)]]
                    plane[pl.ds((fx * FRAME + fy) * 8 + row, 1), :] = outer[b, start : start + 1, :]
    for fx in range(FRAME):
        for fy in range(FRAME):
            dx, vx = frame_axis(fx)
            dy, vy = frame_axis(fy)
            at = ((1 - fx % 2) * 2 + 1 - fy % 2) * 25 + (fx // 2) * 5 + fy // 2
            tiles = []
            for b in range(fine):
                if dx == 0 and dy == 0:
                    start = (vx * EDGE + vy) * EDGE
                    tiles.append(inner[b, start : start + EDGE, :])
                else:
                    start = STARTS[HEADING_INDEX[(dx, dy, 0)]]
                    if dx == 0:
                        start += vx * EDGE
                    elif dy == 0:
                        start += vy * EDGE
                    tiles.append(outer[b, start : start + EDGE, :])
            tiles.append(plane[(fx * FRAME + fy) * 8 : (fx * FRAME + fy) * 8 + 8, :])
            tiles.append(jnp.zeros((8, plane.shape[1]), F32))
            ff_ref[at] = jnp.concatenate(tiles, axis=0).astype(BF16)
    blocks = sel_ref.shape[0]
    lane = lax.broadcasted_iota(jnp.int32, (8, 128), 1)
    row = lax.broadcasted_iota(jnp.int32, (8, 128), 0)

    def pick(j, _):
        for dx in (-1, 0, 1):
            for dy in (-1, 0, 1):
                def brick(b, dz):
                    k = HEADING_INDEX[(dx, dy, dz)]
                    n = owner * fine + b if k == len(HEADINGS) else links_ref[b, k]
                    n = n - j * NBLK
                    return jnp.where((n >= 0) & (n < NBLK), n, -1024)

                tiles = []
                for b in range(fine):
                    tiles.append((lane - (row // 2) * NBLK == brick(b, 0)).astype(F32))
                low = jnp.full((8, 128), -1024, jnp.int32)
                for b in range(fine):
                    for s in range(2):
                        n = brick(b, 2 * s - 1) + (HALF - 1) * (1 - s) * NBLK
                        low = jnp.where(row == 2 * b + s, n, low)
                tiles.append((lane == low).astype(F32))
                tiles.append(jnp.zeros((8, 128), F32))
                sel_ref[j, 3 * (dx + 1) + dy + 1] = jnp.concatenate(tiles, axis=0).astype(BF16)
        return 0

    if blocks == 1:
        pick(0, 0)
    else:
        lax.fori_loop(0, blocks, pick, 0)


def frames(owner, links, inner, outer, blocks):
    chans, fine, q, vox = inner.shape
    rows = 8 * fine + 16
    return pl.pallas_call(
        frame_kernel,
        out_shape=[
            jax.ShapeDtypeStruct((FRAME * FRAME, rows, chans * q), BF16),
            jax.ShapeDtypeStruct((blocks, 9, rows, 128), BF16),
        ],
        in_specs=[pl.BlockSpec(memory_space=SM)] * 2 + [pl.BlockSpec(memory_space=VM)] * 2,
        out_specs=[pl.BlockSpec(memory_space=VM)] * 2,
        scratch_shapes=[
            pltpu.VMEM((fine, vox, chans * q), F32),
            pltpu.VMEM((fine, vox, chans * q), F32),
            pltpu.VMEM((FRAME * FRAME * 8, chans * q), F32),
        ],
        compiler_params=params(),
        name="frames",
    )(owner, links, inner, outer)


def fine_kernel(co_ref, ff_ref, sel_ref, up_ref, w_ref, bias_ref, pair_ref, out_ref, cr, g3):
    chans, blocks, q, _ = co_ref.shape
    c_all = chans * q
    fine = out_ref.shape[0]
    rows = ff_ref.shape[1]
    for ux in range(HALF):
        for uy in range(HALF):
            places = [
                (3 * (a[0] + 1) + b[0] + 1, a[1], b[1])
                for a in axis_places(ux)
                for b in axis_places(uy)
            ]
            col = (ux * HALF + uy) * 128

            def part(j):
                source = jnp.concatenate(
                    [co_ref[c, j, :, col : col + 128] for c in range(chans)], axis=0
                )
                picker = jnp.concatenate([sel_ref[j, d] for d, _, _ in places], axis=0)
                return dot_t(picker, source)

            if blocks == 1:
                got = part(0)
            else:
                got = lax.fori_loop(
                    0,
                    blocks,
                    lambda j, a: a + part(j),
                    jnp.zeros((len(places) * rows, c_all), F32),
                )
            got = got.astype(BF16)
            for i, (_, x, y) in enumerate(places):
                cr[x, y] = got[i * rows : (i + 1) * rows]
    r = lax.broadcasted_iota(jnp.int32, (rows, c_all), 0)
    odd = (r % 2 == 1) ^ (r >= 8 * fine)
    sub = lax.broadcasted_iota(jnp.int32, (5, 8, c_all), 1)
    for px in range(2):
        for py in range(2):
            lift = jnp.concatenate([up_ref[4 * px + 2 * py], up_ref[4 * px + 2 * py + 1]], axis=0)
            for i in range(5):
                x = i + 1 - px
                src = cr[x, 1 - py : 6 - py].reshape(5 * rows, c_all)
                both = dot_t(src, lift).reshape(5, rows, 2 * c_all)
                up = jnp.where(odd[None], both[:, :, c_all:], both[:, :, :c_all])
                at = (px * 2 + py) * 25 + i * 5
                merged = (ff_ref[at : at + 5].astype(F32) + up).astype(BF16).astype(F32)
                fx = 2 * i + 1 - px
                plane = merged[:, 8 * fine : 8 * fine + 8, :]
                for pair in range(fine // 2):
                    made = [[], [], []]
                    for h in range(2):
                        b = 2 * pair + h
                        mid = merged[:, 8 * b : 8 * b + 8, :]
                        made[0].append(
                            jnp.where(
                                sub == 0,
                                pltpu.roll(plane, (8 - 2 * b) % 8, 1),
                                pltpu.roll(mid, 1, 1),
                            )
                        )
                        made[1].append(mid)
                        made[2].append(
                            jnp.where(
                                sub == 7,
                                pltpu.roll(plane, 7 - (2 * b + 1), 1),
                                pltpu.roll(mid, 7, 1),
                            )
                        )
                    for a3 in range(3):
                        tile = jnp.concatenate(made[a3], axis=1).astype(BF16)
                        for j in range(5):
                            g3[a3, pair, fx, 2 * j + 1 - py] = tile[j]
    step = EDGE * 2 * EDGE
    n = EDGE * step
    for pair in range(fine // 2):
        acc = conv_rows(
            w_ref,
            lambda a2, a3: g3[a3, pair, :, a2 : a2 + EDGE].reshape(FRAME * step, c_all),
        )
        res = acc[0:q, 0:n] + acc[q : 2 * q, step : step + n] + acc[2 * q : 3 * q, 2 * step : 2 * step + n]
        res = jnp.maximum(res + bias_ref[...], 0.0).astype(BF16)
        for h in range(n // 256):
            turned = dot(res[:, 256 * h : 256 * h + 256], pair_ref[...]).astype(BF16)
            for b in range(2):
                out_ref[2 * pair + b, :, 128 * h : 128 * h + 128] = turned[:, 128 * b : 128 * b + 128]


def refine(co, ff, sel, up_weight, weight, bias):
    chans, blocks, q, _ = co.shape
    rows = ff.shape[1]
    fine = (rows - 16) // 8
    c_all = chans * q
    return pl.pallas_call(
        fine_kernel,
        out_shape=jax.ShapeDtypeStruct((fine, q, EDGE**3), BF16),
        in_specs=[pl.BlockSpec(memory_space=VM)] * 7,
        out_specs=pl.BlockSpec(memory_space=VM),
        scratch_shapes=[
            pltpu.VMEM((HALF + 2, HALF + 2, rows, c_all), BF16),
            pltpu.VMEM((3, fine // 2, FRAME, FRAME, 2 * EDGE, c_all), BF16),
        ],
        compiler_params=params(),
        cost_estimate=cost(2 * 27 * c_all * q * fine * EDGE**3, 4 * 1024 * 1024),
        name="refine",
    )(co, ff, sel, up_weight, weight, bias, jnp.asarray(pair_selector(), BF16))


def octant_table():
    columns = np.zeros((8, 27), np.int32)
    octants = np.zeros((8, 27), np.int32)
    for o in range(8):
        bits = (o >> 2 & 1, o >> 1 & 1, o & 1)
        for d in range(27):
            go = (d // 9 - 1, d // 3 % 3 - 1, d % 3 - 1)
            cross, land = [], []
            for bit, g in zip(bits, go):
                t = bit + g
                cross.append(-1 if t < 0 else 1 if t > 1 else 0)
                land.append(t % 2)
            columns[o, d] = HEADING_INDEX[tuple(cross)]
            octants[o, d] = land[0] * 4 + land[1] * 2 + land[2]
    return columns, octants


def described(coarse_links, parents, owner, lanes):
    count = coarse_links.shape[0]
    columns, octants = octant_table()
    mine = owner * count + jnp.arange(count, dtype=jnp.int32)
    links = jnp.concatenate([coarse_links, mine[:, None]], axis=1)
    there = links[:, columns.reshape(-1)].reshape(count, 8, 27)
    codes = jnp.where(there >= 0, there * 8 + octants[None], -1).reshape(count * 8, 27) + 1
    ups = jnp.pad(parents[:, None] + 1, ((0, count * 8 - parents.shape[0]), (0, 0)))
    both = jnp.concatenate([codes, ups], axis=1)
    digits = jnp.concatenate([both // 128, both % 128], axis=1)
    return jnp.pad(digits, ((0, 0), (0, lanes - digits.shape[1]))).astype(BF16)


def understood(meta, fine):
    value = meta[:, :, :56].astype(jnp.int32)
    value = value[:, :, :28] * 128 + value[:, :, 28:] - 1
    table = value[:, :, :27].reshape(-1, 27)
    parents = value[:, :fine, 27].reshape(-1)
    return jnp.take(table, parents, axis=0), parents[None, :]


def per_device(
    features,
    fine_links,
    coarse_links,
    parents,
    down_weight,
    coarse_weight,
    up_weight,
    fine_weight,
    coarse_bias,
    fine_bias,
):
    owners = lax.axis_size("brick")
    chans = lax.axis_size("chan")
    owner = lax.axis_index("brick").astype(jnp.int32)
    me = lax.axis_index("chan").astype(jnp.int32)
    fine, q, vox = features.shape
    lanes = fine * CUBE
    meta = described(coarse_links, parents, owner, lanes)
    slots, outer = project(me[None], features, down_weight, chans)
    arrived = [slots[0]] + [
        lax.ppermute(slots[s], "chan", [(i, i ^ s) for i in range(chans)])
        for s in range(1, chans)
    ]
    sending = assemble(arrived, outer, meta, owners)
    recv = lax.all_to_all(sending, "brick", split_axis=0, concat_axis=0, tiled=True)
    proj = lax.all_gather(recv[:, :q], "chan", axis=0)
    target, all_parents = understood(recv[:, recv.shape[1] - meta.shape[0] :], fine)
    co = coarse(proj, target, all_parents, coarse_weight, coarse_bias[:, None])
    co = lax.all_gather(co, "chan", axis=0)
    around = halo(fine_links, recv, fine, q, vox)
    fi = lax.all_gather(features, "chan", axis=0)
    fh = lax.all_gather(around, "chan", axis=0)
    up_all = lax.all_gather(up_weight, "chan", axis=1, tiled=True)
    ff, sel = frames(owner[None], fine_links, fi, fh, co.shape[1])
    return refine(co, ff, sel, up_all, fine_weight, fine_bias[:, None])


def solution(mesh):
    in_specs = (
        P("brick", "chan", None),
        P("brick", None),
        P("brick", None),
        P("brick"),
        P(None, None, "chan"),
        P(None, "chan", None),
        P(None, "chan", None),
        P(None, "chan", None),
        P("chan"),
        P("chan"),
    )
    return jax.shard_map(
        per_device,
        mesh=mesh,
        in_specs=in_specs,
        out_specs=P("brick", "chan", None),
        check_vma=False,
    )
```

```python
import numpy as np
import jax
import jax.numpy as jnp
from jax import lax
from jax.experimental import pallas as pl
from jax.experimental.pallas import tpu as pltpu
from jax.sharding import PartitionSpec as P

EDGE = 8
HALF = EDGE // 2
CUBE = HALF**3
FRAME = EDGE + 2
NBLK = 32
F32 = jnp.float32
BF16 = jnp.bfloat16
VMEM_LIMIT = 56 * 1024 * 1024


def headings():
    face_steps = [(1, 0, 0), (-1, 0, 0), (0, 1, 0), (0, -1, 0), (0, 0, 1), (0, 0, -1)]
    others = []
    for step_x in (-1, 0, 1):
        for step_y in (-1, 0, 1):
            for step_z in (-1, 0, 1):
                if abs(step_x) + abs(step_y) + abs(step_z) >= 2:
                    others.append((step_x, step_y, step_z))
    return face_steps + others


HEADINGS = headings()
HEADING_INDEX = {d: k for k, d in enumerate(HEADINGS)}
HEADING_INDEX[(0, 0, 0)] = len(HEADINGS)


def piece_lanes():
    order = sorted(
        range(len(HEADINGS)), key=lambda k: (sum(1 for e in HEADINGS[k] if e), k)
    )
    starts, voxels, at = [0] * len(HEADINGS), [None] * len(HEADINGS), 0
    for k in order:
        spans = [
            [0] if e == 1 else [EDGE - 1] if e == -1 else list(range(EDGE))
            for e in HEADINGS[k]
        ]
        voxels[k] = [
            (x * EDGE + y) * EDGE + z
            for x in spans[0]
            for y in spans[1]
            for z in spans[2]
        ]
        starts[k] = at
        at += len(voxels[k])
    return starts, voxels


STARTS, VOXELS = piece_lanes()
for k in (2, 3):
    VOXELS[k] = [VOXELS[k][x * EDGE + z] for z in range(EDGE) for x in range(EDGE)]
SENT = [v for k in range(6) for v in VOXELS[k]]
SOURCES = []
for k, heading in enumerate(HEADINGS):
    for f in range(6):
        run = VOXELS[f]
        want = VOXELS[k]
        first = run.index(want[0]) if want[0] in run else -1
        if first >= 0 and run[first : first + len(want)] == want:
            SOURCES.append(EDGE**2 * f + first)
            break
assert len(SOURCES) == len(HEADINGS)


def octant_selector():
    sel = np.zeros((EDGE**3, EDGE**3), np.float32)
    for x in range(EDGE):
        for y in range(EDGE):
            for z in range(EDGE):
                o = (x % 2) * 4 + (y % 2) * 2 + z % 2
                u = ((x // 2) * HALF + y // 2) * HALF + z // 2
                sel[(x * EDGE + y) * EDGE + z, o * CUBE + u] = 1
    return sel


def outer_selector():
    sel = np.zeros((EDGE**3, len(SENT)), np.float32)
    for i, v in enumerate(SENT):
        sel[v, i] = 1
    return sel


def pair_selector():
    sel = np.zeros((256, 256), np.float32)
    for x in range(2):
        for y in range(8):
            for b in range(2):
                for z in range(8):
                    sel[((x * 8 + y) * 2 + b) * 8 + z, ((b * 2 + x) * 8 + y) * 8 + z] = 1
    return sel


def dot(a, b):
    return lax.dot_general(a, b, (((1,), (0,)), ((), ())), preferred_element_type=F32)


def dot_t(a, b):
    return lax.dot_general(a, b, (((1,), (1,)), ((), ())), preferred_element_type=F32)


def params():
    return pltpu.CompilerParams(vmem_limit_bytes=VMEM_LIMIT)


def cost(flops, moved):
    return pl.CostEstimate(flops=flops, bytes_accessed=moved, transcendentals=0)


VM = pltpu.VMEM
SM = pltpu.SMEM


def project_kernel(chans, me_ref, f_ref, oct_ref, w_ref, *rest):
    outs, part = rest[:chans], rest[chans]
    q = w_ref.shape[1]
    fine = f_ref.shape[0] // q
    picked = dot(f_ref[...], oct_ref[...]).astype(BF16)
    acc = None
    for o in range(8):
        z = jnp.concatenate(
            [picked[b * q : (b + 1) * q, o * CUBE : (o + 1) * CUBE] for b in range(fine)],
            axis=1,
        )
        term = lax.dot_general(
            w_ref[o], z, (((0,), (0,)), ((), ())), preferred_element_type=F32
        )
        acc = term if acc is None else acc + term
    part[...] = acc
    me = me_ref[0]
    for s in range(chans):
        outs[s][...] = part[pl.ds(pl.multiple_of((me ^ s) * q, q), q), :].astype(BF16)


def project(me, features, down_weight, chans):
    fine, q, vox = features.shape
    c_out = down_weight.shape[1]
    lanes = fine * CUBE
    return pl.pallas_call(
        lambda *refs: project_kernel(chans, *refs),
        out_shape=[jax.ShapeDtypeStruct((q, lanes), BF16)] * chans,
        in_specs=[pl.BlockSpec(memory_space=SM)] + [pl.BlockSpec(memory_space=VM)] * 3,
        out_specs=[pl.BlockSpec(memory_space=VM)] * chans,
        scratch_shapes=[pltpu.VMEM((c_out, lanes), F32)],
        compiler_params=params(),
        cost_estimate=cost(2 * c_out * 8 * q * lanes, 2 * 1024 * 1024),
        name="project",
    )(
        me,
        features.reshape(fine * q, vox),
        jnp.asarray(octant_selector(), BF16),
        jnp.transpose(down_weight, (0, 2, 1)),
    )


def spread_kernel(f_ref, up_ref, sel_ref, out_ref, pack_ref):
    rows, vox = f_ref.shape
    out_ref[...] = dot(f_ref[...], sel_ref[...]).astype(BF16)
    pack_ref[0:rows] = f_ref[...]
    more = up_ref.shape[0] * up_ref.shape[1] // vox
    for i in range(vox // up_ref.shape[1]):
        part = slice(i * up_ref.shape[1], (i + 1) * up_ref.shape[1])
        pack_ref[rows : rows + more, part] = up_ref[i * more : (i + 1) * more]


def spread_out(features, up_weight):
    fine, q, vox = features.shape
    ups = up_weight.reshape(-1, up_weight.shape[2])
    return pl.pallas_call(
        spread_kernel,
        out_shape=[
            jax.ShapeDtypeStruct((fine * q, len(SENT)), BF16),
            jax.ShapeDtypeStruct((fine * q + ups.size // vox, vox), BF16),
        ],
        in_specs=[pl.BlockSpec(memory_space=VM)] * 3,
        out_specs=[pl.BlockSpec(memory_space=VM)] * 2,
        compiler_params=params(),
        name="spread",
    )(features.reshape(fine * q, vox), ups, jnp.asarray(outer_selector(), BF16))


def assemble_kernel(owner_ref, links_ref, parents_ref, table_ref, *refs):
    slots, outer_ref, out_ref = refs[:-2], refs[-2], refs[-1]
    count, ways = links_ref.shape
    total = slots[0][...].astype(F32)
    for s in slots[1:]:
        total = total + s[...].astype(F32)
    q, lanes = slots[0].shape
    total = total.astype(BF16)
    rows = count * 8
    column, octant = table_ref[0], table_ref[1]
    row = lax.broadcasted_iota(jnp.int32, (rows, 128), 0)
    lane = lax.broadcasted_iota(jnp.int32, (rows, 128), 1)
    code = jnp.zeros((rows, 128), jnp.int32)
    for p in range(count):
        own = row // 8 == p
        for k in range(ways + 1):
            brick = owner_ref[0] * count + p if k == ways else links_ref[p, k]
            code = jnp.where(own & (column == k), jnp.where(brick >= 0, brick * 8 + octant + 1, 0), code)
    for b in range(parents_ref.shape[0]):
        code = jnp.where((row == b) & (lane == 27), parents_ref[b] + 1, code)
    high = lax.shift_right_logical(code, 7)
    digits = [high.astype(F32).astype(BF16), (code - high * 128).astype(F32).astype(BF16)]
    for w in range(out_ref.shape[0]):
        out_ref[w, 0:q, :] = total
        for i in range(2):
            out_ref[w, q : q + rows, 128 * i : 128 * i + 128] = digits[i]
        at, n = q + rows, outer_ref.shape[0]
        out_ref[w, at : at + n, :] = outer_ref[:, 0:256]
        for i in range(2):
            out_ref[w, at + n : at + n + n // 2, 128 * i : 128 * i + 128] = outer_ref[
                i * n // 2 : (i + 1) * n // 2, 256:384
            ]


def assemble(slots, outer, owner, coarse_links, parents, owners):
    q, lanes = slots[0].shape
    count = coarse_links.shape[0]
    columns, octants = octant_table()
    table = np.full((2, count * 8, 128), -1, np.int32)
    table[0, :, :27] = np.tile(columns, (count, 1))
    table[1, :, :27] = np.tile(octants, (count, 1))
    return pl.pallas_call(
        assemble_kernel,
        out_shape=jax.ShapeDtypeStruct((owners, q + count * 8 + outer.size // lanes, lanes), BF16),
        in_specs=[pl.BlockSpec(memory_space=SM)] * 3 + [pl.BlockSpec(memory_space=VM)] * (len(slots) + 2),
        out_specs=pl.BlockSpec(memory_space=VM),
        compiler_params=params(),
        name="assemble",
    )(owner, coarse_links, parents, jnp.asarray(table), *slots, outer)


def exchanged(x, chans):
    return [x] + [
        lax.ppermute(x, "chan", [(i, i ^ s) for i in range(chans)]) for s in range(1, chans)
    ]


def halo_kernel(q, base, links_ref, recv_ref, out_ref):
    fine = out_ref.shape[0]
    lane = lax.broadcasted_iota(jnp.int32, (q, 128), 1)
    for b in range(fine):
        for chunk in range(out_ref.shape[2] // 128):
            here = jnp.zeros((q, 128), F32)
            for k in range(len(HEADINGS)):
                if STARTS[k] // 128 != chunk:
                    continue
                first = STARTS[k] % 128
                last = first + len(VOXELS[k])
                m = links_ref[b, k]
                safe = jnp.maximum(m, 0)
                col = SOURCES[k] // 128
                row = lax.rem(safe, fine)
                if col < 2:
                    lanes = pl.ds(128 * col, 128)
                else:
                    lanes = pl.ds(pl.multiple_of(lax.div(row, fine // 2) * 128, 128), 128)
                    row = fine + lax.rem(row, fine // 2)
                row = pl.multiple_of(base + row * q, 16)
                got = recv_ref[lax.div(safe, fine), pl.ds(row, q), lanes].astype(F32)
                turn = (first - SOURCES[k]) % 128
                if turn:
                    got = pltpu.roll(got, turn, 1)
                got = jnp.where(m >= 0, got, 0.0)
                here = jnp.where((lane >= first) & (lane < last), got, here)
            out_ref[b, :, chunk * 128 : (chunk + 1) * 128] = here.astype(BF16)


def halo(links, recv, base, fine, q, vox):
    return pl.pallas_call(
        lambda *refs: halo_kernel(q, base, *refs),
        out_shape=jax.ShapeDtypeStruct((fine, q, vox), BF16),
        in_specs=[pl.BlockSpec(memory_space=SM), pl.BlockSpec(memory_space=VM)],
        out_specs=pl.BlockSpec(memory_space=VM),
        compiler_params=params(),
        name="halo",
    )(links, recv)


def axis_places(u):
    found = [(0, 1 + u)]
    if u == 0:
        found.append((1, HALF + 1))
    if u == HALF - 1:
        found.append((-1, 0))
    return found


def bias_column(row):
    n = row.shape[1]
    square = jnp.broadcast_to(row, (n, n))
    on = lax.broadcasted_iota(jnp.int32, (n, n), 0) == lax.broadcasted_iota(jnp.int32, (n, n), 1)
    return jnp.sum(jnp.where(on, square, 0.0), axis=1, keepdims=True)


def coarse_kernel(chans, codes, me_ref, *refs):
    slots, refs = refs[:chans], refs[chans:]
    recv_ref, w_ref, bias_ref, out_ref, proj_ref, rows_ref, sel_ref, nb_ref, parent_ref, table_ref = refs
    owners, q, lanes = slots[0].shape
    me = me_ref[0]
    fine = lanes // CUBE
    total = owners * fine

    def spread(w, _):
        block = jnp.concatenate([proj_ref[c, w] for c in range(chans)], axis=0)
        turned = block.astype(F32).T
        for b in range(fine):
            rows_ref[pl.ds(w * fine + b, CUBE, stride=total), :] = turned[b * CUBE : (b + 1) * CUBE]
        return 0

    @pl.when(pl.program_id(0) == 0)
    def _():
        for w in range(owners):
            digits = recv_ref[w, q : q + codes, :]
            table_ref[w * codes : (w + 1) * codes, :] = digits
            digits = digits.astype(F32)
            value = digits[:, 0:128] * 128.0 + digits[:, 128:256] - 1.0
            parent_ref[w * fine : (w + 1) * fine, :] = jnp.broadcast_to(value[0:fine, 27:28], (fine, 128))
        for s in range(chans):
            proj_ref[me ^ s] = slots[s][...]
        if owners <= 8:
            for w in range(owners):
                spread(w, 0)
        else:
            lax.fori_loop(0, owners, spread, 0)

    mine = parent_ref[pl.ds(pl.program_id(0) * NBLK, NBLK), :]
    row = lax.broadcasted_iota(jnp.int32, (NBLK, table_ref.shape[0]), 1).astype(F32)
    own = (mine[:, 0:1] == row).astype(F32).astype(BF16)
    digits = dot(own, table_ref[...])
    target = digits[:, 0:128] * 128.0 + digits[:, 128:256] - 1.0
    on = lax.broadcasted_iota(jnp.int32, (total, total), 0) == lax.broadcasted_iota(jnp.int32, (total, total), 1)
    parents = jnp.sum(jnp.where(on, parent_ref[:, 0:1], 0.0), axis=0, keepdims=True)
    for d in range(27):
        sel_ref[d * NBLK : (d + 1) * NBLK, :] = (target[:, d : d + 1] == parents).astype(F32).astype(BF16)
    for ux in range(HALF):
        for uy in range(HALF):
            for uz in range(HALF):
                places = [
                    (9 * (a[0] + 1) + 3 * (b[0] + 1) + c[0] + 1, a[1], b[1], c[1])
                    for a in axis_places(ux)
                    for b in axis_places(uy)
                    for c in axis_places(uz)
                ]
                u = (ux * HALF + uy) * HALF + uz
                source = rows_ref[u * total : (u + 1) * total, :].astype(BF16)
                picker = jnp.concatenate(
                    [sel_ref[d * NBLK : (d + 1) * NBLK, :] for d, _, _, _ in places], axis=0
                )
                got = dot(picker, source).astype(BF16)
                for i, (_, x, y, z) in enumerate(places):
                    nb_ref[x, y, z] = got[i * NBLK : (i + 1) * NBLK]
    span = HALF + 2
    size = span * HALF * HALF * NBLK
    acc = conv_rows(
        w_ref,
        lambda a2, a3: nb_ref[:, a2 : a2 + HALF, a3 : a3 + HALF].reshape(size, nb_ref.shape[4]),
    )
    step = HALF * HALF * NBLK
    n = HALF * step
    res = acc[0:q, 0:n] + acc[q : 2 * q, step : step + n] + acc[2 * q : 3 * q, 2 * step : 2 * step + n]
    out_ref[0] = jnp.maximum(res + bias_column(bias_ref[...]), 0.0).astype(BF16)


def conv_rows(w_ref, rows_of):
    taps = [(a2, a3) for a2 in range(3) for a3 in range(3)]
    acc = None
    for i in range(0, 9, 2):
        some = taps[i : i + 2]
        lhs = jnp.concatenate(
            [
                jnp.concatenate([w_ref[9 * a1 + 3 * a2 + a3] for a1 in range(3)], axis=0)
                for a2, a3 in some
            ],
            axis=1,
        )
        rhs = jnp.concatenate([rows_of(a2, a3) for a2, a3 in some], axis=1)
        term = dot_t(lhs, rhs)
        acc = term if acc is None else acc + term
    return acc


def coarse(me, slots, recv, codes, weight, bias):
    chans = len(slots)
    owners, q, lanes = slots[0].shape
    total = owners * lanes // CUBE
    blocks = total // NBLK
    c_in = weight.shape[2]
    whole = lambda a: pl.BlockSpec(a.shape, lambda i: (0,) * a.ndim)
    return pl.pallas_call(
        lambda *refs: coarse_kernel(chans, codes, *refs),
        out_shape=jax.ShapeDtypeStruct((blocks, q, CUBE * NBLK), BF16),
        grid=(blocks,),
        in_specs=[pl.BlockSpec(memory_space=SM)]
        + [whole(a) for a in slots]
        + [
            pl.BlockSpec((owners, q + codes, recv.shape[2]), lambda i: (0, 0, 0)),
            whole(weight),
            whole(bias),
        ],
        out_specs=pl.BlockSpec((1, q, CUBE * NBLK), lambda i: (i, 0, 0)),
        scratch_shapes=[
            pltpu.VMEM((chans, owners, q, lanes), BF16),
            pltpu.VMEM((CUBE * total, c_in), F32),
            pltpu.VMEM((27 * NBLK, total), BF16),
            pltpu.VMEM((HALF + 2, HALF + 2, HALF + 2, NBLK, c_in), BF16),
            pltpu.VMEM((total, 128), F32),
            pltpu.VMEM((owners * codes, 256), BF16),
        ],
        compiler_params=params(),
        cost_estimate=cost(2 * 27 * c_in * q * CUBE * total, 2 * 1024 * 1024),
        name="coarse",
    )(me, *slots, recv, weight, bias)


def frame_axis(f):
    if f == 0:
        return -1, EDGE - 1
    if f == FRAME - 1:
        return 1, 0
    return 0, f - 1


def frame_kernel(chans, me_ref, owner_ref, links_ref, *refs):
    packs, halos, refs = refs[:chans], refs[chans : 2 * chans], refs[2 * chans :]
    ff_ref, sel_ref, up_ref, both, inner, outer, plane = refs
    fine, q, vox = halos[0].shape
    owner = owner_ref[0]
    me = me_ref[0]
    for s in range(chans):
        at = pl.ds(pl.multiple_of((me ^ s) * q, q), q)
        for b in range(fine):
            both[0, b, at, :] = packs[s][b * q : (b + 1) * q, :]
            both[1, b, at, :] = halos[s][b]
        for o in range(8):
            row = (fine + o % 2) * q
            up_ref[o, at, :] = packs[s][row : row + q, o // 2 * 128 : o // 2 * 128 + 128]
    for b in range(fine):
        inner[b] = both[0, b].astype(F32).T
        outer[b] = both[1, b].astype(F32).T
    for b in range(fine):
        for s in range(2):
            dz = 2 * s - 1
            row = 2 * b + s
            for fx in range(FRAME):
                dx, vx = frame_axis(fx)
                start = STARTS[HEADING_INDEX[(dx, 0, dz)]] + (0 if dx else vx * EDGE)
                plane[pl.ds((fx * FRAME + 1) * 8 + row, EDGE, stride=8), :] = outer[b, start : start + EDGE, :]
            for fy in (0, FRAME - 1):
                dy = frame_axis(fy)[0]
                start = STARTS[HEADING_INDEX[(0, dy, dz)]]
                plane[pl.ds((FRAME + fy) * 8 + row, EDGE, stride=8 * FRAME), :] = outer[b, start : start + EDGE, :]
                for fx in (0, FRAME - 1):
                    start = STARTS[HEADING_INDEX[(frame_axis(fx)[0], dy, dz)]]
                    plane[pl.ds((fx * FRAME + fy) * 8 + row, 1), :] = outer[b, start : start + 1, :]
    for fx in range(FRAME):
        for fy in range(FRAME):
            dx, vx = frame_axis(fx)
            dy, vy = frame_axis(fy)
            at = ((1 - fx % 2) * 2 + 1 - fy % 2) * 25 + (fx // 2) * 5 + fy // 2
            tiles = []
            for b in range(fine):
                if dx == 0 and dy == 0:
                    start = (vx * EDGE + vy) * EDGE
                    tiles.append(inner[b, start : start + EDGE, :])
                else:
                    start = STARTS[HEADING_INDEX[(dx, dy, 0)]]
                    if dx == 0:
                        tiles.append(outer[b, pl.ds(start + vx, EDGE, stride=EDGE), :])
                    else:
                        start += 0 if dy else vy * EDGE
                        tiles.append(outer[b, start : start + EDGE, :])
            tiles.append(plane[(fx * FRAME + fy) * 8 : (fx * FRAME + fy) * 8 + 8, :])
            tiles.append(jnp.zeros((8, plane.shape[1]), F32))
            ff_ref[at] = jnp.concatenate(tiles, axis=0).astype(BF16)
    blocks = sel_ref.shape[0]
    lane = lax.broadcasted_iota(jnp.int32, (8, 128), 1)
    row = lax.broadcasted_iota(jnp.int32, (8, 128), 0)

    def pick(j, _):
        for dx in (-1, 0, 1):
            for dy in (-1, 0, 1):
                def brick(b, dz):
                    k = HEADING_INDEX[(dx, dy, dz)]
                    n = owner * fine + b if k == len(HEADINGS) else links_ref[b, k]
                    n = n - j * NBLK
                    return jnp.where((n >= 0) & (n < NBLK), n, -1024)

                tiles = []
                for b in range(fine):
                    tiles.append((lane - (row // 2) * NBLK == brick(b, 0)).astype(F32))
                low = jnp.full((8, 128), -1024, jnp.int32)
                for b in range(fine):
                    for s in range(2):
                        n = brick(b, 2 * s - 1) + (HALF - 1) * (1 - s) * NBLK
                        low = jnp.where(row == 2 * b + s, n, low)
                tiles.append((lane == low).astype(F32))
                tiles.append(jnp.zeros((8, 128), F32))
                sel_ref[j, 3 * (dx + 1) + dy + 1] = jnp.concatenate(tiles, axis=0).astype(BF16)
        return 0

    if blocks == 1:
        pick(0, 0)
    else:
        lax.fori_loop(0, blocks, pick, 0)


def frames(me, owner, links, packs, halos, blocks):
    chans = len(packs)
    fine, q, vox = halos[0].shape
    rows = 8 * fine + 16
    c_all = chans * q
    return pl.pallas_call(
        lambda *refs: frame_kernel(chans, *refs),
        out_shape=[
            jax.ShapeDtypeStruct((FRAME * FRAME, rows, c_all), BF16),
            jax.ShapeDtypeStruct((blocks, 9, rows, 128), BF16),
            jax.ShapeDtypeStruct((8, c_all, c_all), BF16),
        ],
        in_specs=[pl.BlockSpec(memory_space=SM)] * 3 + [pl.BlockSpec(memory_space=VM)] * (2 * chans),
        out_specs=[pl.BlockSpec(memory_space=VM)] * 3,
        scratch_shapes=[
            pltpu.VMEM((2, fine, c_all, vox), BF16),
            pltpu.VMEM((fine, vox, c_all), F32),
            pltpu.VMEM((fine, vox, c_all), F32),
            pltpu.VMEM((FRAME * FRAME * 8, c_all), F32),
        ],
        compiler_params=params(),
        name="frames",
    )(me, owner, links, *packs, *halos)


def fine_kernel(chans, me_ref, *refs):
    slots, refs = refs[:chans], refs[chans:]
    ff_ref, sel_ref, up_ref, w_ref, bias_ref, pair_ref, out_ref, co_ref, cr, g3 = refs
    blocks, q, _ = slots[0].shape
    c_all = chans * q
    for s in range(chans):
        co_ref[me_ref[0] ^ s] = slots[s][...]
    fine = out_ref.shape[0]
    rows = ff_ref.shape[1]
    for ux in range(HALF):
        for uy in range(HALF):
            places = [
                (3 * (a[0] + 1) + b[0] + 1, a[1], b[1])
                for a in axis_places(ux)
                for b in axis_places(uy)
            ]
            col = (ux * HALF + uy) * 128

            def part(j):
                source = jnp.concatenate(
                    [co_ref[c, j, :, col : col + 128] for c in range(chans)], axis=0
                )
                picker = jnp.concatenate([sel_ref[j, d] for d, _, _ in places], axis=0)
                return dot_t(picker, source)

            if blocks == 1:
                got = part(0)
            else:
                got = lax.fori_loop(
                    0,
                    blocks,
                    lambda j, a: a + part(j),
                    jnp.zeros((len(places) * rows, c_all), F32),
                )
            got = got.astype(BF16)
            for i, (_, x, y) in enumerate(places):
                cr[x, y] = got[i * rows : (i + 1) * rows]
    r = lax.broadcasted_iota(jnp.int32, (rows, c_all), 0)
    odd = (r % 2 == 1) ^ (r >= 8 * fine)
    sub = lax.broadcasted_iota(jnp.int32, (5, 8, c_all), 1)
    for px in range(2):
        for py in range(2):
            lift = jnp.concatenate([up_ref[4 * px + 2 * py], up_ref[4 * px + 2 * py + 1]], axis=0)
            for i in range(5):
                x = i + 1 - px
                src = cr[x, 1 - py : 6 - py].reshape(5 * rows, c_all)
                both = dot_t(src, lift).reshape(5, rows, 2 * c_all)
                up = jnp.where(odd[None], both[:, :, c_all:], both[:, :, :c_all])
                at = (px * 2 + py) * 25 + i * 5
                merged = (ff_ref[at : at + 5].astype(F32) + up).astype(BF16).astype(F32)
                fx = 2 * i + 1 - px
                plane = merged[:, 8 * fine : 8 * fine + 8, :]
                for pair in range(fine // 2):
                    made = [[], [], []]
                    for h in range(2):
                        b = 2 * pair + h
                        mid = merged[:, 8 * b : 8 * b + 8, :]
                        made[0].append(
                            jnp.where(
                                sub == 0,
                                pltpu.roll(plane, (8 - 2 * b) % 8, 1),
                                pltpu.roll(mid, 1, 1),
                            )
                        )
                        made[1].append(mid)
                        made[2].append(
                            jnp.where(
                                sub == 7,
                                pltpu.roll(plane, 7 - (2 * b + 1), 1),
                                pltpu.roll(mid, 7, 1),
                            )
                        )
                    for a3 in range(3):
                        tile = jnp.concatenate(made[a3], axis=1).astype(BF16)
                        for j in range(5):
                            g3[a3, pair, fx, 2 * j + 1 - py] = tile[j]
    step = EDGE * 2 * EDGE
    n = EDGE * step
    bias = bias_column(bias_ref[...])
    for pair in range(fine // 2):
        acc = conv_rows(
            w_ref,
            lambda a2, a3: g3[a3, pair, :, a2 : a2 + EDGE].reshape(FRAME * step, c_all),
        )
        res = acc[0:q, 0:n] + acc[q : 2 * q, step : step + n] + acc[2 * q : 3 * q, 2 * step : 2 * step + n]
        res = jnp.maximum(res + bias, 0.0).astype(BF16)
        for h in range(n // 256):
            turned = dot(res[:, 256 * h : 256 * h + 256], pair_ref[...]).astype(BF16)
            for b in range(2):
                out_ref[2 * pair + b, :, 128 * h : 128 * h + 128] = turned[:, 128 * b : 128 * b + 128]


def refine(me, slots, ff, sel, up_weight, weight, bias):
    chans = len(slots)
    blocks, q, wide = slots[0].shape
    rows = ff.shape[1]
    fine = (rows - 16) // 8
    c_all = chans * q
    return pl.pallas_call(
        lambda *refs: fine_kernel(chans, *refs),
        out_shape=jax.ShapeDtypeStruct((fine, q, EDGE**3), BF16),
        in_specs=[pl.BlockSpec(memory_space=SM)] + [pl.BlockSpec(memory_space=VM)] * (chans + 6),
        out_specs=pl.BlockSpec(memory_space=VM),
        scratch_shapes=[
            pltpu.VMEM((chans, blocks, q, wide), BF16),
            pltpu.VMEM((HALF + 2, HALF + 2, rows, c_all), BF16),
            pltpu.VMEM((3, fine // 2, FRAME, FRAME, 2 * EDGE, c_all), BF16),
        ],
        compiler_params=params(),
        cost_estimate=cost(2 * 27 * c_all * q * fine * EDGE**3, 4 * 1024 * 1024),
        name="refine",
    )(me, *slots, ff, sel, up_weight, weight, bias, jnp.asarray(pair_selector(), BF16))


def octant_table():
    columns = np.zeros((8, 27), np.int32)
    octants = np.zeros((8, 27), np.int32)
    for o in range(8):
        bits = (o >> 2 & 1, o >> 1 & 1, o & 1)
        for d in range(27):
            go = (d // 9 - 1, d // 3 % 3 - 1, d % 3 - 1)
            cross, land = [], []
            for bit, g in zip(bits, go):
                t = bit + g
                cross.append(-1 if t < 0 else 1 if t > 1 else 0)
                land.append(t % 2)
            columns[o, d] = HEADING_INDEX[tuple(cross)]
            octants[o, d] = land[0] * 4 + land[1] * 2 + land[2]
    return columns, octants


def per_device(
    features,
    fine_links,
    coarse_links,
    parents,
    down_weight,
    coarse_weight,
    up_weight,
    fine_weight,
    coarse_bias,
    fine_bias,
):
    owners = lax.axis_size("brick")
    chans = lax.axis_size("chan")
    owner = lax.axis_index("brick").astype(jnp.int32)
    me = lax.axis_index("chan").astype(jnp.int32)
    fine, q, vox = features.shape
    parts = project(me[None], features, down_weight, chans)
    arrived = [parts[0]] + [
        lax.ppermute(parts[s], "chan", [(i, i ^ s) for i in range(chans)])
        for s in range(1, chans)
    ]
    early, _ = lax.optimization_barrier((features, parts[0]))
    outer, packed = spread_out(early, up_weight)
    codes = 8 * coarse_links.shape[0]
    sending = assemble(arrived, outer, owner[None], coarse_links, parents, owners)
    recv = lax.all_to_all(sending, "brick", split_axis=0, concat_axis=0, tiled=True)
    packs = exchanged(packed, chans)
    recv, packs = lax.optimization_barrier((recv, packs))
    slots = exchanged(recv[:, :q], chans)
    co = coarse(me[None], slots, recv, codes, coarse_weight, coarse_bias[None])
    halos = exchanged(halo(fine_links, recv, q + codes, fine, q, vox), chans)
    cos = exchanged(co, chans)
    ff, sel, up_all = frames(me[None], owner[None], fine_links, packs, halos, co.shape[0])
    return refine(me[None], cos, ff, sel, up_all, fine_weight, fine_bias[None])


def solution(mesh):
    in_specs = (
        P("brick", "chan", None),
        P("brick", None),
        P("brick", None),
        P("brick"),
        P(None, None, "chan"),
        P(None, "chan", None),
        P(None, "chan", None),
        P(None, "chan", None),
        P("chan"),
        P("chan"),
    )
    return jax.shard_map(
        per_device,
        mesh=mesh,
        in_specs=in_specs,
        out_specs=P("brick", "chan", None),
        check_vma=False,
    )
```

```python
import numpy as np
import jax
import jax.numpy as jnp
from jax import lax
from jax.experimental import pallas as pl
from jax.experimental.pallas import tpu as pltpu
from jax.sharding import PartitionSpec as P

EDGE = 8
HALF = EDGE // 2
CUBE = HALF**3
FRAME = EDGE + 2
NBLK = 32
F32 = jnp.float32
BF16 = jnp.bfloat16
VMEM_LIMIT = 56 * 1024 * 1024


def headings():
    face_steps = [(1, 0, 0), (-1, 0, 0), (0, 1, 0), (0, -1, 0), (0, 0, 1), (0, 0, -1)]
    others = []
    for step_x in (-1, 0, 1):
        for step_y in (-1, 0, 1):
            for step_z in (-1, 0, 1):
                if abs(step_x) + abs(step_y) + abs(step_z) >= 2:
                    others.append((step_x, step_y, step_z))
    return face_steps + others


HEADINGS = headings()
HEADING_INDEX = {d: k for k, d in enumerate(HEADINGS)}
HEADING_INDEX[(0, 0, 0)] = len(HEADINGS)


def piece_lanes():
    order = sorted(
        range(len(HEADINGS)), key=lambda k: (sum(1 for e in HEADINGS[k] if e), k)
    )
    starts, voxels, at = [0] * len(HEADINGS), [None] * len(HEADINGS), 0
    for k in order:
        spans = [
            [0] if e == 1 else [EDGE - 1] if e == -1 else list(range(EDGE))
            for e in HEADINGS[k]
        ]
        voxels[k] = [
            (x * EDGE + y) * EDGE + z
            for x in spans[0]
            for y in spans[1]
            for z in spans[2]
        ]
        starts[k] = at
        at += len(voxels[k])
    return starts, voxels


STARTS, VOXELS = piece_lanes()
for k in (2, 3):
    VOXELS[k] = [VOXELS[k][x * EDGE + z] for z in range(EDGE) for x in range(EDGE)]
def octant_selector():
    sel = np.zeros((EDGE**3, EDGE**3), np.float32)
    for x in range(EDGE):
        for y in range(EDGE):
            for z in range(EDGE):
                o = (x % 2) * 4 + (y % 2) * 2 + z % 2
                u = ((x // 2) * HALF + y // 2) * HALF + z // 2
                sel[(x * EDGE + y) * EDGE + z, o * CUBE + u] = 1
    return sel


FACE = EDGE**2
FACES = 6
RIMS = len(HEADINGS) - FACES


def outer_selector():
    sel = np.zeros((EDGE**3, FACES * FACE + -(-RIMS * EDGE // 128) * 128), np.float32)
    for k in range(len(HEADINGS)):
        first = k * FACE if k < FACES else FACES * FACE + (k - FACES) * EDGE
        for i, v in enumerate(VOXELS[k]):
            sel[v, first + i] = 1
    return sel


def entry_tables(fine):
    wide = 128 // fine
    lanes = np.zeros((2, 128), np.int32)
    for b in range(fine):
        for k in range(len(HEADINGS)):
            face = k < FACES
            lanes[:, b * wide + k] = k * 128 if face else FACES * 128 + (k - FACES) * EDGE, face
    kind = lanes[1]
    earlier = (np.arange(128)[:, None] < np.arange(128)[None]) & (kind[:, None] == kind[None])
    return lanes, earlier.astype(np.float32)


def capacities(fine, owners):
    return -(-fine * FACES // owners), -(-fine * RIMS // owners)


def pair_selector():
    sel = np.zeros((256, 256), np.float32)
    for x in range(2):
        for y in range(8):
            for b in range(2):
                for z in range(8):
                    sel[((x * 8 + y) * 2 + b) * 8 + z, ((b * 2 + x) * 8 + y) * 8 + z] = 1
    return sel


def dot(a, b):
    return lax.dot_general(a, b, (((1,), (0,)), ((), ())), preferred_element_type=F32)


def dot_t(a, b):
    return lax.dot_general(a, b, (((1,), (1,)), ((), ())), preferred_element_type=F32)


def params():
    return pltpu.CompilerParams(vmem_limit_bytes=VMEM_LIMIT)


def cost(flops, moved):
    return pl.CostEstimate(flops=flops, bytes_accessed=moved, transcendentals=0)


VM = pltpu.VMEM
SM = pltpu.SMEM


def project_kernel(chans, me_ref, f_ref, sel_ref, w_ref, up_ref, *rest):
    outs, (chunk_ref, pack_ref, part) = rest[:chans], rest[chans:]
    q = w_ref.shape[1]
    rows, vox = f_ref.shape
    fine = rows // q
    x = f_ref[...]
    picked = dot(x, sel_ref[:, :vox]).astype(BF16)
    acc = None
    for o in range(8):
        z = jnp.concatenate(
            [picked[b * q : (b + 1) * q, o * CUBE : (o + 1) * CUBE] for b in range(fine)],
            axis=1,
        )
        term = lax.dot_general(
            w_ref[o], z, (((0,), (0,)), ((), ())), preferred_element_type=F32
        )
        acc = term if acc is None else acc + term
    part[...] = acc
    me = me_ref[0]
    for s in range(chans):
        outs[s][...] = part[pl.ds(pl.multiple_of((me ^ s) * q, q), q), :].astype(BF16)
    got = dot(x, sel_ref[:, vox:])
    low = lax.broadcasted_iota(jnp.int32, (rows, 128), 1) < FACE
    for i in range(FACES // 2):
        pair = got[:, 128 * i : 128 * i + 128]
        turned = pltpu.roll(pair, FACE, 1)
        chunk_ref[2 * i] = jnp.where(low, pair, turned).astype(BF16)
        chunk_ref[2 * i + 1] = jnp.where(low, turned, pair).astype(BF16)
    for i in range(FACES, chunk_ref.shape[0]):
        at = 128 * (i - FACES // 2)
        chunk_ref[i] = got[:, at : at + 128].astype(BF16)
    pack_ref[0:rows] = x
    more = up_ref.shape[0] * up_ref.shape[1] // vox
    for i in range(vox // up_ref.shape[1]):
        part_lanes = slice(i * up_ref.shape[1], (i + 1) * up_ref.shape[1])
        pack_ref[rows : rows + more, part_lanes] = up_ref[i * more : (i + 1) * more]


def project(me, features, down_weight, up_weight, chans):
    fine, q, vox = features.shape
    c_out = down_weight.shape[1]
    lanes = fine * CUBE
    ups = up_weight.reshape(-1, up_weight.shape[2])
    sel = np.concatenate([octant_selector(), outer_selector()], axis=1)
    chunks = (sel.shape[1] - vox) // 128 + FACES // 2
    res = pl.pallas_call(
        lambda *refs: project_kernel(chans, *refs),
        out_shape=[jax.ShapeDtypeStruct((q, lanes), BF16)] * chans
        + [
            jax.ShapeDtypeStruct((chunks, fine * q, 128), BF16),
            jax.ShapeDtypeStruct((fine * q + ups.size // vox, vox), BF16),
        ],
        in_specs=[pl.BlockSpec(memory_space=SM)] + [pl.BlockSpec(memory_space=VM)] * 4,
        out_specs=[pl.BlockSpec(memory_space=VM)] * (chans + 2),
        scratch_shapes=[pltpu.VMEM((c_out, lanes), F32)],
        compiler_params=params(),
        name="project",
    )(
        me,
        features.reshape(fine * q, vox),
        jnp.asarray(sel, BF16),
        jnp.transpose(down_weight, (0, 2, 1)),
        ups,
    )
    return res[:chans], res[chans], res[chans + 1]


def choose(
    fine, q, faces, rims, base, owner_ref, asked_refs, own_ref, lanes_ref, earlier_ref, chunk_ref,
    out_ref, from_ref, table, scalars, sem,
):
    owners = out_ref.shape[0]
    place = lanes_ref[0:1, :]
    is_face = lanes_ref[1:2, :] == 1
    wide = 128 // fine
    asked = jnp.concatenate(
        [
            jnp.concatenate([ref[:, b, :][:, :wide] for ref in asked_refs], axis=0)
            for b in range(fine)
        ],
        axis=1,
    )
    mask = (asked >= 0) & (lax.div(jnp.maximum(asked, 0), fine) == owner_ref[0])
    rank = dot(mask.astype(F32).astype(BF16), earlier_ref[...])
    slot = jnp.where(is_face, rank, rank + faces)
    code = (lax.rem(jnp.maximum(asked, 0), fine) * 1024 + place + 1).astype(F32)
    lane = lax.broadcasted_iota(jnp.int32, (owners, 128), 1)
    found = jnp.zeros((owners, 128), F32)
    for r in range(faces + rims):
        value = jnp.sum(jnp.where(mask & (slot == r), code, 0.0), axis=1, keepdims=True)
        found = jnp.where(lane == r, value, found)
    table[...] = found.astype(jnp.int32) - 1
    copy = pltpu.make_async_copy(table, scalars, sem)
    copy.start()
    own = jnp.concatenate([own_ref[b : b + 1, :wide] for b in range(fine)], axis=1)
    own = jnp.broadcast_to(own, (owners, 128))
    theirs = lax.div(jnp.maximum(own, 0), fine)
    mask = (own >= 0) & (theirs == lax.broadcasted_iota(jnp.int32, (owners, 128), 0))
    rank = dot(mask.astype(F32).astype(BF16), earlier_ref[...])
    at = jnp.where(is_face, rank * FACE, rank * EDGE + faces * FACE) + theirs.astype(F32) * 1024.0 + 1.0
    from_ref[...] = jnp.sum(jnp.where(mask, at, 0.0), axis=0, keepdims=True).astype(jnp.int32) - 1
    copy.wait()
    side = lax.broadcasted_iota(jnp.int32, (q, 128), 1)
    half = q // 2

    def one(r_owner, _):
        w = owner_ref[0] ^ r_owner
        for block in range((out_ref.shape[1] - base) // half):
            here = jnp.zeros((q, 128), F32)
            for r in range(faces + rims):
                pos = r * FACE if r < faces else faces * FACE + (r - faces) * EDGE
                if pos // 128 != block:
                    continue
                v = scalars[r_owner, r]
                safe = jnp.maximum(v, 0)
                b = lax.shift_right_logical(safe, 10)
                chunk = lax.shift_right_logical(safe, 7) & 7
                got = chunk_ref[chunk, pl.ds(pl.multiple_of(b * q, q), q), :].astype(F32)
                first = pos % 128
                size = FACE
                if r >= faces:
                    got = pltpu.roll(got, (first + 128 - (safe & 127)) & 127, 1)
                    size = EDGE
                here = jnp.where((side >= first) & (side < first + size) & (v >= 0), got, here)
            here = here.astype(BF16)
            for i in range(2):
                out_ref[w, base + block * half : base + (block + 1) * half, 128 * i : 128 * i + 128] = here[i * half : (i + 1) * half]
        return 0

    if owners <= 8:
        for w in range(owners):
            one(w, 0)
    else:
        lax.fori_loop(0, owners, one, 0)


def assemble_kernel(chans, asks, fine, faces, rims, owner_ref, links_ref, parents_ref, table_ref, *refs):
    slots, asked_refs, refs = refs[:chans], refs[chans : chans + asks], refs[chans + asks :]
    out_ref = refs[4]
    count, ways = links_ref.shape
    total = slots[0][...].astype(F32)
    for s in slots[1:]:
        total = total + s[...].astype(F32)
    q, lanes = slots[0].shape
    total = total.astype(BF16)
    rows = count * 8
    column, octant = table_ref[0], table_ref[1]
    row = lax.broadcasted_iota(jnp.int32, (rows, 128), 0)
    lane = lax.broadcasted_iota(jnp.int32, (rows, 128), 1)
    code = jnp.zeros((rows, 128), jnp.int32)
    for p in range(count):
        own = row // 8 == p
        for k in range(ways + 1):
            brick = owner_ref[0] * count + p if k == ways else links_ref[p, k]
            code = jnp.where(own & (column == k), jnp.where(brick >= 0, brick * 8 + octant + 1, 0), code)
    for b in range(parents_ref.shape[0]):
        code = jnp.where((row == b) & (lane == 27), parents_ref[b] + 1, code)
    high = lax.shift_right_logical(code, 7)
    digits = [high.astype(F32).astype(BF16), (code - high * 128).astype(F32).astype(BF16)]
    for w in range(out_ref.shape[0]):
        out_ref[w, 0:q, :] = total
        for i in range(2):
            out_ref[w, q : q + rows, 128 * i : 128 * i + 128] = digits[i]
    choose(fine, q, faces, rims, q + rows, owner_ref, asked_refs, *refs)


def assemble(slots, owner, coarse_links, parents, asked, own, chunks, owners):
    q, lanes = slots[0].shape
    count = coarse_links.shape[0]
    fine = parents.shape[0]
    columns, octants = octant_table()
    table = np.full((2, count * 8, 128), -1, np.int32)
    table[0, :, :27] = np.tile(columns, (count, 1))
    table[1, :, :27] = np.tile(octants, (count, 1))
    faces, rims = capacities(fine, owners)
    blocks = -(-(faces * FACE + rims * EDGE) // 128)
    entries, earlier = entry_tables(fine)
    return pl.pallas_call(
        lambda *refs: assemble_kernel(len(slots), len(asked), fine, faces, rims, *refs),
        out_shape=[
            jax.ShapeDtypeStruct((owners, q + count * 8 + blocks * q // 2, lanes), BF16),
            jax.ShapeDtypeStruct((1, 128), jnp.int32),
        ],
        in_specs=[pl.BlockSpec(memory_space=SM)] * 3 + [pl.BlockSpec(memory_space=VM)] * (len(slots) + len(asked) + 5),
        out_specs=[pl.BlockSpec(memory_space=VM)] * 2,
        scratch_shapes=[
            pltpu.VMEM((owners, 128), jnp.int32),
            pltpu.SMEM((owners, 128), jnp.int32),
            pltpu.SemaphoreType.DMA,
        ],
        compiler_params=params(),
        cost_estimate=cost(1024 * 1024, 12 * 1024 * 1024),
        name="assemble",
    )(
        owner, coarse_links, parents, jnp.asarray(table), *slots,
        *asked, own, jnp.asarray(entries), jnp.asarray(earlier, BF16), chunks,
    )


def partner(x, axis, step, count):
    return lax.ppermute(x, axis, [(i, i ^ step) for i in range(count)])


def exchanged(x, chans):
    return [x] + [partner(x, "chan", s, chans) for s in range(1, chans)]


def relayed(x, chans, meanwhile=lambda: None):
    slots, step, other = {0: x}, chans // 2, None
    while step:
        if step == 1:
            other = meanwhile()
            if other is not None:
                slots, other = lax.optimization_barrier((slots, other))
        for s in list(slots):
            slots[s | step] = partner(slots[s], "chan", step, chans)
        step //= 2
    return [slots[s] for s in range(chans)], other


def gathered(x, owners, between):
    have, step, count = [x], 1, 0
    while step < owners:
        now = jnp.concatenate(have, axis=0) if len(have) > 1 else have[0]
        if count < len(between):
            now = between[count](now)
        have = [now, partner(now, "brick", step, owners)]
        step *= 2
        count += 1
    return have


def halo_kernel(q, base, from_ref, recv_ref, out_ref):
    fine = out_ref.shape[0]
    half = q // 2
    lane = lax.broadcasted_iota(jnp.int32, (q, 128), 1)
    for b in range(fine):
        for chunk in range(out_ref.shape[2] // 128):
            here = jnp.zeros((q, 128), F32)
            for k in range(len(HEADINGS)):
                if STARTS[k] // 128 != chunk:
                    continue
                first = STARTS[k] % 128
                last = first + len(VOXELS[k])
                v = from_ref[0, b * (128 // fine) + k]
                safe = jnp.maximum(v, 0)
                w = lax.shift_right_logical(safe, 10)
                block = lax.shift_right_logical(safe, 7) & 7
                row = pl.multiple_of(base + block * half, 16)
                got = jnp.concatenate(
                    [recv_ref[w, pl.ds(row, half), 0:128], recv_ref[w, pl.ds(row, half), 128:256]], axis=0
                ).astype(F32)
                got = pltpu.roll(got, (first + 128 - (safe & 127)) & 127, 1)
                here = jnp.where((lane >= first) & (lane < last) & (v >= 0), got, here)
            out_ref[b, :, chunk * 128 : (chunk + 1) * 128] = here.astype(BF16)


def halo(places, recv, base, fine, q, vox):
    return pl.pallas_call(
        lambda *refs: halo_kernel(q, base, *refs),
        out_shape=jax.ShapeDtypeStruct((fine, q, vox), BF16),
        in_specs=[pl.BlockSpec(memory_space=SM), pl.BlockSpec(memory_space=VM)],
        out_specs=pl.BlockSpec(memory_space=VM),
        compiler_params=params(),
        name="halo",
    )(places, recv)


def axis_places(u):
    found = [(0, 1 + u)]
    if u == 0:
        found.append((1, HALF + 1))
    if u == HALF - 1:
        found.append((-1, 0))
    return found


def bias_column(row):
    n = row.shape[1]
    square = jnp.broadcast_to(row, (n, n))
    on = lax.broadcasted_iota(jnp.int32, (n, n), 0) == lax.broadcasted_iota(jnp.int32, (n, n), 1)
    return jnp.sum(jnp.where(on, square, 0.0), axis=1, keepdims=True)


def coarse_kernel(chans, codes, me_ref, *refs):
    slots, refs = refs[:chans], refs[chans:]
    recv_ref, w_ref, bias_ref, out_ref, proj_ref, rows_ref, sel_ref, nb_ref, parent_ref, table_ref = refs
    owners, q, lanes = slots[0].shape
    me = me_ref[0]
    fine = lanes // CUBE
    total = owners * fine

    def spread(w, _):
        block = jnp.concatenate([proj_ref[c, w] for c in range(chans)], axis=0)
        turned = block.astype(F32).T
        for b in range(fine):
            rows_ref[pl.ds(w * fine + b, CUBE, stride=total), :] = turned[b * CUBE : (b + 1) * CUBE]
        return 0

    @pl.when(pl.program_id(0) == 0)
    def _():
        for w in range(owners):
            digits = recv_ref[w, q : q + codes, :]
            table_ref[w * codes : (w + 1) * codes, :] = digits
            digits = digits.astype(F32)
            value = digits[:, 0:128] * 128.0 + digits[:, 128:256] - 1.0
            parent_ref[w * fine : (w + 1) * fine, :] = jnp.broadcast_to(value[0:fine, 27:28], (fine, 128))
        for s in range(chans):
            proj_ref[me ^ s] = slots[s][...]
        if owners <= 8:
            for w in range(owners):
                spread(w, 0)
        else:
            lax.fori_loop(0, owners, spread, 0)

    mine = parent_ref[pl.ds(pl.program_id(0) * NBLK, NBLK), :]
    row = lax.broadcasted_iota(jnp.int32, (NBLK, table_ref.shape[0]), 1).astype(F32)
    own = (mine[:, 0:1] == row).astype(F32).astype(BF16)
    digits = dot(own, table_ref[...])
    target = digits[:, 0:128] * 128.0 + digits[:, 128:256] - 1.0
    on = lax.broadcasted_iota(jnp.int32, (total, total), 0) == lax.broadcasted_iota(jnp.int32, (total, total), 1)
    parents = jnp.sum(jnp.where(on, parent_ref[:, 0:1], 0.0), axis=0, keepdims=True)
    for d in range(27):
        sel_ref[d * NBLK : (d + 1) * NBLK, :] = (target[:, d : d + 1] == parents).astype(F32).astype(BF16)
    for ux in range(HALF):
        for uy in range(HALF):
            for uz in range(HALF):
                places = [
                    (9 * (a[0] + 1) + 3 * (b[0] + 1) + c[0] + 1, a[1], b[1], c[1])
                    for a in axis_places(ux)
                    for b in axis_places(uy)
                    for c in axis_places(uz)
                ]
                u = (ux * HALF + uy) * HALF + uz
                source = rows_ref[u * total : (u + 1) * total, :].astype(BF16)
                picker = jnp.concatenate(
                    [sel_ref[d * NBLK : (d + 1) * NBLK, :] for d, _, _, _ in places], axis=0
                )
                got = dot(picker, source).astype(BF16)
                for i, (_, x, y, z) in enumerate(places):
                    nb_ref[x, y, z] = got[i * NBLK : (i + 1) * NBLK]
    span = HALF + 2
    size = span * HALF * HALF * NBLK
    acc = conv_rows(
        w_ref,
        lambda a2, a3: nb_ref[:, a2 : a2 + HALF, a3 : a3 + HALF].reshape(size, nb_ref.shape[4]),
    )
    step = HALF * HALF * NBLK
    n = HALF * step
    res = acc[0:q, 0:n] + acc[q : 2 * q, step : step + n] + acc[2 * q : 3 * q, 2 * step : 2 * step + n]
    out_ref[0] = jnp.maximum(res + bias_column(bias_ref[...]), 0.0).astype(BF16)


def conv_rows(w_ref, rows_of):
    taps = [(a2, a3) for a2 in range(3) for a3 in range(3)]
    acc = None
    for i in range(0, 9, 2):
        some = taps[i : i + 2]
        lhs = jnp.concatenate(
            [
                jnp.concatenate([w_ref[9 * a1 + 3 * a2 + a3] for a1 in range(3)], axis=0)
                for a2, a3 in some
            ],
            axis=1,
        )
        rhs = jnp.concatenate([rows_of(a2, a3) for a2, a3 in some], axis=1)
        term = dot_t(lhs, rhs)
        acc = term if acc is None else acc + term
    return acc


def coarse(me, slots, recv, codes, weight, bias):
    chans = len(slots)
    owners, q, lanes = slots[0].shape
    total = owners * lanes // CUBE
    blocks = total // NBLK
    c_in = weight.shape[2]
    whole = lambda a: pl.BlockSpec(a.shape, lambda i: (0,) * a.ndim)
    return pl.pallas_call(
        lambda *refs: coarse_kernel(chans, codes, *refs),
        out_shape=jax.ShapeDtypeStruct((blocks, q, CUBE * NBLK), BF16),
        grid=(blocks,),
        in_specs=[pl.BlockSpec(memory_space=SM)]
        + [whole(a) for a in slots]
        + [
            pl.BlockSpec((owners, q + codes, recv.shape[2]), lambda i: (0, 0, 0)),
            whole(weight),
            whole(bias),
        ],
        out_specs=pl.BlockSpec((1, q, CUBE * NBLK), lambda i: (i, 0, 0)),
        scratch_shapes=[
            pltpu.VMEM((chans, owners, q, lanes), BF16),
            pltpu.VMEM((CUBE * total, c_in), F32),
            pltpu.VMEM((27 * NBLK, total), BF16),
            pltpu.VMEM((HALF + 2, HALF + 2, HALF + 2, NBLK, c_in), BF16),
            pltpu.VMEM((total, 128), F32),
            pltpu.VMEM((owners * codes, 256), BF16),
        ],
        compiler_params=params(),
        cost_estimate=cost(2 * 27 * c_in * q * CUBE * total, 2 * 1024 * 1024),
        name="coarse",
    )(me, *slots, recv, weight, bias)


def frame_axis(f):
    if f == 0:
        return -1, EDGE - 1
    if f == FRAME - 1:
        return 1, 0
    return 0, f - 1


def frame_kernel(chans, me_ref, owner_ref, links_ref, *refs):
    packs, halos, refs = refs[:chans], refs[chans : 2 * chans], refs[2 * chans :]
    ff_ref, sel_ref, up_ref, both, inner, outer, plane = refs
    fine, q, vox = halos[0].shape
    owner = owner_ref[0]
    me = me_ref[0]
    for s in range(chans):
        at = pl.ds(pl.multiple_of((me ^ s) * q, q), q)
        for b in range(fine):
            both[0, b, at, :] = packs[s][b * q : (b + 1) * q, :]
            both[1, b, at, :] = halos[s][b]
        for o in range(8):
            row = (fine + o % 2) * q
            up_ref[o, at, :] = packs[s][row : row + q, o // 2 * 128 : o // 2 * 128 + 128]
    for b in range(fine):
        inner[b] = both[0, b].astype(F32).T
        outer[b] = both[1, b].astype(F32).T
    for b in range(fine):
        for s in range(2):
            dz = 2 * s - 1
            row = 2 * b + s
            for fx in range(FRAME):
                dx, vx = frame_axis(fx)
                start = STARTS[HEADING_INDEX[(dx, 0, dz)]] + (0 if dx else vx * EDGE)
                plane[pl.ds((fx * FRAME + 1) * 8 + row, EDGE, stride=8), :] = outer[b, start : start + EDGE, :]
            for fy in (0, FRAME - 1):
                dy = frame_axis(fy)[0]
                start = STARTS[HEADING_INDEX[(0, dy, dz)]]
                plane[pl.ds((FRAME + fy) * 8 + row, EDGE, stride=8 * FRAME), :] = outer[b, start : start + EDGE, :]
                for fx in (0, FRAME - 1):
                    start = STARTS[HEADING_INDEX[(frame_axis(fx)[0], dy, dz)]]
                    plane[pl.ds((fx * FRAME + fy) * 8 + row, 1), :] = outer[b, start : start + 1, :]
    for fx in range(FRAME):
        for fy in range(FRAME):
            dx, vx = frame_axis(fx)
            dy, vy = frame_axis(fy)
            at = ((1 - fx % 2) * 2 + 1 - fy % 2) * 25 + (fx // 2) * 5 + fy // 2
            tiles = []
            for b in range(fine):
                if dx == 0 and dy == 0:
                    start = (vx * EDGE + vy) * EDGE
                    tiles.append(inner[b, start : start + EDGE, :])
                else:
                    start = STARTS[HEADING_INDEX[(dx, dy, 0)]]
                    if dx == 0:
                        tiles.append(outer[b, pl.ds(start + vx, EDGE, stride=EDGE), :])
                    else:
                        start += 0 if dy else vy * EDGE
                        tiles.append(outer[b, start : start + EDGE, :])
            tiles.append(plane[(fx * FRAME + fy) * 8 : (fx * FRAME + fy) * 8 + 8, :])
            tiles.append(jnp.zeros((8, plane.shape[1]), F32))
            ff_ref[at] = jnp.concatenate(tiles, axis=0).astype(BF16)
    blocks = sel_ref.shape[0]
    lane = lax.broadcasted_iota(jnp.int32, (8, 128), 1)
    row = lax.broadcasted_iota(jnp.int32, (8, 128), 0)

    def pick(j, _):
        for dx in (-1, 0, 1):
            for dy in (-1, 0, 1):
                def brick(b, dz):
                    k = HEADING_INDEX[(dx, dy, dz)]
                    n = owner * fine + b if k == len(HEADINGS) else links_ref[b, k]
                    n = n - j * NBLK
                    return jnp.where((n >= 0) & (n < NBLK), n, -1024)

                tiles = []
                for b in range(fine):
                    tiles.append((lane - (row // 2) * NBLK == brick(b, 0)).astype(F32))
                low = jnp.full((8, 128), -1024, jnp.int32)
                for b in range(fine):
                    for s in range(2):
                        n = brick(b, 2 * s - 1) + (HALF - 1) * (1 - s) * NBLK
                        low = jnp.where(row == 2 * b + s, n, low)
                tiles.append((lane == low).astype(F32))
                tiles.append(jnp.zeros((8, 128), F32))
                sel_ref[j, 3 * (dx + 1) + dy + 1] = jnp.concatenate(tiles, axis=0).astype(BF16)
        return 0

    if blocks == 1:
        pick(0, 0)
    else:
        lax.fori_loop(0, blocks, pick, 0)


def frames(me, owner, links, packs, halos, blocks):
    chans = len(packs)
    fine, q, vox = halos[0].shape
    rows = 8 * fine + 16
    c_all = chans * q
    return pl.pallas_call(
        lambda *refs: frame_kernel(chans, *refs),
        out_shape=[
            jax.ShapeDtypeStruct((FRAME * FRAME, rows, c_all), BF16),
            jax.ShapeDtypeStruct((blocks, 9, rows, 128), BF16),
            jax.ShapeDtypeStruct((8, c_all, c_all), BF16),
        ],
        in_specs=[pl.BlockSpec(memory_space=SM)] * 3 + [pl.BlockSpec(memory_space=VM)] * (2 * chans),
        out_specs=[pl.BlockSpec(memory_space=VM)] * 3,
        scratch_shapes=[
            pltpu.VMEM((2, fine, c_all, vox), BF16),
            pltpu.VMEM((fine, vox, c_all), F32),
            pltpu.VMEM((fine, vox, c_all), F32),
            pltpu.VMEM((FRAME * FRAME * 8, c_all), F32),
        ],
        compiler_params=params(),
        name="frames",
    )(me, owner, links, *packs, *halos)


def fine_kernel(chans, me_ref, *refs):
    slots, refs = refs[:chans], refs[chans:]
    ff_ref, sel_ref, up_ref, w_ref, bias_ref, pair_ref, out_ref, co_ref, cr, g3 = refs
    blocks, q, _ = slots[0].shape
    c_all = chans * q
    for s in range(chans):
        co_ref[me_ref[0] ^ s] = slots[s][...]
    fine = out_ref.shape[0]
    rows = ff_ref.shape[1]
    for ux in range(HALF):
        for uy in range(HALF):
            places = [
                (3 * (a[0] + 1) + b[0] + 1, a[1], b[1])
                for a in axis_places(ux)
                for b in axis_places(uy)
            ]
            col = (ux * HALF + uy) * 128

            def part(j):
                source = jnp.concatenate(
                    [co_ref[c, j, :, col : col + 128] for c in range(chans)], axis=0
                )
                picker = jnp.concatenate([sel_ref[j, d] for d, _, _ in places], axis=0)
                return dot_t(picker, source)

            if blocks == 1:
                got = part(0)
            else:
                got = lax.fori_loop(
                    0,
                    blocks,
                    lambda j, a: a + part(j),
                    jnp.zeros((len(places) * rows, c_all), F32),
                )
            got = got.astype(BF16)
            for i, (_, x, y) in enumerate(places):
                cr[x, y] = got[i * rows : (i + 1) * rows]
    r = lax.broadcasted_iota(jnp.int32, (rows, c_all), 0)
    odd = (r % 2 == 1) ^ (r >= 8 * fine)
    sub = lax.broadcasted_iota(jnp.int32, (5, 8, c_all), 1)
    for px in range(2):
        for py in range(2):
            lift = jnp.concatenate([up_ref[4 * px + 2 * py], up_ref[4 * px + 2 * py + 1]], axis=0)
            for i in range(5):
                x = i + 1 - px
                src = cr[x, 1 - py : 6 - py].reshape(5 * rows, c_all)
                both = dot_t(src, lift).reshape(5, rows, 2 * c_all)
                up = jnp.where(odd[None], both[:, :, c_all:], both[:, :, :c_all])
                at = (px * 2 + py) * 25 + i * 5
                merged = (ff_ref[at : at + 5].astype(F32) + up).astype(BF16).astype(F32)
                fx = 2 * i + 1 - px
                plane = merged[:, 8 * fine : 8 * fine + 8, :]
                for pair in range(fine // 2):
                    made = [[], [], []]
                    for h in range(2):
                        b = 2 * pair + h
                        mid = merged[:, 8 * b : 8 * b + 8, :]
                        made[0].append(
                            jnp.where(
                                sub == 0,
                                pltpu.roll(plane, (8 - 2 * b) % 8, 1),
                                pltpu.roll(mid, 1, 1),
                            )
                        )
                        made[1].append(mid)
                        made[2].append(
                            jnp.where(
                                sub == 7,
                                pltpu.roll(plane, 7 - (2 * b + 1), 1),
                                pltpu.roll(mid, 7, 1),
                            )
                        )
                    for a3 in range(3):
                        tile = jnp.concatenate(made[a3], axis=1).astype(BF16)
                        for j in range(5):
                            g3[a3, pair, fx, 2 * j + 1 - py] = tile[j]
    step = EDGE * 2 * EDGE
    n = EDGE * step
    bias = bias_column(bias_ref[...])
    for pair in range(fine // 2):
        acc = conv_rows(
            w_ref,
            lambda a2, a3: g3[a3, pair, :, a2 : a2 + EDGE].reshape(FRAME * step, c_all),
        )
        res = acc[0:q, 0:n] + acc[q : 2 * q, step : step + n] + acc[2 * q : 3 * q, 2 * step : 2 * step + n]
        res = jnp.maximum(res + bias, 0.0).astype(BF16)
        for h in range(n // 256):
            turned = dot(res[:, 256 * h : 256 * h + 256], pair_ref[...]).astype(BF16)
            for b in range(2):
                out_ref[2 * pair + b, :, 128 * h : 128 * h + 128] = turned[:, 128 * b : 128 * b + 128]


def refine(me, slots, ff, sel, up_weight, weight, bias):
    chans = len(slots)
    blocks, q, wide = slots[0].shape
    rows = ff.shape[1]
    fine = (rows - 16) // 8
    c_all = chans * q
    return pl.pallas_call(
        lambda *refs: fine_kernel(chans, *refs),
        out_shape=jax.ShapeDtypeStruct((fine, q, EDGE**3), BF16),
        in_specs=[pl.BlockSpec(memory_space=SM)] + [pl.BlockSpec(memory_space=VM)] * (chans + 6),
        out_specs=pl.BlockSpec(memory_space=VM),
        scratch_shapes=[
            pltpu.VMEM((chans, blocks, q, wide), BF16),
            pltpu.VMEM((HALF + 2, HALF + 2, rows, c_all), BF16),
            pltpu.VMEM((3, fine // 2, FRAME, FRAME, 2 * EDGE, c_all), BF16),
        ],
        compiler_params=params(),
        cost_estimate=cost(2 * 27 * c_all * q * fine * EDGE**3, 4 * 1024 * 1024),
        name="refine",
    )(me, *slots, ff, sel, up_weight, weight, bias, jnp.asarray(pair_selector(), BF16))


def octant_table():
    columns = np.zeros((8, 27), np.int32)
    octants = np.zeros((8, 27), np.int32)
    for o in range(8):
        bits = (o >> 2 & 1, o >> 1 & 1, o & 1)
        for d in range(27):
            go = (d // 9 - 1, d // 3 % 3 - 1, d % 3 - 1)
            cross, land = [], []
            for bit, g in zip(bits, go):
                t = bit + g
                cross.append(-1 if t < 0 else 1 if t > 1 else 0)
                land.append(t % 2)
            columns[o, d] = HEADING_INDEX[tuple(cross)]
            octants[o, d] = land[0] * 4 + land[1] * 2 + land[2]
    return columns, octants


def per_device(
    features,
    fine_links,
    coarse_links,
    parents,
    down_weight,
    coarse_weight,
    up_weight,
    fine_weight,
    coarse_bias,
    fine_bias,
):
    owners = lax.axis_size("brick")
    chans = lax.axis_size("chan")
    owner = lax.axis_index("brick").astype(jnp.int32)
    me = lax.axis_index("chan").astype(jnp.int32)
    fine, q, vox = features.shape
    own = jnp.pad(fine_links, ((0, -fine % 8), (0, 128 - fine_links.shape[1])), constant_values=-1)
    parts, chunks, packed = project(me[None], features, down_weight, up_weight, chans)
    done = {}

    def projected(now):
        now, done["parts"] = lax.optimization_barrier((now, parts))
        return now

    def reduced(now):
        blocks = done["parts"]
        arrived = [blocks[0]] + [partner(blocks[s], "chan", s, chans) for s in range(1, chans)]
        now, arrived[1] = lax.optimization_barrier((now, arrived[1]))
        done["arrived"] = arrived
        return now

    asked = gathered(own[None], owners, [lambda now: now, projected, reduced])
    arrived = done["arrived"]
    codes = 8 * coarse_links.shape[0]
    sending, places = assemble(arrived, owner[None], coarse_links, parents, asked, own, chunks, owners)
    recv = lax.all_to_all(sending, "brick", split_axis=0, concat_axis=0, tiled=True)
    packs, _ = relayed(packed, chans)
    recv, packs = lax.optimization_barrier((recv, packs))
    slots, around = relayed(recv[:, :q], chans, lambda: halo(places, recv, q + codes, fine, q, vox))
    slots, around = lax.optimization_barrier((slots, around))
    halos, co = relayed(
        around,
        chans,
        lambda: coarse(me[None], slots, recv, codes, coarse_weight, coarse_bias[None]),
    )
    cos, (ff, sel, up_all) = relayed(
        co,
        chans,
        lambda: frames(me[None], owner[None], fine_links, packs, halos, co.shape[0]),
    )
    return refine(me[None], cos, ff, sel, up_all, fine_weight, fine_bias[None])


def solution(mesh):
    in_specs = (
        P("brick", "chan", None),
        P("brick", None),
        P("brick", None),
        P("brick"),
        P(None, None, "chan"),
        P(None, "chan", None),
        P(None, "chan", None),
        P(None, "chan", None),
        P("chan"),
        P("chan"),
    )
    return jax.shard_map(
        per_device,
        mesh=mesh,
        in_specs=in_specs,
        out_specs=P("brick", "chan", None),
        check_vma=False,
    )
```

```python
import numpy as np
import jax
import jax.numpy as jnp
from jax import lax
from jax.experimental import pallas as pl
from jax.experimental.pallas import tpu as pltpu
from jax.sharding import PartitionSpec as P

EDGE = 8
HALF = EDGE // 2
CUBE = HALF**3
FRAME = EDGE + 2
NBLK = 32
F32 = jnp.float32
BF16 = jnp.bfloat16
META = 96
VMEM_LIMIT = 56 * 1024 * 1024


def headings():
    face_steps = [(1, 0, 0), (-1, 0, 0), (0, 1, 0), (0, -1, 0), (0, 0, 1), (0, 0, -1)]
    others = []
    for step_x in (-1, 0, 1):
        for step_y in (-1, 0, 1):
            for step_z in (-1, 0, 1):
                if abs(step_x) + abs(step_y) + abs(step_z) >= 2:
                    others.append((step_x, step_y, step_z))
    return face_steps + others


HEADINGS = headings()
HEADING_INDEX = {d: k for k, d in enumerate(HEADINGS)}
HEADING_INDEX[(0, 0, 0)] = len(HEADINGS)


def piece_lanes():
    order = sorted(
        range(len(HEADINGS)), key=lambda k: (sum(1 for e in HEADINGS[k] if e), k)
    )
    starts, voxels, at = [0] * len(HEADINGS), [None] * len(HEADINGS), 0
    for k in order:
        spans = [
            [0] if e == 1 else [EDGE - 1] if e == -1 else list(range(EDGE))
            for e in HEADINGS[k]
        ]
        voxels[k] = [
            (x * EDGE + y) * EDGE + z
            for x in spans[0]
            for y in spans[1]
            for z in spans[2]
        ]
        starts[k] = at
        at += len(voxels[k])
    return starts, voxels


STARTS, VOXELS = piece_lanes()
for k in (2, 3):
    VOXELS[k] = [VOXELS[k][x * EDGE + z] for z in range(EDGE) for x in range(EDGE)]
def octant_selector():
    sel = np.zeros((EDGE**3, EDGE**3), np.float32)
    for x in range(EDGE):
        for y in range(EDGE):
            for z in range(EDGE):
                o = (x % 2) * 4 + (y % 2) * 2 + z % 2
                u = ((x // 2) * HALF + y // 2) * HALF + z // 2
                sel[(x * EDGE + y) * EDGE + z, o * CUBE + u] = 1
    return sel


FACE = EDGE**2
FACES = 6
RIMS = len(HEADINGS) - FACES


def outer_selector():
    sel = np.zeros((EDGE**3, FACES * FACE + -(-RIMS * EDGE // 128) * 128), np.float32)
    for k in range(len(HEADINGS)):
        first = k * FACE if k < FACES else FACES * FACE + (k - FACES) * EDGE
        for i, v in enumerate(VOXELS[k]):
            sel[v, first + i] = 1
    return sel


def entry_tables(fine):
    wide = 128 // fine
    lanes = np.zeros((2, 128), np.int32)
    for b in range(fine):
        for k in range(len(HEADINGS)):
            face = k < FACES
            lanes[:, b * wide + k] = k * 128 if face else FACES * 128 + (k - FACES) * EDGE, face
    kind = lanes[1]
    earlier = (np.arange(128)[:, None] < np.arange(128)[None]) & (kind[:, None] == kind[None])
    return lanes, earlier.astype(np.float32)


def capacities(fine, owners):
    return -(-fine * FACES // owners), -(-fine * RIMS // owners)


def pair_selector():
    sel = np.zeros((256, 256), np.float32)
    for x in range(2):
        for y in range(8):
            for b in range(2):
                for z in range(8):
                    sel[((x * 8 + y) * 2 + b) * 8 + z, ((b * 2 + x) * 8 + y) * 8 + z] = 1
    return sel


def dot(a, b):
    return lax.dot_general(a, b, (((1,), (0,)), ((), ())), preferred_element_type=F32)


def dot_t(a, b):
    return lax.dot_general(a, b, (((1,), (1,)), ((), ())), preferred_element_type=F32)


def params():
    return pltpu.CompilerParams(vmem_limit_bytes=VMEM_LIMIT)


def cost(flops, moved):
    return pl.CostEstimate(flops=flops, bytes_accessed=moved, transcendentals=0)


VM = pltpu.VMEM
SM = pltpu.SMEM


def project_kernel(chans, me_ref, f_ref, sel_ref, w_ref, up_ref, *rest):
    outs, (chunk_ref, pack_ref, part) = rest[:chans], rest[chans:]
    q = w_ref.shape[1]
    rows, vox = f_ref.shape
    fine = rows // q
    x = f_ref[...]
    picked = dot(x, sel_ref[:, :vox]).astype(BF16)
    acc = None
    for o in range(8):
        z = jnp.concatenate(
            [picked[b * q : (b + 1) * q, o * CUBE : (o + 1) * CUBE] for b in range(fine)],
            axis=1,
        )
        term = lax.dot_general(
            w_ref[o], z, (((0,), (0,)), ((), ())), preferred_element_type=F32
        )
        acc = term if acc is None else acc + term
    part[...] = acc
    me = me_ref[0]
    for s in range(chans):
        outs[s][...] = part[pl.ds(pl.multiple_of((me ^ s) * q, q), q), :].astype(BF16)
    got = dot(x, sel_ref[:, vox:])
    low = lax.broadcasted_iota(jnp.int32, (rows, 128), 1) < FACE
    for i in range(FACES // 2):
        pair = got[:, 128 * i : 128 * i + 128]
        turned = pltpu.roll(pair, FACE, 1)
        chunk_ref[2 * i] = jnp.where(low, pair, turned).astype(BF16)
        chunk_ref[2 * i + 1] = jnp.where(low, turned, pair).astype(BF16)
    for i in range(FACES, chunk_ref.shape[0]):
        at = 128 * (i - FACES // 2)
        chunk_ref[i] = got[:, at : at + 128].astype(BF16)
    pack_ref[0:rows] = x
    more = up_ref.shape[0] * up_ref.shape[1] // vox
    for i in range(vox // up_ref.shape[1]):
        part_lanes = slice(i * up_ref.shape[1], (i + 1) * up_ref.shape[1])
        pack_ref[rows : rows + more, part_lanes] = up_ref[i * more : (i + 1) * more]


def project(me, features, down_weight, up_weight, chans):
    fine, q, vox = features.shape
    c_out = down_weight.shape[1]
    lanes = fine * CUBE
    ups = up_weight.reshape(-1, up_weight.shape[2])
    sel = np.concatenate([octant_selector(), outer_selector()], axis=1)
    chunks = (sel.shape[1] - vox) // 128 + FACES // 2
    res = pl.pallas_call(
        lambda *refs: project_kernel(chans, *refs),
        out_shape=[jax.ShapeDtypeStruct((q, lanes), BF16)] * chans
        + [
            jax.ShapeDtypeStruct((chunks, fine * q, 128), BF16),
            jax.ShapeDtypeStruct((fine * q + ups.size // vox, vox), BF16),
        ],
        in_specs=[pl.BlockSpec(memory_space=SM)] + [pl.BlockSpec(memory_space=VM)] * 4,
        out_specs=[pl.BlockSpec(memory_space=VM)] * (chans + 2),
        scratch_shapes=[pltpu.VMEM((c_out, lanes), F32)],
        compiler_params=params(),
        name="project",
    )(
        me,
        features.reshape(fine * q, vox),
        jnp.asarray(sel, BF16),
        jnp.transpose(down_weight, (0, 2, 1)),
        ups,
    )
    return res[:chans], res[chans], res[chans + 1]


def padded(rows, wide):
    return jnp.concatenate([rows, jnp.full((rows.shape[0], wide - rows.shape[1]), -1, jnp.int32)], axis=1)


def choose(
    fine, q, faces, rims, digits, owner_ref, asked_refs, own_ref, lanes_ref, earlier_ref, chunk_ref,
    out_ref, from_ref, table, scalars, sem,
):
    order = xor_order(out_ref.shape[0])
    owners = out_ref.shape[0]
    place = lanes_ref[0:1, :]
    is_face = lanes_ref[1:2, :] == 1
    wide = 128 // fine
    asked = jnp.concatenate(
        [
            jnp.concatenate([padded(ref[:, b, :], wide) for ref in asked_refs], axis=0)
            for b in range(fine)
        ],
        axis=1,
    )
    mask = (asked >= 0) & (lax.div(jnp.maximum(asked, 0), fine) == owner_ref[0])
    rank = dot(mask.astype(F32).astype(BF16), earlier_ref[...])
    slot = jnp.where(is_face, rank, rank + faces)
    code = (lax.rem(jnp.maximum(asked, 0), fine) * 1024 + place + 1).astype(F32)
    lane = lax.broadcasted_iota(jnp.int32, (owners, 128), 1)
    found = jnp.zeros((owners, 128), F32)
    for r in range(faces + rims):
        value = jnp.sum(jnp.where(mask & (slot == r), code, 0.0), axis=1, keepdims=True)
        found = jnp.where(lane == r, value, found)
    table[...] = found.astype(jnp.int32) - 1
    copy = pltpu.make_async_copy(table, scalars, sem)
    copy.start()
    own = jnp.concatenate([padded(own_ref[b : b + 1, :], wide) for b in range(fine)], axis=1)
    own = jnp.broadcast_to(own, (owners, 128))
    theirs = lax.div(jnp.maximum(own, 0), fine)
    mask = (own >= 0) & (theirs == lax.broadcasted_iota(jnp.int32, (owners, 128), 0))
    rank = dot(mask.astype(F32).astype(BF16), earlier_ref[...])
    at = jnp.where(is_face, rank * FACE, rank * EDGE + faces * FACE) + theirs.astype(F32) * 1024.0 + 1.0
    from_ref[...] = jnp.sum(jnp.where(mask, at, 0.0), axis=0, keepdims=True).astype(jnp.int32) - 1
    copy.wait()
    side = lax.broadcasted_iota(jnp.int32, (q, 128), 1)
    half = q // 2

    def one(r_owner, _):
        w = owner_ref[0] ^ (order[r_owner] if owners <= 8 else reversed_bits(r_owner, owners))
        blocks = (out_ref.shape[1] - q) // half
        for block in range(blocks):
            here = jnp.zeros((q, 128), F32)
            for r in range(faces + rims):
                pos = r * FACE if r < faces else faces * FACE + (r - faces) * EDGE
                if pos // 128 != block:
                    continue
                v = scalars[r_owner, r]
                safe = jnp.maximum(v, 0)
                b = lax.shift_right_logical(safe, 10)
                chunk = lax.shift_right_logical(safe, 7) & 7
                got = chunk_ref[chunk, pl.ds(pl.multiple_of(b * q, q), q), :].astype(F32)
                first = pos % 128
                size = FACE
                if r >= faces:
                    got = pltpu.roll(got, (first + 128 - (safe & 127)) & 127, 1)
                    size = EDGE
                here = jnp.where((side >= first) & (side < first + size) & (v >= 0), got, here)
            at = q + block * half
            for i in range(2):
                part = here[i * half : (i + 1) * half]
                if block == blocks - 1:
                    part = part + digits[i]
                out_ref[w, at : at + half, 128 * i : 128 * i + 128] = part.astype(BF16)
        return 0

    if owners <= 8:
        for w in range(owners):
            one(w, 0)
    else:
        lax.fori_loop(0, owners, one, 0)


def assemble_kernel(chans, asks, fine, faces, rims, owner_ref, links_ref, parents_ref, table_ref, *refs):
    slots, asked_refs, refs = refs[:chans], refs[chans : chans + asks], refs[chans + asks :]
    out_ref = refs[4]
    count, ways = links_ref.shape
    total = slots[0][...].astype(F32)
    for s in slots[1:]:
        total = total + s[...].astype(F32)
    q, lanes = slots[0].shape
    total = total.astype(BF16)
    rows = count * 8
    column, octant = table_ref[0], table_ref[1]
    row = lax.broadcasted_iota(jnp.int32, (rows, 128), 0)
    lane = lax.broadcasted_iota(jnp.int32, (rows, 128), 1)
    code = jnp.zeros((rows, 128), jnp.int32)
    for p in range(count):
        own = row // 8 == p
        for k in range(ways + 1):
            brick = owner_ref[0] * count + p if k == ways else links_ref[p, k]
            code = jnp.where(own & (column == k), jnp.where(brick >= 0, brick * 8 + octant + 1, 0), code)
    for b in range(parents_ref.shape[0]):
        code = jnp.where((row == b) & (lane == META + 27), parents_ref[b] + 1, code)
    high = lax.shift_right_logical(code, 7)
    digits = [high.astype(F32), (code - high * 128).astype(F32)]
    for w in range(out_ref.shape[0]):
        out_ref[w, 0:q, :] = total
    choose(fine, q, faces, rims, digits, owner_ref, asked_refs, *refs)


def assemble(slots, owner, coarse_links, parents, asked, own, chunks, owners):
    q, lanes = slots[0].shape
    count = coarse_links.shape[0]
    fine = parents.shape[0]
    columns, octants = octant_table()
    table = np.full((2, count * 8, 128), -1, np.int32)
    table[0, :, META : META + 27] = np.tile(columns, (count, 1))
    table[1, :, META : META + 27] = np.tile(octants, (count, 1))
    faces, rims = capacities(fine, owners)
    blocks = -(-(faces * FACE + rims * EDGE) // 128)
    assert count * 8 == q // 2 and (faces * FACE + rims * EDGE - 1) % 128 < META
    entries, earlier = entry_tables(fine)
    return pl.pallas_call(
        lambda *refs: assemble_kernel(len(slots), len(asked), fine, faces, rims, *refs),
        out_shape=[
            jax.ShapeDtypeStruct((owners, q + blocks * q // 2, lanes), BF16),
            jax.ShapeDtypeStruct((1, 128), jnp.int32),
        ],
        in_specs=[pl.BlockSpec(memory_space=SM)] * 3 + [pl.BlockSpec(memory_space=VM)] * (len(slots) + len(asked) + 5),
        out_specs=[pl.BlockSpec(memory_space=VM)] * 2,
        scratch_shapes=[
            pltpu.VMEM((owners, 128), jnp.int32),
            pltpu.SMEM((owners, 128), jnp.int32),
            pltpu.SemaphoreType.DMA,
        ],
        compiler_params=params(),
        cost_estimate=cost(1024 * 1024, 12 * 1024 * 1024),
        name="assemble",
    )(
        owner, coarse_links, parents, jnp.asarray(table), *slots,
        *asked, own, jnp.asarray(entries), jnp.asarray(earlier, BF16), chunks,
    )


def partner(x, axis, step, count):
    return lax.ppermute(x, axis, [(i, i ^ step) for i in range(count)])


def exchanged(x, chans):
    return [x] + [partner(x, "chan", s, chans) for s in range(1, chans)]


def relayed(x, chans, meanwhile=lambda: None):
    slots, step, other = {0: x}, chans // 2, None
    while step:
        if step == 1:
            other = meanwhile()
            if other is not None:
                slots, other = lax.optimization_barrier((slots, other))
        for s in list(slots):
            slots[s | step] = partner(slots[s], "chan", step, chans)
        step //= 2
    return [slots[s] for s in range(chans)], other


def reversed_bits(r, count):
    out, bit = 0, 1
    while bit < count:
        out = out * 2 + r % 2
        r = r // 2
        bit *= 2
    return out


def xor_order(count):
    return [reversed_bits(r, count) for r in range(count)]


def gathered(x, owners, between):
    have, step, count = [x], owners // 2, 0
    while step:
        now = jnp.concatenate(have, axis=0) if len(have) > 1 else have[0]
        if count < len(between):
            now = between[count](now)
        have = [now, partner(now, "brick", step, owners)]
        step //= 2
        count += 1
    return have


def halo_kernel(q, base, from_ref, recv_ref, out_ref):
    fine = out_ref.shape[0]
    half = q // 2
    lane = lax.broadcasted_iota(jnp.int32, (q, 128), 1)
    for b in range(fine):
        for chunk in range(out_ref.shape[2] // 128):
            here = jnp.zeros((q, 128), F32)
            for k in range(len(HEADINGS)):
                if STARTS[k] // 128 != chunk:
                    continue
                first = STARTS[k] % 128
                last = first + len(VOXELS[k])
                v = from_ref[0, b * (128 // fine) + k]
                safe = jnp.maximum(v, 0)
                w = lax.shift_right_logical(safe, 10)
                block = lax.shift_right_logical(safe, 7) & 7
                row = pl.multiple_of(base + block * half, 16)
                got = jnp.concatenate(
                    [recv_ref[w, pl.ds(row, half), 0:128], recv_ref[w, pl.ds(row, half), 128:256]], axis=0
                ).astype(F32)
                got = pltpu.roll(got, (first + 128 - (safe & 127)) & 127, 1)
                here = jnp.where((lane >= first) & (lane < last) & (v >= 0), got, here)
            out_ref[b, :, chunk * 128 : (chunk + 1) * 128] = here.astype(BF16)


def halo(places, recv, base, fine, q, vox):
    return pl.pallas_call(
        lambda *refs: halo_kernel(q, base, *refs),
        out_shape=jax.ShapeDtypeStruct((fine, q, vox), BF16),
        in_specs=[pl.BlockSpec(memory_space=SM), pl.BlockSpec(memory_space=VM)],
        out_specs=pl.BlockSpec(memory_space=VM),
        compiler_params=params(),
        name="halo",
    )(places, recv)


def axis_places(u):
    found = [(0, 1 + u)]
    if u == 0:
        found.append((1, HALF + 1))
    if u == HALF - 1:
        found.append((-1, 0))
    return found


def bias_column(row):
    n = row.shape[1]
    square = jnp.broadcast_to(row, (n, n))
    on = lax.broadcasted_iota(jnp.int32, (n, n), 0) == lax.broadcasted_iota(jnp.int32, (n, n), 1)
    return jnp.sum(jnp.where(on, square, 0.0), axis=1, keepdims=True)


def coarse_kernel(chans, codes, me_ref, *refs):
    slots, refs = refs[:chans], refs[chans:]
    recv_ref, w_ref, bias_ref, out_ref, proj_ref, rows_ref, sel_ref, nb_ref, parent_ref, table_ref = refs
    owners, q, lanes = slots[0].shape
    me = me_ref[0]
    fine = lanes // CUBE
    total = owners * fine

    def spread(w, _):
        block = jnp.concatenate([proj_ref[c, w] for c in range(chans)], axis=0)
        turned = block.astype(F32).T
        for b in range(fine):
            rows_ref[pl.ds(w * fine + b, CUBE, stride=total), :] = turned[b * CUBE : (b + 1) * CUBE]
        return 0

    @pl.when(pl.program_id(0) == 0)
    def _():
        for w in range(owners):
            digits = recv_ref[w]
            table_ref[w * codes : (w + 1) * codes, :] = digits
            digits = digits.astype(F32)
            value = digits[:, 0:128] * 128.0 + digits[:, 128:256] - 1.0
            parent_ref[w * fine : (w + 1) * fine, :] = jnp.broadcast_to(value[0:fine, META + 27 : META + 28], (fine, 128))
        for s in range(chans):
            proj_ref[me ^ s] = slots[s][...]
        if owners <= 8:
            for w in range(owners):
                spread(w, 0)
        else:
            lax.fori_loop(0, owners, spread, 0)

    mine = parent_ref[pl.ds(pl.program_id(0) * NBLK, NBLK), :]
    row = lax.broadcasted_iota(jnp.int32, (NBLK, table_ref.shape[0]), 1).astype(F32)
    own = (mine[:, 0:1] == row).astype(F32).astype(BF16)
    digits = dot(own, table_ref[...])
    target = digits[:, 0:128] * 128.0 + digits[:, 128:256] - 1.0
    on = lax.broadcasted_iota(jnp.int32, (total, total), 0) == lax.broadcasted_iota(jnp.int32, (total, total), 1)
    parents = jnp.sum(jnp.where(on, parent_ref[:, 0:1], 0.0), axis=0, keepdims=True)
    for d in range(27):
        sel_ref[d * NBLK : (d + 1) * NBLK, :] = (target[:, META + d : META + d + 1] == parents).astype(F32).astype(BF16)
    for ux in range(HALF):
        for uy in range(HALF):
            for uz in range(HALF):
                places = [
                    (9 * (a[0] + 1) + 3 * (b[0] + 1) + c[0] + 1, a[1], b[1], c[1])
                    for a in axis_places(ux)
                    for b in axis_places(uy)
                    for c in axis_places(uz)
                ]
                u = (ux * HALF + uy) * HALF + uz
                source = rows_ref[u * total : (u + 1) * total, :].astype(BF16)
                picker = jnp.concatenate(
                    [sel_ref[d * NBLK : (d + 1) * NBLK, :] for d, _, _, _ in places], axis=0
                )
                got = dot(picker, source).astype(BF16)
                for i, (_, x, y, z) in enumerate(places):
                    nb_ref[x, y, z] = got[i * NBLK : (i + 1) * NBLK]
    span = HALF + 2
    size = span * HALF * HALF * NBLK
    acc = conv_rows(
        w_ref,
        lambda a2, a3: nb_ref[:, a2 : a2 + HALF, a3 : a3 + HALF].reshape(size, nb_ref.shape[4]),
        2,
    )
    step = HALF * HALF * NBLK
    n = HALF * step
    res = acc[0:q, 0:n] + acc[q : 2 * q, step : step + n] + acc[2 * q : 3 * q, 2 * step : 2 * step + n]
    out_ref[0] = jnp.maximum(res + bias_column(bias_ref[...]), 0.0).astype(BF16)


def conv_rows(w_ref, rows_of, together):
    taps = [(a2, a3) for a2 in range(3) for a3 in range(3)]
    acc = None
    for i in range(0, 9, together):
        some = taps[i : i + together]
        lhs = jnp.concatenate(
            [
                jnp.concatenate([w_ref[9 * a1 + 3 * a2 + a3] for a1 in range(3)], axis=0)
                for a2, a3 in some
            ],
            axis=1,
        )
        rhs = jnp.concatenate([rows_of(a2, a3) for a2, a3 in some], axis=1)
        term = dot_t(lhs, rhs)
        acc = term if acc is None else acc + term
    return acc


def coarse(me, slots, recv, codes, weight, bias):
    chans = len(slots)
    owners, q, lanes = slots[0].shape
    total = owners * lanes // CUBE
    blocks = total // NBLK
    c_in = weight.shape[2]
    whole = lambda a: pl.BlockSpec(a.shape, lambda i: (0,) * a.ndim)
    return pl.pallas_call(
        lambda *refs: coarse_kernel(chans, codes, *refs),
        out_shape=jax.ShapeDtypeStruct((blocks, q, CUBE * NBLK), BF16),
        grid=(blocks,),
        in_specs=[pl.BlockSpec(memory_space=SM)]
        + [whole(a) for a in slots]
        + [
            pl.BlockSpec((owners, codes, recv.shape[2]), lambda i: (0, recv.shape[1] // codes - 1, 0)),
            whole(weight),
            whole(bias),
        ],
        out_specs=pl.BlockSpec((1, q, CUBE * NBLK), lambda i: (i, 0, 0)),
        scratch_shapes=[
            pltpu.VMEM((chans, owners, q, lanes), BF16),
            pltpu.VMEM((CUBE * total, c_in), F32),
            pltpu.VMEM((27 * NBLK, total), BF16),
            pltpu.VMEM((HALF + 2, HALF + 2, HALF + 2, NBLK, c_in), BF16),
            pltpu.VMEM((total, 128), F32),
            pltpu.VMEM((owners * codes, 256), BF16),
        ],
        compiler_params=params(),
        cost_estimate=cost(2 * 27 * c_in * q * CUBE * total, 2 * 1024 * 1024),
        name="coarse",
    )(me, *slots, recv, weight, bias)


def frame_axis(f):
    if f == 0:
        return -1, EDGE - 1
    if f == FRAME - 1:
        return 1, 0
    return 0, f - 1


def frame_kernel(chans, me_ref, owner_ref, links_ref, *refs):
    packs, halos, refs = refs[:chans], refs[chans : 2 * chans], refs[2 * chans :]
    ff_ref, sel_ref, up_ref, both, inner, outer, plane = refs
    fine, q, vox = halos[0].shape
    owner = owner_ref[0]
    me = me_ref[0]
    for s in range(chans):
        at = pl.ds(pl.multiple_of((me ^ s) * q, q), q)
        for b in range(fine):
            both[0, b, at, :] = packs[s][b * q : (b + 1) * q, :]
            both[1, b, at, :] = halos[s][b]
        for o in range(8):
            row = (fine + o % 2) * q
            up_ref[o, at, :] = packs[s][row : row + q, o // 2 * 128 : o // 2 * 128 + 128]
    for b in range(fine):
        inner[b] = both[0, b].astype(F32).T
        outer[b] = both[1, b].astype(F32).T
    for b in range(fine):
        for s in range(2):
            dz = 2 * s - 1
            row = 2 * b + s
            for fx in range(FRAME):
                dx, vx = frame_axis(fx)
                start = STARTS[HEADING_INDEX[(dx, 0, dz)]] + (0 if dx else vx * EDGE)
                plane[pl.ds((fx * FRAME + 1) * 8 + row, EDGE, stride=8), :] = outer[b, start : start + EDGE, :]
            for fy in (0, FRAME - 1):
                dy = frame_axis(fy)[0]
                start = STARTS[HEADING_INDEX[(0, dy, dz)]]
                plane[pl.ds((FRAME + fy) * 8 + row, EDGE, stride=8 * FRAME), :] = outer[b, start : start + EDGE, :]
                for fx in (0, FRAME - 1):
                    start = STARTS[HEADING_INDEX[(frame_axis(fx)[0], dy, dz)]]
                    plane[pl.ds((fx * FRAME + fy) * 8 + row, 1), :] = outer[b, start : start + 1, :]
    for fx in range(FRAME):
        for fy in range(FRAME):
            dx, vx = frame_axis(fx)
            dy, vy = frame_axis(fy)
            at = ((1 - fx % 2) * 2 + 1 - fy % 2) * 25 + (fx // 2) * 5 + fy // 2
            tiles = []
            for b in range(fine):
                if dx == 0 and dy == 0:
                    start = (vx * EDGE + vy) * EDGE
                    tiles.append(inner[b, start : start + EDGE, :])
                else:
                    start = STARTS[HEADING_INDEX[(dx, dy, 0)]]
                    if dx == 0:
                        tiles.append(outer[b, pl.ds(start + vx, EDGE, stride=EDGE), :])
                    else:
                        start += 0 if dy else vy * EDGE
                        tiles.append(outer[b, start : start + EDGE, :])
            tiles.append(plane[(fx * FRAME + fy) * 8 : (fx * FRAME + fy) * 8 + 8, :])
            tiles.append(jnp.zeros((8, plane.shape[1]), F32))
            ff_ref[at] = jnp.concatenate(tiles, axis=0).astype(BF16)
    blocks = sel_ref.shape[0]
    lane = lax.broadcasted_iota(jnp.int32, (8, 128), 1)
    row = lax.broadcasted_iota(jnp.int32, (8, 128), 0)

    def pick(j, _):
        for dx in (-1, 0, 1):
            for dy in (-1, 0, 1):
                def brick(b, dz):
                    k = HEADING_INDEX[(dx, dy, dz)]
                    n = owner * fine + b if k == len(HEADINGS) else links_ref[b, k]
                    n = n - j * NBLK
                    return jnp.where((n >= 0) & (n < NBLK), n, -1024)

                tiles = []
                for b in range(fine):
                    tiles.append((lane - (row // 2) * NBLK == brick(b, 0)).astype(F32))
                low = jnp.full((8, 128), -1024, jnp.int32)
                for b in range(fine):
                    for s in range(2):
                        n = brick(b, 2 * s - 1) + (HALF - 1) * (1 - s) * NBLK
                        low = jnp.where(row == 2 * b + s, n, low)
                tiles.append((lane == low).astype(F32))
                tiles.append(jnp.zeros((8, 128), F32))
                sel_ref[j, 3 * (dx + 1) + dy + 1] = jnp.concatenate(tiles, axis=0).astype(BF16)
        return 0

    if blocks == 1:
        pick(0, 0)
    else:
        lax.fori_loop(0, blocks, pick, 0)


def frames(me, owner, links, packs, halos, blocks):
    chans = len(packs)
    fine, q, vox = halos[0].shape
    rows = 8 * fine + 16
    c_all = chans * q
    return pl.pallas_call(
        lambda *refs: frame_kernel(chans, *refs),
        out_shape=[
            jax.ShapeDtypeStruct((FRAME * FRAME, rows, c_all), BF16),
            jax.ShapeDtypeStruct((blocks, 9, rows, 128), BF16),
            jax.ShapeDtypeStruct((8, c_all, c_all), BF16),
        ],
        in_specs=[pl.BlockSpec(memory_space=SM)] * 3 + [pl.BlockSpec(memory_space=VM)] * (2 * chans),
        out_specs=[pl.BlockSpec(memory_space=VM)] * 3,
        scratch_shapes=[
            pltpu.VMEM((2, fine, c_all, vox), BF16),
            pltpu.VMEM((fine, vox, c_all), F32),
            pltpu.VMEM((fine, vox, c_all), F32),
            pltpu.VMEM((FRAME * FRAME * 8, c_all), F32),
        ],
        compiler_params=params(),
        name="frames",
    )(me, owner, links, *packs, *halos)


def fine_kernel(chans, me_ref, *refs):
    slots, refs = refs[:chans], refs[chans:]
    ff_ref, sel_ref, up_ref, w_ref, bias_ref, pair_ref, out_ref, co_ref, cr, g3 = refs
    blocks, q, _ = slots[0].shape
    c_all = chans * q
    for s in range(chans):
        co_ref[me_ref[0] ^ s] = slots[s][...]
    fine = out_ref.shape[0]
    rows = ff_ref.shape[1]
    for ux in range(HALF):
        for uy in range(HALF):
            places = [
                (3 * (a[0] + 1) + b[0] + 1, a[1], b[1])
                for a in axis_places(ux)
                for b in axis_places(uy)
            ]
            col = (ux * HALF + uy) * 128

            def part(j):
                source = jnp.concatenate(
                    [co_ref[c, j, :, col : col + 128] for c in range(chans)], axis=0
                )
                picker = jnp.concatenate([sel_ref[j, d] for d, _, _ in places], axis=0)
                return dot_t(picker, source)

            if blocks == 1:
                got = part(0)
            else:
                got = lax.fori_loop(
                    0,
                    blocks,
                    lambda j, a: a + part(j),
                    jnp.zeros((len(places) * rows, c_all), F32),
                )
            got = got.astype(BF16)
            for i, (_, x, y) in enumerate(places):
                cr[x, y] = got[i * rows : (i + 1) * rows]
    r = lax.broadcasted_iota(jnp.int32, (rows, c_all), 0)
    odd = (r % 2 == 1) ^ (r >= 8 * fine)
    sub = lax.broadcasted_iota(jnp.int32, (5, 8, c_all), 1)
    for px in range(2):
        for py in range(2):
            lift = jnp.concatenate([up_ref[4 * px + 2 * py], up_ref[4 * px + 2 * py + 1]], axis=0)
            for i in range(5):
                x = i + 1 - px
                src = cr[x, 1 - py : 6 - py].reshape(5 * rows, c_all)
                both = dot_t(src, lift).reshape(5, rows, 2 * c_all)
                up = jnp.where(odd[None], both[:, :, c_all:], both[:, :, :c_all])
                at = (px * 2 + py) * 25 + i * 5
                merged = (ff_ref[at : at + 5].astype(F32) + up).astype(BF16).astype(F32)
                fx = 2 * i + 1 - px
                plane = merged[:, 8 * fine : 8 * fine + 8, :]
                for pair in range(fine // 2):
                    made = [[], [], []]
                    for h in range(2):
                        b = 2 * pair + h
                        mid = merged[:, 8 * b : 8 * b + 8, :]
                        made[0].append(
                            jnp.where(
                                sub == 0,
                                pltpu.roll(plane, (8 - 2 * b) % 8, 1),
                                pltpu.roll(mid, 1, 1),
                            )
                        )
                        made[1].append(mid)
                        made[2].append(
                            jnp.where(
                                sub == 7,
                                pltpu.roll(plane, 7 - (2 * b + 1), 1),
                                pltpu.roll(mid, 7, 1),
                            )
                        )
                    for a3 in range(3):
                        tile = jnp.concatenate(made[a3], axis=1).astype(BF16)
                        for j in range(5):
                            g3[a3, pair, fx, 2 * j + 1 - py] = tile[j]
    step = EDGE * 2 * EDGE
    n = EDGE * step
    bias = bias_column(bias_ref[...])
    for pair in range(fine // 2):
        acc = conv_rows(
            w_ref,
            lambda a2, a3: g3[a3, pair, :, a2 : a2 + EDGE].reshape(FRAME * step, c_all),
            9,
        )
        res = acc[0:q, 0:n] + acc[q : 2 * q, step : step + n] + acc[2 * q : 3 * q, 2 * step : 2 * step + n]
        res = jnp.maximum(res + bias, 0.0).astype(BF16)
        for h in range(n // 256):
            turned = dot(res[:, 256 * h : 256 * h + 256], pair_ref[...]).astype(BF16)
            for b in range(2):
                out_ref[2 * pair + b, :, 128 * h : 128 * h + 128] = turned[:, 128 * b : 128 * b + 128]


def refine(me, slots, ff, sel, up_weight, weight, bias):
    chans = len(slots)
    blocks, q, wide = slots[0].shape
    rows = ff.shape[1]
    fine = (rows - 16) // 8
    c_all = chans * q
    return pl.pallas_call(
        lambda *refs: fine_kernel(chans, *refs),
        out_shape=jax.ShapeDtypeStruct((fine, q, EDGE**3), BF16),
        in_specs=[pl.BlockSpec(memory_space=SM)] + [pl.BlockSpec(memory_space=VM)] * (chans + 6),
        out_specs=pl.BlockSpec(memory_space=VM),
        scratch_shapes=[
            pltpu.VMEM((chans, blocks, q, wide), BF16),
            pltpu.VMEM((HALF + 2, HALF + 2, rows, c_all), BF16),
            pltpu.VMEM((3, fine // 2, FRAME, FRAME, 2 * EDGE, c_all), BF16),
        ],
        compiler_params=params(),
        cost_estimate=cost(2 * 27 * c_all * q * fine * EDGE**3, 4 * 1024 * 1024),
        name="refine",
    )(me, *slots, ff, sel, up_weight, weight, bias, jnp.asarray(pair_selector(), BF16))


def octant_table():
    columns = np.zeros((8, 27), np.int32)
    octants = np.zeros((8, 27), np.int32)
    for o in range(8):
        bits = (o >> 2 & 1, o >> 1 & 1, o & 1)
        for d in range(27):
            go = (d // 9 - 1, d // 3 % 3 - 1, d % 3 - 1)
            cross, land = [], []
            for bit, g in zip(bits, go):
                t = bit + g
                cross.append(-1 if t < 0 else 1 if t > 1 else 0)
                land.append(t % 2)
            columns[o, d] = HEADING_INDEX[tuple(cross)]
            octants[o, d] = land[0] * 4 + land[1] * 2 + land[2]
    return columns, octants


def per_device(
    features,
    fine_links,
    coarse_links,
    parents,
    down_weight,
    coarse_weight,
    up_weight,
    fine_weight,
    coarse_bias,
    fine_bias,
):
    owners = lax.axis_size("brick")
    chans = lax.axis_size("chan")
    owner = lax.axis_index("brick").astype(jnp.int32)
    me = lax.axis_index("chan").astype(jnp.int32)
    fine, q, vox = features.shape
    parts, chunks, packed = project(me[None], features, down_weight, up_weight, chans)
    done = {}

    def projected(now):
        now, done["parts"] = lax.optimization_barrier((now, parts))
        return now

    def reduced(now):
        blocks = done["parts"]
        arrived = [blocks[0]] + [partner(blocks[s], "chan", s, chans) for s in range(1, chans)]
        now, arrived[1] = lax.optimization_barrier((now, arrived[1]))
        done["arrived"] = arrived
        return now

    asked = gathered(fine_links[None], owners, [lambda now: now, projected, reduced])
    arrived = done["arrived"]
    codes = 8 * coarse_links.shape[0]
    sending, places = assemble(arrived, owner[None], coarse_links, parents, asked, fine_links, chunks, owners)
    recv = lax.all_to_all(sending, "brick", split_axis=0, concat_axis=0, tiled=True)
    packs, _ = relayed(packed, chans)
    recv, packs = lax.optimization_barrier((recv, packs))
    slots, around = relayed(recv[:, :q], chans, lambda: halo(places, recv, q, fine, q, vox))
    halos, co = relayed(
        around,
        chans,
        lambda: coarse(me[None], slots, recv, codes, coarse_weight, coarse_bias[None]),
    )
    cos, (ff, sel, up_all) = relayed(
        co,
        chans,
        lambda: frames(me[None], owner[None], fine_links, packs, halos, co.shape[0]),
    )
    return refine(me[None], cos, ff, sel, up_all, fine_weight, fine_bias[None])


def solution(mesh):
    in_specs = (
        P("brick", "chan", None),
        P("brick", None),
        P("brick", None),
        P("brick"),
        P(None, None, "chan"),
        P(None, "chan", None),
        P(None, "chan", None),
        P(None, "chan", None),
        P("chan"),
        P("chan"),
    )
    return jax.shard_map(
        per_device,
        mesh=mesh,
        in_specs=in_specs,
        out_specs=P("brick", "chan", None),
        check_vma=False,
    )
```

```python
import numpy as np
import jax
import jax.numpy as jnp
from jax import lax
from jax.experimental import pallas as pl
from jax.experimental.pallas import tpu as pltpu
from jax.sharding import PartitionSpec as P

EDGE = 8
HALF = EDGE // 2
CUBE = HALF**3
FRAME = EDGE + 2
NBLK = 32
F32 = jnp.float32
BF16 = jnp.bfloat16
META = 96
MIB = 1024 * 1024


def headings():
    face_steps = [(1, 0, 0), (-1, 0, 0), (0, 1, 0), (0, -1, 0), (0, 0, 1), (0, 0, -1)]
    others = []
    for step_x in (-1, 0, 1):
        for step_y in (-1, 0, 1):
            for step_z in (-1, 0, 1):
                if abs(step_x) + abs(step_y) + abs(step_z) >= 2:
                    others.append((step_x, step_y, step_z))
    return face_steps + others


HEADINGS = headings()
HEADING_INDEX = {d: k for k, d in enumerate(HEADINGS)}
HEADING_INDEX[(0, 0, 0)] = len(HEADINGS)


def piece_lanes():
    order = sorted(
        range(len(HEADINGS)), key=lambda k: (sum(1 for e in HEADINGS[k] if e), k)
    )
    starts, voxels, at = [0] * len(HEADINGS), [None] * len(HEADINGS), 0
    for k in order:
        spans = [
            [0] if e == 1 else [EDGE - 1] if e == -1 else list(range(EDGE))
            for e in HEADINGS[k]
        ]
        voxels[k] = [
            (x * EDGE + y) * EDGE + z
            for x in spans[0]
            for y in spans[1]
            for z in spans[2]
        ]
        starts[k] = at
        at += len(voxels[k])
    return starts, voxels


STARTS, VOXELS = piece_lanes()
for k in (2, 3):
    VOXELS[k] = [VOXELS[k][x * EDGE + z] for z in range(EDGE) for x in range(EDGE)]
def octant_selector():
    sel = np.zeros((EDGE**3, EDGE**3), np.float32)
    for x in range(EDGE):
        for y in range(EDGE):
            for z in range(EDGE):
                o = (x % 2) * 4 + (y % 2) * 2 + z % 2
                u = ((x // 2) * HALF + y // 2) * HALF + z // 2
                sel[(x * EDGE + y) * EDGE + z, o * CUBE + u] = 1
    return sel


FACE = EDGE**2
FACES = 6
RIMS = len(HEADINGS) - FACES


def outer_selector():
    sel = np.zeros((EDGE**3, FACES * FACE + -(-RIMS * EDGE // 128) * 128), np.float32)
    for k in range(len(HEADINGS)):
        first = k * FACE if k < FACES else FACES * FACE + (k - FACES) * EDGE
        for i, v in enumerate(VOXELS[k]):
            sel[v, first + i] = 1
    return sel


def entry_tables(fine):
    wide = 128 // fine
    lanes = np.zeros((2, 128), np.int32)
    for b in range(fine):
        for k in range(len(HEADINGS)):
            face = k < FACES
            lanes[:, b * wide + k] = k * 128 if face else FACES * 128 + (k - FACES) * EDGE, face
    kind = lanes[1]
    earlier = (np.arange(128)[:, None] < np.arange(128)[None]) & (kind[:, None] == kind[None])
    return lanes, earlier.astype(np.float32)


def capacities(fine, owners):
    return -(-fine * FACES // owners), -(-fine * RIMS // owners)


def pair_selector():
    sel = np.zeros((256, 256), np.float32)
    for x in range(2):
        for y in range(8):
            for b in range(2):
                for z in range(8):
                    sel[((x * 8 + y) * 2 + b) * 8 + z, ((b * 2 + x) * 8 + y) * 8 + z] = 1
    return sel


def dot(a, b):
    return lax.dot_general(a, b, (((1,), (0,)), ((), ())), preferred_element_type=F32)


def dot_t(a, b):
    return lax.dot_general(a, b, (((1,), (1,)), ((), ())), preferred_element_type=F32)


def params():
    return pltpu.CompilerParams(vmem_limit_bytes=min(56, 12 + lax.axis_size("brick")) * MIB)


def cost(flops, moved):
    return pl.CostEstimate(flops=flops, bytes_accessed=moved, transcendentals=0)


VM = pltpu.VMEM
SM = pltpu.SMEM


def project_kernel(chans, me_ref, f_ref, sel_ref, w_ref, up_ref, *rest):
    outs, (chunk_ref, pack_ref, part) = rest[:chans], rest[chans:]
    q = w_ref.shape[1]
    rows, vox = f_ref.shape
    fine = rows // q
    x = f_ref[...]
    picked = dot(x, sel_ref[:, :vox]).astype(BF16)
    acc = None
    for o in range(8):
        z = jnp.concatenate(
            [picked[b * q : (b + 1) * q, o * CUBE : (o + 1) * CUBE] for b in range(fine)],
            axis=1,
        )
        term = lax.dot_general(
            w_ref[o], z, (((0,), (0,)), ((), ())), preferred_element_type=F32
        )
        acc = term if acc is None else acc + term
    part[...] = acc
    me = me_ref[0]
    for s in range(chans):
        outs[s][...] = part[pl.ds(pl.multiple_of((me ^ s) * q, q), q), :].astype(BF16)
    got = dot(x, sel_ref[:, vox:])
    low = lax.broadcasted_iota(jnp.int32, (rows, 128), 1) < FACE
    for i in range(FACES // 2):
        pair = got[:, 128 * i : 128 * i + 128]
        turned = pltpu.roll(pair, FACE, 1)
        chunk_ref[2 * i] = jnp.where(low, pair, turned).astype(BF16)
        chunk_ref[2 * i + 1] = jnp.where(low, turned, pair).astype(BF16)
    for i in range(FACES, chunk_ref.shape[0]):
        at = 128 * (i - FACES // 2)
        chunk_ref[i] = got[:, at : at + 128].astype(BF16)
    pack_ref[0:rows] = x
    more = up_ref.shape[0] * up_ref.shape[1] // vox
    for i in range(vox // up_ref.shape[1]):
        part_lanes = slice(i * up_ref.shape[1], (i + 1) * up_ref.shape[1])
        pack_ref[rows : rows + more, part_lanes] = up_ref[i * more : (i + 1) * more]


def project(me, features, down_weight, up_weight, chans):
    fine, q, vox = features.shape
    c_out = down_weight.shape[1]
    lanes = fine * CUBE
    ups = up_weight.reshape(-1, up_weight.shape[2])
    sel = np.concatenate([octant_selector(), outer_selector()], axis=1)
    chunks = (sel.shape[1] - vox) // 128 + FACES // 2
    res = pl.pallas_call(
        lambda *refs: project_kernel(chans, *refs),
        out_shape=[jax.ShapeDtypeStruct((q, lanes), BF16)] * chans
        + [
            jax.ShapeDtypeStruct((chunks, fine * q, 128), BF16),
            jax.ShapeDtypeStruct((fine * q + ups.size // vox, vox), BF16),
        ],
        in_specs=[pl.BlockSpec(memory_space=SM)] + [pl.BlockSpec(memory_space=VM)] * 4,
        out_specs=[pl.BlockSpec(memory_space=VM)] * (chans + 2),
        scratch_shapes=[pltpu.VMEM((c_out, lanes), F32)],
        compiler_params=params(),
        name="project",
    )(
        me,
        features.reshape(fine * q, vox),
        jnp.asarray(sel, BF16),
        jnp.transpose(down_weight, (0, 2, 1)),
        ups,
    )
    return res[:chans], res[chans], res[chans + 1]


def padded(rows, wide):
    return jnp.concatenate([rows, jnp.full((rows.shape[0], wide - rows.shape[1]), -1, jnp.int32)], axis=1)


def choose(
    fine, q, faces, rims, digits, owner_ref, asked_refs, own_ref, lanes_ref, earlier_ref, chunk_ref,
    out_ref, from_ref, table, scalars, sem,
):
    order = xor_order(out_ref.shape[0])
    owners = out_ref.shape[0]
    place = lanes_ref[0:1, :]
    is_face = lanes_ref[1:2, :] == 1
    wide = 128 // fine
    asked = jnp.concatenate(
        [
            jnp.concatenate([padded(ref[:, b, :], wide) for ref in asked_refs], axis=0)
            for b in range(fine)
        ],
        axis=1,
    )
    mask = (asked >= 0) & (lax.div(jnp.maximum(asked, 0), fine) == owner_ref[0])
    rank = dot(mask.astype(F32).astype(BF16), earlier_ref[...])
    slot = jnp.where(is_face, rank, rank + faces)
    code = (lax.rem(jnp.maximum(asked, 0), fine) * 1024 + place + 1).astype(F32)
    lane = lax.broadcasted_iota(jnp.int32, (owners, 128), 1)
    found = jnp.zeros((owners, 128), F32)
    for r in range(faces + rims):
        value = jnp.sum(jnp.where(mask & (slot == r), code, 0.0), axis=1, keepdims=True)
        found = jnp.where(lane == r, value, found)
    table[...] = found.astype(jnp.int32) - 1
    copy = pltpu.make_async_copy(table, scalars, sem)
    copy.start()
    own = jnp.concatenate([padded(own_ref[b : b + 1, :], wide) for b in range(fine)], axis=1)
    own = jnp.broadcast_to(own, (owners, 128))
    theirs = lax.div(jnp.maximum(own, 0), fine)
    mask = (own >= 0) & (theirs == lax.broadcasted_iota(jnp.int32, (owners, 128), 0))
    rank = dot(mask.astype(F32).astype(BF16), earlier_ref[...])
    at = jnp.where(is_face, rank * FACE, rank * EDGE + faces * FACE) + theirs.astype(F32) * 1024.0 + 1.0
    from_ref[...] = jnp.sum(jnp.where(mask, at, 0.0), axis=0, keepdims=True).astype(jnp.int32) - 1
    copy.wait()
    side = lax.broadcasted_iota(jnp.int32, (q, 128), 1)
    half = q // 2

    def one(r_owner, _):
        w = owner_ref[0] ^ (order[r_owner] if owners <= 8 else reversed_bits(r_owner, owners))
        blocks = (out_ref.shape[1] - q) // half
        for block in range(blocks):
            here = jnp.zeros((q, 128), F32)
            for r in range(faces + rims):
                pos = r * FACE if r < faces else faces * FACE + (r - faces) * EDGE
                if pos // 128 != block:
                    continue
                safe = jnp.maximum(scalars[r_owner, r], 0)
                b = lax.shift_right_logical(safe, 10)
                chunk = lax.shift_right_logical(safe, 7) & 7
                got = chunk_ref[chunk, pl.ds(pl.multiple_of(b * q, q), q), :].astype(F32)
                first = pos % 128
                size = FACE
                if r >= faces:
                    got = pltpu.roll(got, (first + 128 - (safe & 127)) & 127, 1)
                    size = EDGE
                here = jnp.where((side >= first) & (side < first + size), got, here)
            at = q + block * half
            for i in range(2):
                part = here[i * half : (i + 1) * half]
                if block == blocks - 1:
                    part = part + digits[i]
                out_ref[w, at : at + half, 128 * i : 128 * i + 128] = part.astype(BF16)
        return 0

    if owners <= 8:
        for w in range(owners):
            one(w, 0)
    else:
        lax.fori_loop(0, owners, one, 0)


def assemble_kernel(chans, asks, fine, faces, rims, owner_ref, links_ref, parents_ref, table_ref, *refs):
    slots, asked_refs, refs = refs[:chans], refs[chans : chans + asks], refs[chans + asks :]
    out_ref = refs[4]
    count, ways = links_ref.shape
    total = slots[0][...].astype(F32)
    for s in slots[1:]:
        total = total + s[...].astype(F32)
    q, lanes = slots[0].shape
    total = total.astype(BF16)
    rows = count * 8
    column, octant = table_ref[0], table_ref[1]
    row = lax.broadcasted_iota(jnp.int32, (rows, 128), 0)
    lane = lax.broadcasted_iota(jnp.int32, (rows, 128), 1)
    code = jnp.zeros((rows, 128), jnp.int32)
    for p in range(count):
        own = row // 8 == p
        for k in range(ways + 1):
            brick = owner_ref[0] * count + p if k == ways else links_ref[p, k]
            code = jnp.where(own & (column == k), jnp.where(brick >= 0, brick * 8 + octant + 1, 0), code)
    for b in range(parents_ref.shape[0]):
        code = jnp.where((row == b) & (lane == META + 27), parents_ref[b] + 1, code)
    high = lax.shift_right_logical(code, 7)
    digits = [high.astype(F32), (code - high * 128).astype(F32)]
    for w in range(out_ref.shape[0]):
        out_ref[w, 0:q, :] = total
    choose(fine, q, faces, rims, digits, owner_ref, asked_refs, *refs)


def assemble(slots, owner, coarse_links, parents, asked, own, chunks, owners):
    q, lanes = slots[0].shape
    count = coarse_links.shape[0]
    fine = parents.shape[0]
    columns, octants = octant_table()
    table = np.full((2, count * 8, 128), -1, np.int32)
    table[0, :, META : META + 27] = np.tile(columns, (count, 1))
    table[1, :, META : META + 27] = np.tile(octants, (count, 1))
    faces, rims = capacities(fine, owners)
    blocks = -(-(faces * FACE + rims * EDGE) // 128)
    assert count * 8 == q // 2 and (faces * FACE + rims * EDGE - 1) % 128 < META
    entries, earlier = entry_tables(fine)
    return pl.pallas_call(
        lambda *refs: assemble_kernel(len(slots), len(asked), fine, faces, rims, *refs),
        out_shape=[
            jax.ShapeDtypeStruct((owners, q + blocks * q // 2, lanes), BF16),
            jax.ShapeDtypeStruct((1, 128), jnp.int32),
        ],
        in_specs=[pl.BlockSpec(memory_space=SM)] * 3 + [pl.BlockSpec(memory_space=VM)] * (len(slots) + len(asked) + 5),
        out_specs=[pl.BlockSpec(memory_space=VM)] * 2,
        scratch_shapes=[
            pltpu.VMEM((owners, 128), jnp.int32),
            pltpu.SMEM((owners, 128), jnp.int32),
            pltpu.SemaphoreType.DMA,
        ],
        compiler_params=params(),
        cost_estimate=cost(1024 * 1024, 12 * 1024 * 1024),
        name="assemble",
    )(
        owner, coarse_links, parents, jnp.asarray(table), *slots,
        *asked, own, jnp.asarray(entries), jnp.asarray(earlier, BF16), chunks,
    )


def partner(x, axis, step, count):
    return lax.ppermute(x, axis, [(i, i ^ step) for i in range(count)])


def exchanged(x, chans):
    return [x] + [partner(x, "chan", s, chans) for s in range(1, chans)]


def relayed(x, chans, meanwhile=lambda: None):
    slots, step, other = {0: x}, chans // 2, None
    while step:
        if step == 1:
            other = meanwhile()
            if other is not None:
                slots, other = lax.optimization_barrier((slots, other))
        for s in list(slots):
            slots[s | step] = partner(slots[s], "chan", step, chans)
        step //= 2
    return [slots[s] for s in range(chans)], other


def reversed_bits(r, count):
    out, bit = 0, 1
    while bit < count:
        out = out * 2 + r % 2
        r = r // 2
        bit *= 2
    return out


def xor_order(count):
    return [reversed_bits(r, count) for r in range(count)]


def gathered(x, owners, between):
    have, step, count = [x], owners // 2, 0
    while step:
        now = jnp.concatenate(have, axis=0) if len(have) > 1 else have[0]
        if count < len(between):
            now = between[count](now)
        have = [now, partner(now, "brick", step, owners)]
        step //= 2
        count += 1
    return have


def halo_kernel(q, base, from_ref, recv_ref, out_ref):
    fine = out_ref.shape[0]
    half = q // 2
    lane = lax.broadcasted_iota(jnp.int32, (q, 128), 1)
    for b in range(fine):
        for chunk in range(out_ref.shape[2] // 128):
            here = jnp.zeros((q, 128), F32)
            for k in range(len(HEADINGS)):
                if STARTS[k] // 128 != chunk:
                    continue
                first = STARTS[k] % 128
                last = first + len(VOXELS[k])
                v = from_ref[0, b * (128 // fine) + k]
                safe = jnp.maximum(v, 0)
                w = lax.shift_right_logical(safe, 10)
                block = lax.shift_right_logical(safe, 7) & 7
                row = pl.multiple_of(base + block * half, 16)
                got = jnp.concatenate(
                    [recv_ref[w, pl.ds(row, half), 0:128], recv_ref[w, pl.ds(row, half), 128:256]], axis=0
                ).astype(F32)
                got = pltpu.roll(got, (first + 128 - (safe & 127)) & 127, 1)
                here = jnp.where((lane >= first) & (lane < last) & (v >= 0), got, here)
            out_ref[b, :, chunk * 128 : (chunk + 1) * 128] = here.astype(BF16)


def halo(places, recv, base, fine, q, vox):
    return pl.pallas_call(
        lambda *refs: halo_kernel(q, base, *refs),
        out_shape=jax.ShapeDtypeStruct((fine, q, vox), BF16),
        in_specs=[pl.BlockSpec(memory_space=SM), pl.BlockSpec(memory_space=VM)],
        out_specs=pl.BlockSpec(memory_space=VM),
        compiler_params=params(),
        name="halo",
    )(places, recv)


def axis_places(u):
    found = [(0, 1 + u)]
    if u == 0:
        found.append((1, HALF + 1))
    if u == HALF - 1:
        found.append((-1, 0))
    return found


def bias_column(row):
    n = row.shape[1]
    square = jnp.broadcast_to(row, (n, n))
    on = lax.broadcasted_iota(jnp.int32, (n, n), 0) == lax.broadcasted_iota(jnp.int32, (n, n), 1)
    return jnp.sum(jnp.where(on, square, 0.0), axis=1, keepdims=True)


def coarse_kernel(chans, codes, me_ref, *refs):
    slots, refs = refs[:chans], refs[chans:]
    recv_ref, w_ref, bias_ref, out_ref, proj_ref, rows_ref, sel_ref, nb_ref, parent_ref, table_ref = refs
    owners, q, lanes = slots[0].shape
    me = me_ref[0]
    fine = lanes // CUBE
    total = owners * fine

    def spread(w, _):
        block = jnp.concatenate([proj_ref[c, w] for c in range(chans)], axis=0)
        turned = block.astype(F32).T
        for b in range(fine):
            rows_ref[pl.ds(w * fine + b, CUBE, stride=total), :] = turned[b * CUBE : (b + 1) * CUBE]
        return 0

    @pl.when(pl.program_id(0) == 0)
    def _():
        for w in range(owners):
            digits = recv_ref[w]
            table_ref[w * codes : (w + 1) * codes, :] = digits
            digits = digits.astype(F32)
            value = digits[:, 0:128] * 128.0 + digits[:, 128:256] - 1.0
            parent_ref[w * fine : (w + 1) * fine, :] = jnp.broadcast_to(value[0:fine, META + 27 : META + 28], (fine, 128))
        for s in range(chans):
            proj_ref[me ^ s] = slots[s][...]
        if owners <= 8:
            for w in range(owners):
                spread(w, 0)
        else:
            lax.fori_loop(0, owners, spread, 0)

    mine = parent_ref[pl.ds(pl.program_id(0) * NBLK, NBLK), :]
    row = lax.broadcasted_iota(jnp.int32, (NBLK, table_ref.shape[0]), 1).astype(F32)
    own = (mine[:, 0:1] == row).astype(F32).astype(BF16)
    digits = dot(own, table_ref[...])
    target = digits[:, 0:128] * 128.0 + digits[:, 128:256] - 1.0
    on = lax.broadcasted_iota(jnp.int32, (total, total), 0) == lax.broadcasted_iota(jnp.int32, (total, total), 1)
    parents = jnp.sum(jnp.where(on, parent_ref[:, 0:1], 0.0), axis=0, keepdims=True)
    for d in range(27):
        sel_ref[d * NBLK : (d + 1) * NBLK, :] = (target[:, META + d : META + d + 1] == parents).astype(F32).astype(BF16)
    for ux in range(HALF):
        for uy in range(HALF):
            for uz in range(HALF):
                places = [
                    (9 * (a[0] + 1) + 3 * (b[0] + 1) + c[0] + 1, a[1], b[1], c[1])
                    for a in axis_places(ux)
                    for b in axis_places(uy)
                    for c in axis_places(uz)
                ]
                u = (ux * HALF + uy) * HALF + uz
                source = rows_ref[u * total : (u + 1) * total, :].astype(BF16)
                picker = jnp.concatenate(
                    [sel_ref[d * NBLK : (d + 1) * NBLK, :] for d, _, _, _ in places], axis=0
                )
                got = dot(picker, source).astype(BF16)
                for i, (_, x, y, z) in enumerate(places):
                    nb_ref[x, y, z] = got[i * NBLK : (i + 1) * NBLK]
    span = HALF + 2
    size = span * HALF * HALF * NBLK
    acc = conv_rows(
        w_ref,
        lambda a2, a3: nb_ref[:, a2 : a2 + HALF, a3 : a3 + HALF].reshape(size, nb_ref.shape[4]),
        2,
    )
    step = HALF * HALF * NBLK
    n = HALF * step
    res = acc[0:q, 0:n] + acc[q : 2 * q, step : step + n] + acc[2 * q : 3 * q, 2 * step : 2 * step + n]
    out_ref[0] = jnp.maximum(res + bias_column(bias_ref[...]), 0.0).astype(BF16)


def conv_rows(w_ref, rows_of, together):
    taps = [(a2, a3) for a2 in range(3) for a3 in range(3)]
    acc = None
    for i in range(0, 9, together):
        some = taps[i : i + together]
        lhs = jnp.concatenate(
            [
                jnp.concatenate([w_ref[9 * a1 + 3 * a2 + a3] for a1 in range(3)], axis=0)
                for a2, a3 in some
            ],
            axis=1,
        )
        rhs = jnp.concatenate([rows_of(a2, a3) for a2, a3 in some], axis=1)
        term = dot_t(lhs, rhs)
        acc = term if acc is None else acc + term
    return acc


def coarse(me, slots, recv, codes, weight, bias):
    chans = len(slots)
    owners, q, lanes = slots[0].shape
    total = owners * lanes // CUBE
    blocks = total // NBLK
    c_in = weight.shape[2]
    whole = lambda a: pl.BlockSpec(a.shape, lambda i: (0,) * a.ndim)
    return pl.pallas_call(
        lambda *refs: coarse_kernel(chans, codes, *refs),
        out_shape=jax.ShapeDtypeStruct((blocks, q, CUBE * NBLK), BF16),
        grid=(blocks,),
        in_specs=[pl.BlockSpec(memory_space=SM)]
        + [whole(a) for a in slots]
        + [
            pl.BlockSpec((owners, codes, recv.shape[2]), lambda i: (0, recv.shape[1] // codes - 1, 0)),
            whole(weight),
            whole(bias),
        ],
        out_specs=pl.BlockSpec((1, q, CUBE * NBLK), lambda i: (i, 0, 0)),
        scratch_shapes=[
            pltpu.VMEM((chans, owners, q, lanes), BF16),
            pltpu.VMEM((CUBE * total, c_in), F32),
            pltpu.VMEM((27 * NBLK, total), BF16),
            pltpu.VMEM((HALF + 2, HALF + 2, HALF + 2, NBLK, c_in), BF16),
            pltpu.VMEM((total, 128), F32),
            pltpu.VMEM((owners * codes, 256), BF16),
        ],
        compiler_params=params(),
        cost_estimate=cost(2 * 27 * c_in * q * CUBE * total, 2 * 1024 * 1024),
        name="coarse",
    )(me, *slots, recv, weight, bias)


def frame_axis(f):
    if f == 0:
        return -1, EDGE - 1
    if f == FRAME - 1:
        return 1, 0
    return 0, f - 1


def frame_kernel(chans, me_ref, owner_ref, links_ref, *refs):
    packs, halos, refs = refs[:chans], refs[chans : 2 * chans], refs[2 * chans :]
    ff_ref, sel_ref, up_ref, both, inner, outer, plane = refs
    fine, q, vox = halos[0].shape
    owner = owner_ref[0]
    me = me_ref[0]
    for s in range(chans):
        at = pl.ds(pl.multiple_of((me ^ s) * q, q), q)
        for b in range(fine):
            both[0, b, at, :] = packs[s][b * q : (b + 1) * q, :]
            both[1, b, at, :] = halos[s][b]
        for o in range(8):
            row = (fine + o % 2) * q
            up_ref[o, at, :] = packs[s][row : row + q, o // 2 * 128 : o // 2 * 128 + 128]
    for b in range(fine):
        inner[b] = both[0, b].astype(F32).T
        outer[b] = both[1, b].astype(F32).T
    for b in range(fine):
        for s in range(2):
            dz = 2 * s - 1
            row = 2 * b + s
            for fx in range(FRAME):
                dx, vx = frame_axis(fx)
                start = STARTS[HEADING_INDEX[(dx, 0, dz)]] + (0 if dx else vx * EDGE)
                plane[pl.ds((fx * FRAME + 1) * 8 + row, EDGE, stride=8), :] = outer[b, start : start + EDGE, :]
            for fy in (0, FRAME - 1):
                dy = frame_axis(fy)[0]
                start = STARTS[HEADING_INDEX[(0, dy, dz)]]
                plane[pl.ds((FRAME + fy) * 8 + row, EDGE, stride=8 * FRAME), :] = outer[b, start : start + EDGE, :]
                for fx in (0, FRAME - 1):
                    start = STARTS[HEADING_INDEX[(frame_axis(fx)[0], dy, dz)]]
                    plane[pl.ds((fx * FRAME + fy) * 8 + row, 1), :] = outer[b, start : start + 1, :]
    for fx in range(FRAME):
        for fy in range(FRAME):
            dx, vx = frame_axis(fx)
            dy, vy = frame_axis(fy)
            at = ((1 - fx % 2) * 2 + 1 - fy % 2) * 25 + (fx // 2) * 5 + fy // 2
            tiles = []
            for b in range(fine):
                if dx == 0 and dy == 0:
                    start = (vx * EDGE + vy) * EDGE
                    tiles.append(inner[b, start : start + EDGE, :])
                else:
                    start = STARTS[HEADING_INDEX[(dx, dy, 0)]]
                    if dx == 0:
                        tiles.append(outer[b, pl.ds(start + vx, EDGE, stride=EDGE), :])
                    else:
                        start += 0 if dy else vy * EDGE
                        tiles.append(outer[b, start : start + EDGE, :])
            tiles.append(plane[(fx * FRAME + fy) * 8 : (fx * FRAME + fy) * 8 + 8, :])
            tiles.append(jnp.zeros((8, plane.shape[1]), F32))
            ff_ref[at] = jnp.concatenate(tiles, axis=0).astype(BF16)
    blocks = sel_ref.shape[0]
    lane = lax.broadcasted_iota(jnp.int32, (8, 128), 1)
    row = lax.broadcasted_iota(jnp.int32, (8, 128), 0)

    def pick(j, _):
        for dx in (-1, 0, 1):
            for dy in (-1, 0, 1):
                def brick(b, dz):
                    k = HEADING_INDEX[(dx, dy, dz)]
                    n = owner * fine + b if k == len(HEADINGS) else links_ref[b, k]
                    n = n - j * NBLK
                    return jnp.where((n >= 0) & (n < NBLK), n, -1024)

                tiles = []
                for b in range(fine):
                    tiles.append((lane - (row // 2) * NBLK == brick(b, 0)).astype(F32))
                low = jnp.full((8, 128), -1024, jnp.int32)
                for b in range(fine):
                    for s in range(2):
                        n = brick(b, 2 * s - 1) + (HALF - 1) * (1 - s) * NBLK
                        low = jnp.where(row == 2 * b + s, n, low)
                tiles.append((lane == low).astype(F32))
                tiles.append(jnp.zeros((8, 128), F32))
                sel_ref[j, 3 * (dx + 1) + dy + 1] = jnp.concatenate(tiles, axis=0).astype(BF16)
        return 0

    if blocks == 1:
        pick(0, 0)
    else:
        lax.fori_loop(0, blocks, pick, 0)


def frames(me, owner, links, packs, halos, blocks):
    chans = len(packs)
    fine, q, vox = halos[0].shape
    rows = 8 * fine + 16
    c_all = chans * q
    return pl.pallas_call(
        lambda *refs: frame_kernel(chans, *refs),
        out_shape=[
            jax.ShapeDtypeStruct((FRAME * FRAME, rows, c_all), BF16),
            jax.ShapeDtypeStruct((blocks, 9, rows, 128), BF16),
            jax.ShapeDtypeStruct((8, c_all, c_all), BF16),
        ],
        in_specs=[pl.BlockSpec(memory_space=SM)] * 3 + [pl.BlockSpec(memory_space=VM)] * (2 * chans),
        out_specs=[pl.BlockSpec(memory_space=VM)] * 3,
        scratch_shapes=[
            pltpu.VMEM((2, fine, c_all, vox), BF16),
            pltpu.VMEM((fine, vox, c_all), F32),
            pltpu.VMEM((fine, vox, c_all), F32),
            pltpu.VMEM((FRAME * FRAME * 8, c_all), F32),
        ],
        compiler_params=params(),
        name="frames",
    )(me, owner, links, *packs, *halos)


def fine_kernel(chans, me_ref, *refs):
    slots, refs = refs[:chans], refs[chans:]
    ff_ref, sel_ref, up_ref, w_ref, bias_ref, pair_ref, out_ref, co_ref, cr, g3 = refs
    blocks, q, _ = slots[0].shape
    c_all = chans * q
    for s in range(chans):
        co_ref[me_ref[0] ^ s] = slots[s][...]
    fine = out_ref.shape[0]
    rows = ff_ref.shape[1]
    for ux in range(HALF):
        for uy in range(HALF):
            places = [
                (3 * (a[0] + 1) + b[0] + 1, a[1], b[1])
                for a in axis_places(ux)
                for b in axis_places(uy)
            ]
            col = (ux * HALF + uy) * 128

            def part(j):
                source = jnp.concatenate(
                    [co_ref[c, j, :, col : col + 128] for c in range(chans)], axis=0
                )
                picker = jnp.concatenate([sel_ref[j, d] for d, _, _ in places], axis=0)
                return dot_t(picker, source)

            if blocks == 1:
                got = part(0)
            else:
                got = lax.fori_loop(
                    0,
                    blocks,
                    lambda j, a: a + part(j),
                    jnp.zeros((len(places) * rows, c_all), F32),
                )
            got = got.astype(BF16)
            for i, (_, x, y) in enumerate(places):
                cr[x, y] = got[i * rows : (i + 1) * rows]
    r = lax.broadcasted_iota(jnp.int32, (rows, c_all), 0)
    odd = (r % 2 == 1) ^ (r >= 8 * fine)
    sub = lax.broadcasted_iota(jnp.int32, (5, 8, c_all), 1)
    for px in range(2):
        for py in range(2):
            lift = jnp.concatenate([up_ref[4 * px + 2 * py], up_ref[4 * px + 2 * py + 1]], axis=0)
            for i in range(5):
                x = i + 1 - px
                src = cr[x, 1 - py : 6 - py].reshape(5 * rows, c_all)
                both = dot_t(src, lift).reshape(5, rows, 2 * c_all)
                up = jnp.where(odd[None], both[:, :, c_all:], both[:, :, :c_all])
                at = (px * 2 + py) * 25 + i * 5
                merged = (ff_ref[at : at + 5].astype(F32) + up).astype(BF16).astype(F32)
                fx = 2 * i + 1 - px
                plane = merged[:, 8 * fine : 8 * fine + 8, :]
                for pair in range(fine // 2):
                    made = [[], [], []]
                    for h in range(2):
                        b = 2 * pair + h
                        mid = merged[:, 8 * b : 8 * b + 8, :]
                        made[0].append(
                            jnp.where(
                                sub == 0,
                                pltpu.roll(plane, (8 - 2 * b) % 8, 1),
                                pltpu.roll(mid, 1, 1),
                            )
                        )
                        made[1].append(mid)
                        made[2].append(
                            jnp.where(
                                sub == 7,
                                pltpu.roll(plane, 7 - (2 * b + 1), 1),
                                pltpu.roll(mid, 7, 1),
                            )
                        )
                    for a3 in range(3):
                        tile = jnp.concatenate(made[a3], axis=1).astype(BF16)
                        for j in range(5):
                            g3[a3, pair, fx, 2 * j + 1 - py] = tile[j]
    step = EDGE * 2 * EDGE
    n = EDGE * step
    bias = bias_column(bias_ref[...])
    for pair in range(fine // 2):
        acc = conv_rows(
            w_ref,
            lambda a2, a3: g3[a3, pair, :, a2 : a2 + EDGE].reshape(FRAME * step, c_all),
            9,
        )
        res = acc[0:q, 0:n] + acc[q : 2 * q, step : step + n] + acc[2 * q : 3 * q, 2 * step : 2 * step + n]
        res = jnp.maximum(res + bias, 0.0).astype(BF16)
        for h in range(n // 256):
            turned = dot(res[:, 256 * h : 256 * h + 256], pair_ref[...]).astype(BF16)
            for b in range(2):
                out_ref[2 * pair + b, :, 128 * h : 128 * h + 128] = turned[:, 128 * b : 128 * b + 128]


def refine(me, slots, ff, sel, up_weight, weight, bias):
    chans = len(slots)
    blocks, q, wide = slots[0].shape
    rows = ff.shape[1]
    fine = (rows - 16) // 8
    c_all = chans * q
    return pl.pallas_call(
        lambda *refs: fine_kernel(chans, *refs),
        out_shape=jax.ShapeDtypeStruct((fine, q, EDGE**3), BF16),
        in_specs=[pl.BlockSpec(memory_space=SM)] + [pl.BlockSpec(memory_space=VM)] * (chans + 6),
        out_specs=pl.BlockSpec(memory_space=VM),
        scratch_shapes=[
            pltpu.VMEM((chans, blocks, q, wide), BF16),
            pltpu.VMEM((HALF + 2, HALF + 2, rows, c_all), BF16),
            pltpu.VMEM((3, fine // 2, FRAME, FRAME, 2 * EDGE, c_all), BF16),
        ],
        compiler_params=params(),
        cost_estimate=cost(2 * 27 * c_all * q * fine * EDGE**3, 4 * 1024 * 1024),
        name="refine",
    )(me, *slots, ff, sel, up_weight, weight, bias, jnp.asarray(pair_selector(), BF16))


def octant_table():
    columns = np.zeros((8, 27), np.int32)
    octants = np.zeros((8, 27), np.int32)
    for o in range(8):
        bits = (o >> 2 & 1, o >> 1 & 1, o & 1)
        for d in range(27):
            go = (d // 9 - 1, d // 3 % 3 - 1, d % 3 - 1)
            cross, land = [], []
            for bit, g in zip(bits, go):
                t = bit + g
                cross.append(-1 if t < 0 else 1 if t > 1 else 0)
                land.append(t % 2)
            columns[o, d] = HEADING_INDEX[tuple(cross)]
            octants[o, d] = land[0] * 4 + land[1] * 2 + land[2]
    return columns, octants


def per_device(
    features,
    fine_links,
    coarse_links,
    parents,
    down_weight,
    coarse_weight,
    up_weight,
    fine_weight,
    coarse_bias,
    fine_bias,
):
    owners = lax.axis_size("brick")
    chans = lax.axis_size("chan")
    owner = lax.axis_index("brick").astype(jnp.int32)
    me = lax.axis_index("chan").astype(jnp.int32)
    fine, q, vox = features.shape
    parts, chunks, packed = project(me[None], features, down_weight, up_weight, chans)
    done = {}

    def projected(now):
        now, done["parts"] = lax.optimization_barrier((now, parts))
        return now

    def reduced(now):
        blocks = done["parts"]
        arrived = [blocks[0]] + [partner(blocks[s], "chan", s, chans) for s in range(1, chans)]
        now, arrived[1] = lax.optimization_barrier((now, arrived[1]))
        done["arrived"] = arrived
        return now

    asked = gathered(fine_links[None], owners, [lambda now: now, projected, reduced])
    arrived = done["arrived"]
    codes = 8 * coarse_links.shape[0]
    sending, places = assemble(arrived, owner[None], coarse_links, parents, asked, fine_links, chunks, owners)
    recv = lax.all_to_all(sending, "brick", split_axis=0, concat_axis=0, tiled=True)
    packs, _ = relayed(packed, chans)
    recv, packs = lax.optimization_barrier((recv, packs))
    slots, around = relayed(recv[:, :q], chans, lambda: halo(places, recv, q, fine, q, vox))
    halos, co = relayed(
        around,
        chans,
        lambda: coarse(me[None], slots, recv, codes, coarse_weight, coarse_bias[None]),
    )
    cos, (ff, sel, up_all) = relayed(
        co,
        chans,
        lambda: frames(me[None], owner[None], fine_links, packs, halos, co.shape[0]),
    )
    return refine(me[None], cos, ff, sel, up_all, fine_weight, fine_bias[None])


def solution(mesh):
    in_specs = (
        P("brick", "chan", None),
        P("brick", None),
        P("brick", None),
        P("brick"),
        P(None, None, "chan"),
        P(None, "chan", None),
        P(None, "chan", None),
        P(None, "chan", None),
        P("chan"),
        P("chan"),
    )
    return jax.shard_map(
        per_device,
        mesh=mesh,
        in_specs=in_specs,
        out_specs=P("brick", "chan", None),
        check_vma=False,
    )
```

```python
import numpy as np
import jax
import jax.numpy as jnp
from jax import lax
from jax.experimental import pallas as pl
from jax.experimental.pallas import tpu as pltpu
from jax.sharding import PartitionSpec as P

EDGE = 8
HALF = EDGE // 2
CUBE = HALF**3
FRAME = EDGE + 2
NBLK = 32
F32 = jnp.float32
BF16 = jnp.bfloat16
META = 96
MIB = 1024 * 1024


def headings():
    face_steps = [(1, 0, 0), (-1, 0, 0), (0, 1, 0), (0, -1, 0), (0, 0, 1), (0, 0, -1)]
    others = []
    for step_x in (-1, 0, 1):
        for step_y in (-1, 0, 1):
            for step_z in (-1, 0, 1):
                if abs(step_x) + abs(step_y) + abs(step_z) >= 2:
                    others.append((step_x, step_y, step_z))
    return face_steps + others


HEADINGS = headings()
HEADING_INDEX = {d: k for k, d in enumerate(HEADINGS)}
HEADING_INDEX[(0, 0, 0)] = len(HEADINGS)


def piece_lanes():
    order = sorted(
        range(len(HEADINGS)), key=lambda k: (sum(1 for e in HEADINGS[k] if e), k)
    )
    starts, voxels, at = [0] * len(HEADINGS), [None] * len(HEADINGS), 0
    for k in order:
        spans = [
            [0] if e == 1 else [EDGE - 1] if e == -1 else list(range(EDGE))
            for e in HEADINGS[k]
        ]
        voxels[k] = [
            (x * EDGE + y) * EDGE + z
            for x in spans[0]
            for y in spans[1]
            for z in spans[2]
        ]
        starts[k] = at
        at += len(voxels[k])
    return starts, voxels


STARTS, VOXELS = piece_lanes()
for k in (2, 3):
    VOXELS[k] = [VOXELS[k][x * EDGE + z] for z in range(EDGE) for x in range(EDGE)]
def octant_selector():
    sel = np.zeros((EDGE**3, EDGE**3), np.float32)
    for x in range(EDGE):
        for y in range(EDGE):
            for z in range(EDGE):
                o = (x % 2) * 4 + (y % 2) * 2 + z % 2
                u = ((x // 2) * HALF + y // 2) * HALF + z // 2
                sel[(x * EDGE + y) * EDGE + z, o * CUBE + u] = 1
    return sel


FACE = EDGE**2
FACES = 6
RIMS = len(HEADINGS) - FACES


def outer_selector():
    sel = np.zeros((EDGE**3, FACES * FACE + -(-RIMS * EDGE // 128) * 128), np.float32)
    for k in range(len(HEADINGS)):
        first = k * FACE if k < FACES else FACES * FACE + (k - FACES) * EDGE
        for i, v in enumerate(VOXELS[k]):
            sel[v, first + i] = 1
    return sel


def entry_tables(fine):
    wide = 128 // fine
    lanes = np.zeros((2, 128), np.int32)
    for b in range(fine):
        for k in range(len(HEADINGS)):
            face = k < FACES
            lanes[:, b * wide + k] = k * 128 if face else FACES * 128 + (k - FACES) * EDGE, face
    kind = lanes[1]
    earlier = (np.arange(128)[:, None] < np.arange(128)[None]) & (kind[:, None] == kind[None])
    return lanes, earlier.astype(np.float32)


def capacities(fine, owners):
    return -(-fine * FACES // owners), -(-fine * RIMS // owners)


def pair_selector():
    sel = np.zeros((256, 256), np.float32)
    for x in range(2):
        for y in range(8):
            for b in range(2):
                for z in range(8):
                    sel[((x * 8 + y) * 2 + b) * 8 + z, ((b * 2 + x) * 8 + y) * 8 + z] = 1
    return sel


def dot(a, b):
    return lax.dot_general(a, b, (((1,), (0,)), ((), ())), preferred_element_type=F32)


def dot_t(a, b):
    return lax.dot_general(a, b, (((1,), (1,)), ((), ())), preferred_element_type=F32)


def params():
    return pltpu.CompilerParams(vmem_limit_bytes=min(56, 12 + lax.axis_size("brick")) * MIB)


def cost(flops, moved):
    return pl.CostEstimate(flops=flops, bytes_accessed=moved, transcendentals=0)


VM = pltpu.VMEM
SM = pltpu.SMEM


def project_kernel(chans, me_ref, f_ref, sel_ref, w_ref, up_ref, *rest):
    outs, (chunk_ref, pack_ref, part) = rest[:chans], rest[chans:]
    q = w_ref.shape[1]
    rows, vox = f_ref.shape
    fine = rows // q
    x = f_ref[...]
    picked = dot(x, sel_ref[:, :vox]).astype(BF16)
    acc = None
    for o in range(8):
        z = jnp.concatenate(
            [picked[b * q : (b + 1) * q, o * CUBE : (o + 1) * CUBE] for b in range(fine)],
            axis=1,
        )
        term = lax.dot_general(
            w_ref[o], z, (((0,), (0,)), ((), ())), preferred_element_type=F32
        )
        acc = term if acc is None else acc + term
    part[...] = acc
    me = me_ref[0]
    for s in range(chans):
        outs[s][...] = part[pl.ds(pl.multiple_of((me ^ s) * q, q), q), :].astype(BF16)
    got = dot(x, sel_ref[:, vox:])
    low = lax.broadcasted_iota(jnp.int32, (rows, 128), 1) < FACE
    for i in range(FACES // 2):
        pair = got[:, 128 * i : 128 * i + 128]
        turned = pltpu.roll(pair, FACE, 1)
        chunk_ref[2 * i] = jnp.where(low, pair, turned).astype(BF16)
        chunk_ref[2 * i + 1] = jnp.where(low, turned, pair).astype(BF16)
    for i in range(FACES, chunk_ref.shape[0]):
        at = 128 * (i - FACES // 2)
        chunk_ref[i] = got[:, at : at + 128].astype(BF16)
    pack_ref[0:rows] = x
    more = up_ref.shape[0] * up_ref.shape[1] // vox
    for i in range(vox // up_ref.shape[1]):
        part_lanes = slice(i * up_ref.shape[1], (i + 1) * up_ref.shape[1])
        pack_ref[rows : rows + more, part_lanes] = up_ref[i * more : (i + 1) * more]


def project(me, features, down_weight, up_weight, chans):
    fine, q, vox = features.shape
    c_out = down_weight.shape[1]
    lanes = fine * CUBE
    ups = up_weight.reshape(-1, up_weight.shape[2])
    sel = np.concatenate([octant_selector(), outer_selector()], axis=1)
    chunks = (sel.shape[1] - vox) // 128 + FACES // 2
    res = pl.pallas_call(
        lambda *refs: project_kernel(chans, *refs),
        out_shape=[jax.ShapeDtypeStruct((q, lanes), BF16)] * chans
        + [
            jax.ShapeDtypeStruct((chunks, fine * q, 128), BF16),
            jax.ShapeDtypeStruct((fine * q + ups.size // vox, vox), BF16),
        ],
        in_specs=[pl.BlockSpec(memory_space=SM)] + [pl.BlockSpec(memory_space=VM)] * 4,
        out_specs=[pl.BlockSpec(memory_space=VM)] * (chans + 2),
        scratch_shapes=[pltpu.VMEM((c_out, lanes), F32)],
        compiler_params=params(),
        name="project",
    )(
        me,
        features.reshape(fine * q, vox),
        jnp.asarray(sel, BF16),
        jnp.transpose(down_weight, (0, 2, 1)),
        ups,
    )
    return res[:chans], res[chans], res[chans + 1]


def padded(rows, wide):
    return jnp.concatenate([rows, jnp.full((rows.shape[0], wide - rows.shape[1]), -1, jnp.int32)], axis=1)


def choose(
    fine, q, faces, rims, digits, owner_ref, asked_refs, own_ref, lanes_ref, earlier_ref, chunk_ref,
    out_ref, from_ref, table, scalars, sem,
):
    order = xor_order(out_ref.shape[0])
    owners = out_ref.shape[0]
    place = lanes_ref[0:1, :]
    is_face = lanes_ref[1:2, :] == 1
    wide = 128 // fine
    asked = jnp.concatenate(
        [
            jnp.concatenate([padded(ref[:, b, :], wide) for ref in asked_refs], axis=0)
            for b in range(fine)
        ],
        axis=1,
    )
    mask = (asked >= 0) & (lax.div(jnp.maximum(asked, 0), fine) == owner_ref[0])
    rank = dot(mask.astype(F32).astype(BF16), earlier_ref[...])
    slot = jnp.where(is_face, rank, rank + faces)
    code = (lax.rem(jnp.maximum(asked, 0), fine) * 1024 + place + 1).astype(F32)
    lane = lax.broadcasted_iota(jnp.int32, (owners, 128), 1)
    found = jnp.zeros((owners, 128), F32)
    for r in range(faces + rims):
        value = jnp.sum(jnp.where(mask & (slot == r), code, 0.0), axis=1, keepdims=True)
        found = jnp.where(lane == r, value, found)
    table[...] = found.astype(jnp.int32) - 1
    copy = pltpu.make_async_copy(table, scalars, sem)
    copy.start()
    own = jnp.concatenate([padded(own_ref[b : b + 1, :], wide) for b in range(fine)], axis=1)
    own = jnp.broadcast_to(own, (owners, 128))
    theirs = lax.div(jnp.maximum(own, 0), fine)
    mask = (own >= 0) & (theirs == lax.broadcasted_iota(jnp.int32, (owners, 128), 0))
    rank = dot(mask.astype(F32).astype(BF16), earlier_ref[...])
    at = jnp.where(is_face, rank * FACE, rank * EDGE + faces * FACE) + theirs.astype(F32) * 1024.0 + 1.0
    from_ref[...] = jnp.sum(jnp.where(mask, at, 0.0), axis=0, keepdims=True).astype(jnp.int32) - 1
    copy.wait()
    side = lax.broadcasted_iota(jnp.int32, (q, 128), 1)
    half = q // 2

    def one(r_owner, _):
        w = owner_ref[0] ^ (order[r_owner] if owners <= 8 else reversed_bits(r_owner, owners))
        blocks = (out_ref.shape[1] - q) // half
        for block in range(blocks):
            here = jnp.zeros((q, 128), F32)
            for r in range(faces + rims):
                pos = r * FACE if r < faces else faces * FACE + (r - faces) * EDGE
                if pos // 128 != block:
                    continue
                safe = jnp.maximum(scalars[r_owner, r], 0)
                b = lax.shift_right_logical(safe, 10)
                chunk = lax.shift_right_logical(safe, 7) & 7
                got = chunk_ref[chunk, pl.ds(pl.multiple_of(b * q, q), q), :].astype(F32)
                first = pos % 128
                size = FACE
                if r >= faces:
                    got = pltpu.roll(got, (first + 128 - (safe & 127)) & 127, 1)
                    size = EDGE
                here = jnp.where((side >= first) & (side < first + size), got, here)
            at = q + block * half
            for i in range(2):
                part = here[i * half : (i + 1) * half]
                if block == blocks - 1:
                    part = part + digits[i]
                out_ref[w, at : at + half, 128 * i : 128 * i + 128] = part.astype(BF16)
        return 0

    if owners <= 8:
        for w in range(owners):
            one(w, 0)
    else:
        lax.fori_loop(0, owners, one, 0)


def assemble_kernel(chans, asks, fine, faces, rims, owner_ref, links_ref, parents_ref, table_ref, *refs):
    slots, asked_refs, refs = refs[:chans], refs[chans : chans + asks], refs[chans + asks :]
    out_ref = refs[4]
    count, ways = links_ref.shape
    total = slots[0][...].astype(F32)
    for s in slots[1:]:
        total = total + s[...].astype(F32)
    q, lanes = slots[0].shape
    total = total.astype(BF16)
    rows = count * 8
    column, octant = table_ref[0], table_ref[1]
    row = lax.broadcasted_iota(jnp.int32, (rows, 128), 0)
    lane = lax.broadcasted_iota(jnp.int32, (rows, 128), 1)
    code = jnp.zeros((rows, 128), jnp.int32)
    for p in range(count):
        own = row // 8 == p
        for k in range(ways + 1):
            brick = owner_ref[0] * count + p if k == ways else links_ref[p, k]
            code = jnp.where(own & (column == k), jnp.where(brick >= 0, brick * 8 + octant + 1, 0), code)
    for b in range(parents_ref.shape[0]):
        code = jnp.where((row == b) & (lane == META + 27), parents_ref[b] + 1, code)
    high = lax.shift_right_logical(code, 7)
    digits = [high.astype(F32), (code - high * 128).astype(F32)]
    for w in range(out_ref.shape[0]):
        out_ref[w, 0:q, :] = total
    choose(fine, q, faces, rims, digits, owner_ref, asked_refs, *refs)


def assemble(slots, owner, coarse_links, parents, asked, own, chunks, owners):
    q, lanes = slots[0].shape
    count = coarse_links.shape[0]
    fine = parents.shape[0]
    columns, octants = octant_table()
    table = np.full((2, count * 8, 128), -1, np.int32)
    table[0, :, META : META + 27] = np.tile(columns, (count, 1))
    table[1, :, META : META + 27] = np.tile(octants, (count, 1))
    faces, rims = capacities(fine, owners)
    blocks = -(-(faces * FACE + rims * EDGE) // 128)
    assert count * 8 == q // 2 and (faces * FACE + rims * EDGE - 1) % 128 < META
    entries, earlier = entry_tables(fine)
    return pl.pallas_call(
        lambda *refs: assemble_kernel(len(slots), len(asked), fine, faces, rims, *refs),
        out_shape=[
            jax.ShapeDtypeStruct((owners, q + blocks * q // 2, lanes), BF16),
            jax.ShapeDtypeStruct((1, 128), jnp.int32),
        ],
        in_specs=[pl.BlockSpec(memory_space=SM)] * 3 + [pl.BlockSpec(memory_space=VM)] * (len(slots) + len(asked) + 5),
        out_specs=[pl.BlockSpec(memory_space=VM)] * 2,
        scratch_shapes=[
            pltpu.VMEM((owners, 128), jnp.int32),
            pltpu.SMEM((owners, 128), jnp.int32),
            pltpu.SemaphoreType.DMA,
        ],
        compiler_params=params(),
        cost_estimate=cost(1024 * 1024, 12 * 1024 * 1024),
        name="assemble",
    )(
        owner, coarse_links, parents, jnp.asarray(table), *slots,
        *asked, own, jnp.asarray(entries), jnp.asarray(earlier, BF16), chunks,
    )


def partner(x, axis, step, count):
    return lax.ppermute(x, axis, [(i, i ^ step) for i in range(count)])


def exchanged(x, chans):
    return [x] + [partner(x, "chan", s, chans) for s in range(1, chans)]


def relayed(x, chans, meanwhile=lambda: None):
    slots, step, other = {0: x}, chans // 2, None
    while step:
        if step == 1:
            other = meanwhile()
            if other is not None:
                slots, other = lax.optimization_barrier((slots, other))
        for s in list(slots):
            slots[s | step] = partner(slots[s], "chan", step, chans)
        step //= 2
    return [slots[s] for s in range(chans)], other


def reversed_bits(r, count):
    out, bit = 0, 1
    while bit < count:
        out = out * 2 + r % 2
        r = r // 2
        bit *= 2
    return out


def xor_order(count):
    return [reversed_bits(r, count) for r in range(count)]


def gathered(x, owners, between):
    have, step, count = [x], owners // 2, 0
    while step:
        now = jnp.concatenate(have, axis=0) if len(have) > 1 else have[0]
        if count < len(between):
            now = between[count](now)
        have = [now, partner(now, "brick", step, owners)]
        step //= 2
        count += 1
    return have


def halo_kernel(q, base, owner_ref, links_ref, from_ref, recv_ref, out_ref, sel_ref):
    fine = out_ref.shape[0]

    def selectors(block, _):
        sel_ref[block] = jnp.concatenate(line_selectors(fine, owner_ref[0], links_ref, block), axis=0)
        return 0

    if sel_ref.shape[0] == 1:
        selectors(0, 0)
    else:
        lax.fori_loop(0, sel_ref.shape[0], selectors, 0)
    half = q // 2
    lane = lax.broadcasted_iota(jnp.int32, (q, 128), 1)
    for b in range(fine):
        for chunk in range(out_ref.shape[2] // 128):
            here = jnp.zeros((q, 128), F32)
            for k in range(len(HEADINGS)):
                if STARTS[k] // 128 != chunk:
                    continue
                first = STARTS[k] % 128
                last = first + len(VOXELS[k])
                v = from_ref[0, b * (128 // fine) + k]
                safe = jnp.maximum(v, 0)
                w = lax.shift_right_logical(safe, 10)
                block = lax.shift_right_logical(safe, 7) & 7
                row = pl.multiple_of(base + block * half, 16)
                got = jnp.concatenate(
                    [recv_ref[w, pl.ds(row, half), 0:128], recv_ref[w, pl.ds(row, half), 128:256]], axis=0
                ).astype(F32)
                got = pltpu.roll(got, (first + 128 - (safe & 127)) & 127, 1)
                here = jnp.where((lane >= first) & (lane < last) & (v >= 0), got, here)
            out_ref[b, :, chunk * 128 : (chunk + 1) * 128] = here.astype(BF16)


def halo(owner, links, places, recv, base, fine, q, vox):
    return pl.pallas_call(
        lambda *refs: halo_kernel(q, base, *refs),
        out_shape=[
            jax.ShapeDtypeStruct((fine, q, vox), BF16),
            jax.ShapeDtypeStruct((recv.shape[0] * fine // NBLK, 9 * 8 * fine, 128), BF16),
        ],
        in_specs=[pl.BlockSpec(memory_space=SM)] * 3 + [pl.BlockSpec(memory_space=VM)],
        out_specs=[pl.BlockSpec(memory_space=VM)] * 2,
        compiler_params=params(),
        name="halo",
    )(owner, links, places, recv)


def axis_places(u):
    found = [(0, 1 + u)]
    if u == 0:
        found.append((1, HALF + 1))
    if u == HALF - 1:
        found.append((-1, 0))
    return found


def bias_column(row):
    n = row.shape[1]
    square = jnp.broadcast_to(row, (n, n))
    on = lax.broadcasted_iota(jnp.int32, (n, n), 0) == lax.broadcasted_iota(jnp.int32, (n, n), 1)
    return jnp.sum(jnp.where(on, square, 0.0), axis=1, keepdims=True)


LINES = [
    (ux, uy, a, b)
    for ux in range(HALF)
    for uy in range(HALF)
    for a in axis_places(ux)
    for b in axis_places(uy)
]


def line_selectors(fine, owner, links_ref, block):
    lane = lax.broadcasted_iota(jnp.int32, (8, 128), 1)
    row = lax.broadcasted_iota(jnp.int32, (8, 128), 0)
    made = []
    for dx in (-1, 0, 1):
        for dy in (-1, 0, 1):
            tiles = []
            for b in range(fine):
                at = []
                for dz in (-1, 0, 1):
                    k = HEADING_INDEX[(dx, dy, dz)]
                    n = owner * fine + b if k == len(HEADINGS) else links_ref[b, k]
                    n = n - block * NBLK
                    at.append(jnp.where((n >= 0) & (n < NBLK), n, -1024))
                want = jnp.where(row == 0, at[0] + (HALF - 1) * NBLK, at[1] + (row - 1) * NBLK)
                want = jnp.where(row == HALF + 1, at[2], want)
                tiles.append(((lane == want) & (row < HALF + 2)).astype(F32))
            made.append(jnp.concatenate(tiles, axis=0).astype(BF16))
    return made


def line_spreader(fine, rows):
    wide = 8 * fine
    lines = 128 // wide
    sel = np.zeros((lines * rows, 128), np.float32)
    for i in range(lines):
        for b in range(fine):
            first = i * wide + b * 8
            for z in range(EDGE):
                sel[i * rows + b * EDGE + z, first + 1 + z // 2] = 1
            for side in range(2):
                sel[i * rows + wide + 2 * b + side, first + side * (HALF + 1)] = 1
    return sel


def coarse_kernel(chans, codes, me_ref, picker_ref, *refs):
    slots, refs = refs[:chans], refs[chans:]
    recv_ref, w_ref, bias_ref, out_ref, proj_ref, rows_ref, sel_ref, nb_ref, parent_ref, table_ref = refs
    owners, q, lanes = slots[0].shape
    me = me_ref[0]
    fine = lanes // CUBE
    total = owners * fine

    def spread(w, _):
        block = jnp.concatenate([proj_ref[c, w] for c in range(chans)], axis=0)
        turned = block.astype(F32).T
        for b in range(fine):
            rows_ref[pl.ds(w * fine + b, CUBE, stride=total), :] = turned[b * CUBE : (b + 1) * CUBE]
        return 0

    @pl.when(pl.program_id(0) == 0)
    def _():
        for w in range(owners):
            digits = recv_ref[w]
            table_ref[w * codes : (w + 1) * codes, :] = digits
            digits = digits.astype(F32)
            value = digits[:, 0:128] * 128.0 + digits[:, 128:256] - 1.0
            parent_ref[w * fine : (w + 1) * fine, :] = jnp.broadcast_to(value[0:fine, META + 27 : META + 28], (fine, 128))
        for s in range(chans):
            proj_ref[me ^ s] = slots[s][...]
        if owners <= 8:
            for w in range(owners):
                spread(w, 0)
        else:
            lax.fori_loop(0, owners, spread, 0)

    mine = parent_ref[pl.ds(pl.program_id(0) * NBLK, NBLK), :]
    row = lax.broadcasted_iota(jnp.int32, (NBLK, table_ref.shape[0]), 1).astype(F32)
    own = (mine[:, 0:1] == row).astype(F32).astype(BF16)
    digits = dot(own, table_ref[...])
    target = digits[:, 0:128] * 128.0 + digits[:, 128:256] - 1.0
    on = lax.broadcasted_iota(jnp.int32, (total, total), 0) == lax.broadcasted_iota(jnp.int32, (total, total), 1)
    parents = jnp.sum(jnp.where(on, parent_ref[:, 0:1], 0.0), axis=0, keepdims=True)
    for d in range(27):
        sel_ref[d * NBLK : (d + 1) * NBLK, :] = (target[:, META + d : META + d + 1] == parents).astype(F32).astype(BF16)
    for ux in range(HALF):
        for uy in range(HALF):
            for uz in range(HALF):
                places = [
                    (9 * (a[0] + 1) + 3 * (b[0] + 1) + c[0] + 1, a[1], b[1], c[1])
                    for a in axis_places(ux)
                    for b in axis_places(uy)
                    for c in axis_places(uz)
                ]
                u = (ux * HALF + uy) * HALF + uz
                source = rows_ref[u * total : (u + 1) * total, :].astype(BF16)
                picker = jnp.concatenate(
                    [sel_ref[d * NBLK : (d + 1) * NBLK, :] for d, _, _, _ in places], axis=0
                )
                got = dot(picker, source).astype(BF16)
                for i, (_, x, y, z) in enumerate(places):
                    nb_ref[x, y, z] = got[i * NBLK : (i + 1) * NBLK]
    span = HALF + 2
    size = span * HALF * HALF * NBLK
    acc = conv_rows(
        w_ref,
        lambda a2, a3: nb_ref[:, a2 : a2 + HALF, a3 : a3 + HALF].reshape(size, nb_ref.shape[4]),
        2,
    )
    step = HALF * HALF * NBLK
    n = HALF * step
    res = acc[0:q, 0:n] + acc[q : 2 * q, step : step + n] + acc[2 * q : 3 * q, 2 * step : 2 * step + n]
    res = jnp.maximum(res + bias_column(bias_ref[...]), 0.0).astype(BF16)
    size = picker_ref.shape[1] // 9
    pickers = [picker_ref[0, i * size : (i + 1) * size, :] for i in range(9)]
    found = []
    for ux in range(HALF):
        for uy in range(HALF):
            col = (ux * HALF + uy) * 128
            mine = [pickers[3 * (a[0] + 1) + b[0] + 1] for x, y, a, b in LINES if (x, y) == (ux, uy)]
            found.append(dot_t(res[:, col : col + 128], jnp.concatenate(mine, axis=0)))
    found = jnp.concatenate(found, axis=1).astype(BF16)
    if pl.num_programs(0) == 1:
        out_ref[...] = found
    else:
        before = out_ref[...]
        out_ref[...] = jnp.where(pl.program_id(0) == 0, jnp.zeros_like(before), before) + found


def conv_rows(w_ref, rows_of, together):
    taps = [(a2, a3) for a2 in range(3) for a3 in range(3)]
    acc = None
    for i in range(0, 9, together):
        some = taps[i : i + together]
        lhs = jnp.concatenate(
            [
                jnp.concatenate([w_ref[9 * a1 + 3 * a2 + a3] for a1 in range(3)], axis=0)
                for a2, a3 in some
            ],
            axis=1,
        )
        rhs = jnp.concatenate([rows_of(a2, a3) for a2, a3 in some], axis=1)
        term = dot_t(lhs, rhs)
        acc = term if acc is None else acc + term
    return acc


def coarse(me, pickers, slots, recv, codes, weight, bias):
    chans = len(slots)
    owners, q, lanes = slots[0].shape
    fine = lanes // CUBE
    total = owners * fine
    blocks = total // NBLK
    c_in = weight.shape[2]
    whole = lambda a: pl.BlockSpec(a.shape, lambda i: (0,) * a.ndim)
    return pl.pallas_call(
        lambda *refs: coarse_kernel(chans, codes, *refs),
        out_shape=jax.ShapeDtypeStruct((q, len(LINES) * 8 * fine), BF16),
        grid=(blocks,),
        in_specs=[pl.BlockSpec(memory_space=SM), pl.BlockSpec((1,) + pickers.shape[1:], lambda i: (i, 0, 0))]
        + [whole(a) for a in slots]
        + [
            pl.BlockSpec((owners, codes, recv.shape[2]), lambda i: (0, recv.shape[1] // codes - 1, 0)),
            whole(weight),
            whole(bias),
        ],
        out_specs=pl.BlockSpec((q, len(LINES) * 8 * fine), lambda i: (0, 0)),
        scratch_shapes=[
            pltpu.VMEM((chans, owners, q, lanes), BF16),
            pltpu.VMEM((CUBE * total, c_in), F32),
            pltpu.VMEM((27 * NBLK, total), BF16),
            pltpu.VMEM((HALF + 2, HALF + 2, HALF + 2, NBLK, c_in), BF16),
            pltpu.VMEM((total, 128), F32),
            pltpu.VMEM((owners * codes, 256), BF16),
        ],
        compiler_params=params(),
        cost_estimate=cost(2 * 27 * c_in * q * CUBE * total, 2 * 1024 * 1024),
        name="coarse",
    )(me, pickers, *slots, recv, weight, bias)


def frame_axis(f):
    if f == 0:
        return -1, EDGE - 1
    if f == FRAME - 1:
        return 1, 0
    return 0, f - 1


def frame_kernel(chans, me_ref, *refs):
    packs, halos, refs = refs[:chans], refs[chans : 2 * chans], refs[2 * chans :]
    ff_ref, up_ref, both, inner, outer, plane = refs
    fine, q, vox = halos[0].shape
    me = me_ref[0]
    for s in range(chans):
        at = pl.ds(pl.multiple_of((me ^ s) * q, q), q)
        for b in range(fine):
            both[0, b, at, :] = packs[s][b * q : (b + 1) * q, :]
            both[1, b, at, :] = halos[s][b]
        for o in range(8):
            row = (fine + o % 2) * q
            up_ref[o, at, :] = packs[s][row : row + q, o // 2 * 128 : o // 2 * 128 + 128]
    for b in range(fine):
        inner[b] = both[0, b].astype(F32).T
        outer[b] = both[1, b].astype(F32).T
    for b in range(fine):
        for s in range(2):
            dz = 2 * s - 1
            row = 2 * b + s
            for fx in range(FRAME):
                dx, vx = frame_axis(fx)
                start = STARTS[HEADING_INDEX[(dx, 0, dz)]] + (0 if dx else vx * EDGE)
                plane[pl.ds((fx * FRAME + 1) * 8 + row, EDGE, stride=8), :] = outer[b, start : start + EDGE, :]
            for fy in (0, FRAME - 1):
                dy = frame_axis(fy)[0]
                start = STARTS[HEADING_INDEX[(0, dy, dz)]]
                plane[pl.ds((FRAME + fy) * 8 + row, EDGE, stride=8 * FRAME), :] = outer[b, start : start + EDGE, :]
                for fx in (0, FRAME - 1):
                    start = STARTS[HEADING_INDEX[(frame_axis(fx)[0], dy, dz)]]
                    plane[pl.ds((fx * FRAME + fy) * 8 + row, 1), :] = outer[b, start : start + 1, :]
    for fx in range(FRAME):
        for fy in range(FRAME):
            dx, vx = frame_axis(fx)
            dy, vy = frame_axis(fy)
            at = ((1 - fx % 2) * 2 + 1 - fy % 2) * 25 + (fx // 2) * 5 + fy // 2
            tiles = []
            for b in range(fine):
                if dx == 0 and dy == 0:
                    start = (vx * EDGE + vy) * EDGE
                    tiles.append(inner[b, start : start + EDGE, :])
                else:
                    start = STARTS[HEADING_INDEX[(dx, dy, 0)]]
                    if dx == 0:
                        tiles.append(outer[b, pl.ds(start + vx, EDGE, stride=EDGE), :])
                    else:
                        start += 0 if dy else vy * EDGE
                        tiles.append(outer[b, start : start + EDGE, :])
            tiles.append(plane[(fx * FRAME + fy) * 8 : (fx * FRAME + fy) * 8 + 8, :])
            tiles.append(jnp.zeros((8, plane.shape[1]), F32))
            ff_ref[at] = jnp.concatenate(tiles, axis=0).astype(BF16)


def frames(me, packs, halos):
    chans = len(packs)
    fine, q, vox = halos[0].shape
    rows = 8 * fine + 16
    c_all = chans * q
    return pl.pallas_call(
        lambda *refs: frame_kernel(chans, *refs),
        out_shape=[
            jax.ShapeDtypeStruct((FRAME * FRAME, rows, c_all), BF16),
            jax.ShapeDtypeStruct((8, c_all, c_all), BF16),
        ],
        in_specs=[pl.BlockSpec(memory_space=SM)] + [pl.BlockSpec(memory_space=VM)] * (2 * chans),
        out_specs=[pl.BlockSpec(memory_space=VM)] * 2,
        scratch_shapes=[
            pltpu.VMEM((2, fine, c_all, vox), BF16),
            pltpu.VMEM((fine, vox, c_all), F32),
            pltpu.VMEM((fine, vox, c_all), F32),
            pltpu.VMEM((FRAME * FRAME * 8, c_all), F32),
        ],
        compiler_params=params(),
        name="frames",
    )(me, *packs, *halos)


def fine_kernel(chans, me_ref, *refs):
    slots, refs = refs[:chans], refs[chans:]
    ff_ref, sel_ref, up_ref, w_ref, bias_ref, pair_ref, out_ref, co_ref, cr, g3 = refs
    q = slots[0].shape[0]
    c_all = chans * q
    for s in range(chans):
        co_ref[me_ref[0] ^ s] = slots[s][...]
    fine = out_ref.shape[0]
    rows = ff_ref.shape[1]
    lines = 128 // (8 * fine)
    for i in range(0, len(LINES), lines):
        col = i * 8 * fine
        source = jnp.concatenate([co_ref[c, :, col : col + 128] for c in range(chans)], axis=0)
        got = dot_t(sel_ref[...], source).astype(BF16)
        for j, (_, _, x, y) in enumerate(LINES[i : i + lines]):
            cr[x[1], y[1]] = got[j * rows : (j + 1) * rows]
    r = lax.broadcasted_iota(jnp.int32, (rows, c_all), 0)
    odd = (r % 2 == 1) ^ (r >= 8 * fine)
    sub = lax.broadcasted_iota(jnp.int32, (5, 8, c_all), 1)
    for px in range(2):
        for py in range(2):
            lift = jnp.concatenate([up_ref[4 * px + 2 * py], up_ref[4 * px + 2 * py + 1]], axis=0)
            for i in range(5):
                x = i + 1 - px
                src = cr[x, 1 - py : 6 - py].reshape(5 * rows, c_all)
                both = dot_t(src, lift).reshape(5, rows, 2 * c_all)
                up = jnp.where(odd[None], both[:, :, c_all:], both[:, :, :c_all])
                at = (px * 2 + py) * 25 + i * 5
                merged = (ff_ref[at : at + 5].astype(F32) + up).astype(BF16).astype(F32)
                fx = 2 * i + 1 - px
                plane = merged[:, 8 * fine : 8 * fine + 8, :]
                for pair in range(fine // 2):
                    made = [[], [], []]
                    for h in range(2):
                        b = 2 * pair + h
                        mid = merged[:, 8 * b : 8 * b + 8, :]
                        made[0].append(
                            jnp.where(
                                sub == 0,
                                pltpu.roll(plane, (8 - 2 * b) % 8, 1),
                                pltpu.roll(mid, 1, 1),
                            )
                        )
                        made[1].append(mid)
                        made[2].append(
                            jnp.where(
                                sub == 7,
                                pltpu.roll(plane, 7 - (2 * b + 1), 1),
                                pltpu.roll(mid, 7, 1),
                            )
                        )
                    for a3 in range(3):
                        tile = jnp.concatenate(made[a3], axis=1).astype(BF16)
                        for j in range(5):
                            g3[a3, pair, fx, 2 * j + 1 - py] = tile[j]
    step = EDGE * 2 * EDGE
    n = EDGE * step
    bias = bias_column(bias_ref[...])
    for pair in range(fine // 2):
        acc = conv_rows(
            w_ref,
            lambda a2, a3: g3[a3, pair, :, a2 : a2 + EDGE].reshape(FRAME * step, c_all),
            9,
        )
        res = acc[0:q, 0:n] + acc[q : 2 * q, step : step + n] + acc[2 * q : 3 * q, 2 * step : 2 * step + n]
        res = jnp.maximum(res + bias, 0.0).astype(BF16)
        for h in range(n // 256):
            turned = dot(res[:, 256 * h : 256 * h + 256], pair_ref[...]).astype(BF16)
            for b in range(2):
                out_ref[2 * pair + b, :, 128 * h : 128 * h + 128] = turned[:, 128 * b : 128 * b + 128]


def refine(me, slots, ff, up_weight, weight, bias):
    chans = len(slots)
    q, wide = slots[0].shape
    rows = ff.shape[1]
    fine = (rows - 16) // 8
    c_all = chans * q
    return pl.pallas_call(
        lambda *refs: fine_kernel(chans, *refs),
        out_shape=jax.ShapeDtypeStruct((fine, q, EDGE**3), BF16),
        in_specs=[pl.BlockSpec(memory_space=SM)] + [pl.BlockSpec(memory_space=VM)] * (chans + 6),
        out_specs=pl.BlockSpec(memory_space=VM),
        scratch_shapes=[
            pltpu.VMEM((chans, q, wide), BF16),
            pltpu.VMEM((HALF + 2, HALF + 2, rows, c_all), BF16),
            pltpu.VMEM((3, fine // 2, FRAME, FRAME, 2 * EDGE, c_all), BF16),
        ],
        compiler_params=params(),
        cost_estimate=cost(2 * 27 * c_all * q * fine * EDGE**3, 4 * 1024 * 1024),
        name="refine",
    )(me, *slots, ff, jnp.asarray(line_spreader(fine, rows), BF16), up_weight, weight, bias, jnp.asarray(pair_selector(), BF16))


def octant_table():
    columns = np.zeros((8, 27), np.int32)
    octants = np.zeros((8, 27), np.int32)
    for o in range(8):
        bits = (o >> 2 & 1, o >> 1 & 1, o & 1)
        for d in range(27):
            go = (d // 9 - 1, d // 3 % 3 - 1, d % 3 - 1)
            cross, land = [], []
            for bit, g in zip(bits, go):
                t = bit + g
                cross.append(-1 if t < 0 else 1 if t > 1 else 0)
                land.append(t % 2)
            columns[o, d] = HEADING_INDEX[tuple(cross)]
            octants[o, d] = land[0] * 4 + land[1] * 2 + land[2]
    return columns, octants


def per_device(
    features,
    fine_links,
    coarse_links,
    parents,
    down_weight,
    coarse_weight,
    up_weight,
    fine_weight,
    coarse_bias,
    fine_bias,
):
    owners = lax.axis_size("brick")
    chans = lax.axis_size("chan")
    owner = lax.axis_index("brick").astype(jnp.int32)
    me = lax.axis_index("chan").astype(jnp.int32)
    fine, q, vox = features.shape
    parts, chunks, packed = project(me[None], features, down_weight, up_weight, chans)
    done = {}

    def projected(now):
        now, done["parts"] = lax.optimization_barrier((now, parts))
        return now

    def reduced(now):
        blocks = done["parts"]
        arrived = [blocks[0]] + [partner(blocks[s], "chan", s, chans) for s in range(1, chans)]
        now, arrived[1] = lax.optimization_barrier((now, arrived[1]))
        done["arrived"] = arrived
        return now

    asked = gathered(fine_links[None], owners, [lambda now: now, projected, reduced])
    arrived = done["arrived"]
    codes = 8 * coarse_links.shape[0]
    sending, places = assemble(arrived, owner[None], coarse_links, parents, asked, fine_links, chunks, owners)
    recv = lax.all_to_all(sending, "brick", split_axis=0, concat_axis=0, tiled=True)
    packs, _ = relayed(packed, chans)
    recv, packs = lax.optimization_barrier((recv, packs))
    slots, (around, pickers) = relayed(
        recv[:, :q],
        chans,
        lambda: halo(owner[None], fine_links, places, recv, q, fine, q, vox),
    )
    halos, co = relayed(
        around,
        chans,
        lambda: coarse(me[None], pickers, slots, recv, codes, coarse_weight, coarse_bias[None]),
    )
    cos, (ff, up_all) = relayed(co, chans, lambda: frames(me[None], packs, halos))
    return refine(me[None], cos, ff, up_all, fine_weight, fine_bias[None])


def solution(mesh):
    in_specs = (
        P("brick", "chan", None),
        P("brick", None),
        P("brick", None),
        P("brick"),
        P(None, None, "chan"),
        P(None, "chan", None),
        P(None, "chan", None),
        P(None, "chan", None),
        P("chan"),
        P("chan"),
    )
    return jax.shard_map(
        per_device,
        mesh=mesh,
        in_specs=in_specs,
        out_specs=P("brick", "chan", None),
        check_vma=False,
    )
```

```python
import numpy as np
import jax
import jax.numpy as jnp
from jax import lax
from jax.experimental import pallas as pl
from jax.experimental.pallas import tpu as pltpu
from jax.sharding import PartitionSpec as P

EDGE = 8
HALF = EDGE // 2
CUBE = HALF**3
FRAME = EDGE + 2
NBLK = 32
F32 = jnp.float32
BF16 = jnp.bfloat16
META = 96
MIB = 1024 * 1024


def headings():
    face_steps = [(1, 0, 0), (-1, 0, 0), (0, 1, 0), (0, -1, 0), (0, 0, 1), (0, 0, -1)]
    others = []
    for step_x in (-1, 0, 1):
        for step_y in (-1, 0, 1):
            for step_z in (-1, 0, 1):
                if abs(step_x) + abs(step_y) + abs(step_z) >= 2:
                    others.append((step_x, step_y, step_z))
    return face_steps + others


HEADINGS = headings()
HEADING_INDEX = {d: k for k, d in enumerate(HEADINGS)}
HEADING_INDEX[(0, 0, 0)] = len(HEADINGS)


def piece_lanes():
    order = sorted(
        range(len(HEADINGS)), key=lambda k: (sum(1 for e in HEADINGS[k] if e), k)
    )
    starts, voxels, at = [0] * len(HEADINGS), [None] * len(HEADINGS), 0
    for k in order:
        spans = [
            [0] if e == 1 else [EDGE - 1] if e == -1 else list(range(EDGE))
            for e in HEADINGS[k]
        ]
        voxels[k] = [
            (x * EDGE + y) * EDGE + z
            for x in spans[0]
            for y in spans[1]
            for z in spans[2]
        ]
        starts[k] = at
        at += len(voxels[k])
    return starts, voxels


STARTS, VOXELS = piece_lanes()
for k in (2, 3):
    VOXELS[k] = [VOXELS[k][x * EDGE + z] for z in range(EDGE) for x in range(EDGE)]
def octant_selector():
    sel = np.zeros((EDGE**3, EDGE**3), np.float32)
    for x in range(EDGE):
        for y in range(EDGE):
            for z in range(EDGE):
                o = (x % 2) * 4 + (y % 2) * 2 + z % 2
                u = ((x // 2) * HALF + y // 2) * HALF + z // 2
                sel[(x * EDGE + y) * EDGE + z, o * CUBE + u] = 1
    return sel


FACE = EDGE**2
FACES = 6
RIMS = len(HEADINGS) - FACES


def outer_selector():
    sel = np.zeros((EDGE**3, FACES * FACE + -(-RIMS * EDGE // 128) * 128), np.float32)
    for k in range(len(HEADINGS)):
        first = k * FACE if k < FACES else FACES * FACE + (k - FACES) * EDGE
        for i, v in enumerate(VOXELS[k]):
            sel[v, first + i] = 1
    return sel


def entry_tables(fine):
    wide = 128 // fine
    lanes = np.zeros((2, 128), np.int32)
    for b in range(fine):
        for k in range(len(HEADINGS)):
            face = k < FACES
            lanes[:, b * wide + k] = k * 128 if face else FACES * 128 + (k - FACES) * EDGE, face
    kind = lanes[1]
    earlier = (np.arange(128)[:, None] < np.arange(128)[None]) & (kind[:, None] == kind[None])
    return lanes, earlier.astype(np.float32)


def capacities(fine, owners):
    return -(-fine * FACES // owners), -(-fine * RIMS // owners)


def pair_selector():
    sel = np.zeros((256, 256), np.float32)
    for x in range(2):
        for y in range(8):
            for b in range(2):
                for z in range(8):
                    sel[((x * 8 + y) * 2 + b) * 8 + z, ((b * 2 + x) * 8 + y) * 8 + z] = 1
    return sel


def dot(a, b):
    return lax.dot_general(a, b, (((1,), (0,)), ((), ())), preferred_element_type=F32)


def dot_t(a, b):
    return lax.dot_general(a, b, (((1,), (1,)), ((), ())), preferred_element_type=F32)


def params():
    return pltpu.CompilerParams(vmem_limit_bytes=min(56, 12 + lax.axis_size("brick")) * MIB)


def cost(flops, moved):
    return pl.CostEstimate(flops=flops, bytes_accessed=moved, transcendentals=0)


VM = pltpu.VMEM
SM = pltpu.SMEM


def project_kernel(chans, me_ref, f_ref, sel_ref, w_ref, up_ref, *rest):
    outs, (chunk_ref, pack_ref, part) = rest[:chans], rest[chans:]
    q = w_ref.shape[1]
    rows, vox = f_ref.shape
    fine = rows // q
    x = f_ref[...]
    picked = dot(x, sel_ref[:, :vox]).astype(BF16)
    acc = None
    for o in range(8):
        z = jnp.concatenate(
            [picked[b * q : (b + 1) * q, o * CUBE : (o + 1) * CUBE] for b in range(fine)],
            axis=1,
        )
        term = lax.dot_general(
            w_ref[o], z, (((0,), (0,)), ((), ())), preferred_element_type=F32
        )
        acc = term if acc is None else acc + term
    part[...] = acc
    me = me_ref[0]
    for s in range(chans):
        outs[s][...] = part[pl.ds(pl.multiple_of((me ^ s) * q, q), q), :].astype(BF16)
    got = dot(x, sel_ref[:, vox:])
    low = lax.broadcasted_iota(jnp.int32, (rows, 128), 1) < FACE
    for i in range(FACES // 2):
        pair = got[:, 128 * i : 128 * i + 128]
        turned = pltpu.roll(pair, FACE, 1)
        chunk_ref[2 * i] = jnp.where(low, pair, turned).astype(BF16)
        chunk_ref[2 * i + 1] = jnp.where(low, turned, pair).astype(BF16)
    for i in range(FACES, chunk_ref.shape[0]):
        at = 128 * (i - FACES // 2)
        chunk_ref[i] = got[:, at : at + 128].astype(BF16)
    pack_ref[0:rows] = x
    more = up_ref.shape[0] * up_ref.shape[1] // vox
    for i in range(vox // up_ref.shape[1]):
        part_lanes = slice(i * up_ref.shape[1], (i + 1) * up_ref.shape[1])
        pack_ref[rows : rows + more, part_lanes] = up_ref[i * more : (i + 1) * more]


def project(me, features, down_weight, up_weight, chans):
    fine, q, vox = features.shape
    c_out = down_weight.shape[1]
    lanes = fine * CUBE
    ups = up_weight.reshape(-1, up_weight.shape[2])
    sel = np.concatenate([octant_selector(), outer_selector()], axis=1)
    chunks = (sel.shape[1] - vox) // 128 + FACES // 2
    res = pl.pallas_call(
        lambda *refs: project_kernel(chans, *refs),
        out_shape=[jax.ShapeDtypeStruct((q, lanes), BF16)] * chans
        + [
            jax.ShapeDtypeStruct((chunks, fine * q, 128), BF16),
            jax.ShapeDtypeStruct((fine * q + ups.size // vox, vox), BF16),
        ],
        in_specs=[pl.BlockSpec(memory_space=SM)] + [pl.BlockSpec(memory_space=VM)] * 4,
        out_specs=[pl.BlockSpec(memory_space=VM)] * (chans + 2),
        scratch_shapes=[pltpu.VMEM((c_out, lanes), F32)],
        compiler_params=params(),
        name="project",
    )(
        me,
        features.reshape(fine * q, vox),
        jnp.asarray(sel, BF16),
        jnp.transpose(down_weight, (0, 2, 1)),
        ups,
    )
    return res[:chans], res[chans], res[chans + 1]


def padded(rows, wide):
    return jnp.concatenate([rows, jnp.full((rows.shape[0], wide - rows.shape[1]), -1, jnp.int32)], axis=1)


def choose(
    fine, q, faces, rims, digits, owner_ref, asked_refs, own_ref, lanes_ref, earlier_ref, chunk_ref,
    out_ref, from_ref, table, scalars, sem,
):
    order = xor_order(out_ref.shape[0])
    owners = out_ref.shape[0]
    place = lanes_ref[0:1, :]
    is_face = lanes_ref[1:2, :] == 1
    wide = 128 // fine
    asked = jnp.concatenate(
        [
            jnp.concatenate([padded(ref[:, b, :], wide) for ref in asked_refs], axis=0)
            for b in range(fine)
        ],
        axis=1,
    )
    mask = (asked >= 0) & (lax.div(jnp.maximum(asked, 0), fine) == owner_ref[0])
    rank = dot(mask.astype(F32).astype(BF16), earlier_ref[...])
    slot = jnp.where(is_face, rank, rank + faces)
    code = (lax.rem(jnp.maximum(asked, 0), fine) * 1024 + place + 1).astype(F32)
    lane = lax.broadcasted_iota(jnp.int32, (owners, 128), 1)
    found = jnp.zeros((owners, 128), F32)
    for r in range(faces + rims):
        value = jnp.sum(jnp.where(mask & (slot == r), code, 0.0), axis=1, keepdims=True)
        found = jnp.where(lane == r, value, found)
    table[...] = found.astype(jnp.int32) - 1
    copy = pltpu.make_async_copy(table, scalars, sem)
    copy.start()
    own = jnp.concatenate([padded(own_ref[b : b + 1, :], wide) for b in range(fine)], axis=1)
    own = jnp.broadcast_to(own, (owners, 128))
    theirs = lax.div(jnp.maximum(own, 0), fine)
    mask = (own >= 0) & (theirs == lax.broadcasted_iota(jnp.int32, (owners, 128), 0))
    rank = dot(mask.astype(F32).astype(BF16), earlier_ref[...])
    at = jnp.where(is_face, rank * FACE, rank * EDGE + faces * FACE) + theirs.astype(F32) * 1024.0 + 1.0
    from_ref[...] = jnp.sum(jnp.where(mask, at, 0.0), axis=0, keepdims=True).astype(jnp.int32) - 1
    copy.wait()
    side = lax.broadcasted_iota(jnp.int32, (q, 128), 1)
    half = q // 2

    def one(r_owner, _):
        w = owner_ref[0] ^ (order[r_owner] if owners <= 8 else reversed_bits(r_owner, owners))
        blocks = (out_ref.shape[1] - q) // half
        for block in range(blocks):
            here = jnp.zeros((q, 128), F32)
            for r in range(faces + rims):
                pos = r * FACE if r < faces else faces * FACE + (r - faces) * EDGE
                if pos // 128 != block:
                    continue
                safe = jnp.maximum(scalars[r_owner, r], 0)
                b = lax.shift_right_logical(safe, 10)
                chunk = lax.shift_right_logical(safe, 7) & 7
                got = chunk_ref[chunk, pl.ds(pl.multiple_of(b * q, q), q), :].astype(F32)
                first = pos % 128
                size = FACE
                if r >= faces:
                    got = pltpu.roll(got, (first + 128 - (safe & 127)) & 127, 1)
                    size = EDGE
                here = jnp.where((side >= first) & (side < first + size), got, here)
            at = q + block * half
            for i in range(2):
                part = here[i * half : (i + 1) * half]
                if block == blocks - 1:
                    part = part + digits[i]
                out_ref[w, at : at + half, 128 * i : 128 * i + 128] = part.astype(BF16)
        return 0

    if owners <= 8:
        for w in range(owners):
            one(w, 0)
    else:
        lax.fori_loop(0, owners, one, 0)


def assemble_kernel(chans, asks, fine, faces, rims, owner_ref, links_ref, parents_ref, table_ref, *refs):
    slots, asked_refs, refs = refs[:chans], refs[chans : chans + asks], refs[chans + asks :]
    out_ref = refs[4]
    count, ways = links_ref.shape
    total = slots[0][...].astype(F32)
    for s in slots[1:]:
        total = total + s[...].astype(F32)
    q, lanes = slots[0].shape
    total = total.astype(BF16)
    rows = count * 8
    column, octant = table_ref[0], table_ref[1]
    row = lax.broadcasted_iota(jnp.int32, (rows, 128), 0)
    lane = lax.broadcasted_iota(jnp.int32, (rows, 128), 1)
    code = jnp.zeros((rows, 128), jnp.int32)
    for p in range(count):
        own = row // 8 == p
        for k in range(ways + 1):
            brick = owner_ref[0] * count + p if k == ways else links_ref[p, k]
            code = jnp.where(own & (column == k), jnp.where(brick >= 0, brick * 8 + octant + 1, 0), code)
    for b in range(parents_ref.shape[0]):
        code = jnp.where((row == b) & (lane == META + 27), parents_ref[b] + 1, code)
    high = lax.shift_right_logical(code, 7)
    digits = [high.astype(F32), (code - high * 128).astype(F32)]
    for w in range(out_ref.shape[0]):
        out_ref[w, 0:q, :] = total
    choose(fine, q, faces, rims, digits, owner_ref, asked_refs, *refs)


def assemble(slots, owner, coarse_links, parents, asked, own, chunks, owners):
    q, lanes = slots[0].shape
    count = coarse_links.shape[0]
    fine = parents.shape[0]
    columns, octants = octant_table()
    table = np.full((2, count * 8, 128), -1, np.int32)
    table[0, :, META : META + 27] = np.tile(columns, (count, 1))
    table[1, :, META : META + 27] = np.tile(octants, (count, 1))
    faces, rims = capacities(fine, owners)
    blocks = -(-(faces * FACE + rims * EDGE) // 128)
    assert count * 8 == q // 2 and (faces * FACE + rims * EDGE - 1) % 128 < META
    entries, earlier = entry_tables(fine)
    return pl.pallas_call(
        lambda *refs: assemble_kernel(len(slots), len(asked), fine, faces, rims, *refs),
        out_shape=[
            jax.ShapeDtypeStruct((owners, q + blocks * q // 2, lanes), BF16),
            jax.ShapeDtypeStruct((1, 128), jnp.int32),
        ],
        in_specs=[pl.BlockSpec(memory_space=SM)] * 3 + [pl.BlockSpec(memory_space=VM)] * (len(slots) + len(asked) + 5),
        out_specs=[pl.BlockSpec(memory_space=VM)] * 2,
        scratch_shapes=[
            pltpu.VMEM((owners, 128), jnp.int32),
            pltpu.SMEM((owners, 128), jnp.int32),
            pltpu.SemaphoreType.DMA,
        ],
        compiler_params=params(),
        cost_estimate=cost(1024 * 1024, 12 * 1024 * 1024),
        name="assemble",
    )(
        owner, coarse_links, parents, jnp.asarray(table), *slots,
        *asked, own, jnp.asarray(entries), jnp.asarray(earlier, BF16), chunks,
    )


def partner(x, axis, step, count):
    return lax.ppermute(x, axis, [(i, i ^ step) for i in range(count)])


def exchanged(x, chans):
    return [x] + [partner(x, "chan", s, chans) for s in range(1, chans)]


def relayed(x, chans, meanwhile=lambda: None):
    slots, step, other = {0: x}, chans // 2, None
    while step:
        if step == 1:
            other = meanwhile()
            if other is not None:
                slots, other = lax.optimization_barrier((slots, other))
        for s in list(slots):
            slots[s | step] = partner(slots[s], "chan", step, chans)
        step //= 2
    return [slots[s] for s in range(chans)], other


def reversed_bits(r, count):
    out, bit = 0, 1
    while bit < count:
        out = out * 2 + r % 2
        r = r // 2
        bit *= 2
    return out


def xor_order(count):
    return [reversed_bits(r, count) for r in range(count)]


def gathered(x, owners, between):
    have, step, count = [x], owners // 2, 0
    while step:
        now = jnp.concatenate(have, axis=0) if len(have) > 1 else have[0]
        if count < len(between):
            now = between[count](now)
        have = [now, partner(now, "brick", step, owners)]
        step //= 2
        count += 1
    return have


def halo_kernel(q, base, owner_ref, links_ref, from_ref, recv_ref, out_ref, sel_ref):
    fine = out_ref.shape[0]

    def selectors(block, _):
        sel_ref[block] = jnp.concatenate(line_selectors(fine, owner_ref[0], links_ref, block), axis=0)
        return 0

    if sel_ref.shape[0] == 1:
        selectors(0, 0)
    else:
        lax.fori_loop(0, sel_ref.shape[0], selectors, 0)
    half = q // 2
    lane = lax.broadcasted_iota(jnp.int32, (q, 128), 1)
    for b in range(fine):
        for chunk in range(out_ref.shape[2] // 128):
            here = jnp.zeros((q, 128), F32)
            for k in range(len(HEADINGS)):
                if STARTS[k] // 128 != chunk:
                    continue
                first = STARTS[k] % 128
                last = first + len(VOXELS[k])
                v = from_ref[0, b * (128 // fine) + k]
                safe = jnp.maximum(v, 0)
                w = lax.shift_right_logical(safe, 10)
                block = lax.shift_right_logical(safe, 7) & 7
                row = pl.multiple_of(base + block * half, 16)
                got = jnp.concatenate(
                    [recv_ref[w, pl.ds(row, half), 0:128], recv_ref[w, pl.ds(row, half), 128:256]], axis=0
                ).astype(F32)
                got = pltpu.roll(got, (first + 128 - (safe & 127)) & 127, 1)
                here = jnp.where((lane >= first) & (lane < last) & (v >= 0), got, here)
            out_ref[b, :, chunk * 128 : (chunk + 1) * 128] = here.astype(BF16)


def halo(owner, links, places, recv, base, fine, q, vox):
    return pl.pallas_call(
        lambda *refs: halo_kernel(q, base, *refs),
        out_shape=[
            jax.ShapeDtypeStruct((fine, q, vox), BF16),
            jax.ShapeDtypeStruct((recv.shape[0] * fine // NBLK, 9 * 8 * fine, 128), BF16),
        ],
        in_specs=[pl.BlockSpec(memory_space=SM)] * 3 + [pl.BlockSpec(memory_space=VM)],
        out_specs=[pl.BlockSpec(memory_space=VM)] * 2,
        compiler_params=params(),
        name="halo",
    )(owner, links, places, recv)


def axis_places(u):
    found = [(0, 1 + u)]
    if u == 0:
        found.append((1, HALF + 1))
    if u == HALF - 1:
        found.append((-1, 0))
    return found


def bias_column(row):
    n = row.shape[1]
    square = jnp.broadcast_to(row, (n, n))
    on = lax.broadcasted_iota(jnp.int32, (n, n), 0) == lax.broadcasted_iota(jnp.int32, (n, n), 1)
    return jnp.sum(jnp.where(on, square, 0.0), axis=1, keepdims=True)


LINES = [
    (ux, uy, a, b)
    for ux in range(HALF)
    for uy in range(HALF)
    for a in axis_places(ux)
    for b in axis_places(uy)
]


def line_selectors(fine, owner, links_ref, block):
    lane = lax.broadcasted_iota(jnp.int32, (8, 128), 1)
    row = lax.broadcasted_iota(jnp.int32, (8, 128), 0)
    made = []
    for dx in (-1, 0, 1):
        for dy in (-1, 0, 1):
            tiles = []
            for b in range(fine):
                at = []
                for dz in (-1, 0, 1):
                    k = HEADING_INDEX[(dx, dy, dz)]
                    n = owner * fine + b if k == len(HEADINGS) else links_ref[b, k]
                    n = n - block * NBLK
                    at.append(jnp.where((n >= 0) & (n < NBLK), n, -1024))
                want = jnp.where(row == 0, at[0] + (HALF - 1) * NBLK, at[1] + (row - 1) * NBLK)
                want = jnp.where(row == HALF + 1, at[2], want)
                tiles.append(((lane == want) & (row < HALF + 2)).astype(F32))
            made.append(jnp.concatenate(tiles, axis=0).astype(BF16))
    return made


def line_spreader(fine, rows):
    wide = 8 * fine
    lines = 128 // wide
    sel = np.zeros((lines * rows, 128), np.float32)
    for i in range(lines):
        for b in range(fine):
            first = i * wide + b * 8
            for z in range(EDGE):
                sel[i * rows + b * EDGE + z, first + 1 + z // 2] = 1
            for side in range(2):
                sel[i * rows + wide + 2 * b + side, first + side * (HALF + 1)] = 1
    return sel


def coarse_kernel(chans, codes, me_ref, picker_ref, *refs):
    slots, refs = refs[:chans], refs[chans:]
    recv_ref, w_ref, bias_ref, out_ref, proj_ref, rows_ref, sel_ref, nb_ref, parent_ref, table_ref = refs
    owners, q, lanes = slots[0].shape
    me = me_ref[0]
    fine = lanes // CUBE
    total = owners * fine

    def spread(w, _):
        block = jnp.concatenate([proj_ref[c, w] for c in range(chans)], axis=0)
        turned = block.astype(F32).T
        for b in range(fine):
            rows_ref[pl.ds(w * fine + b, CUBE, stride=total), :] = turned[b * CUBE : (b + 1) * CUBE]
        return 0

    @pl.when(pl.program_id(0) == 0)
    def _():
        for w in range(owners):
            digits = recv_ref[w]
            table_ref[w * codes : (w + 1) * codes, :] = digits
            digits = digits.astype(F32)
            value = digits[:, 0:128] * 128.0 + digits[:, 128:256] - 1.0
            parent_ref[w * fine : (w + 1) * fine, :] = jnp.broadcast_to(value[0:fine, META + 27 : META + 28], (fine, 128))
        for s in range(chans):
            proj_ref[me ^ s] = slots[s][...]
        if owners <= 8:
            for w in range(owners):
                spread(w, 0)
        else:
            lax.fori_loop(0, owners, spread, 0)

    mine = parent_ref[pl.ds(pl.program_id(0) * NBLK, NBLK), :]
    row = lax.broadcasted_iota(jnp.int32, (NBLK, table_ref.shape[0]), 1).astype(F32)
    own = (mine[:, 0:1] == row).astype(F32).astype(BF16)
    digits = dot(own, table_ref[...])
    target = digits[:, 0:128] * 128.0 + digits[:, 128:256] - 1.0
    on = lax.broadcasted_iota(jnp.int32, (total, total), 0) == lax.broadcasted_iota(jnp.int32, (total, total), 1)
    parents = jnp.sum(jnp.where(on, parent_ref[:, 0:1], 0.0), axis=0, keepdims=True)
    for d in range(27):
        sel_ref[d * NBLK : (d + 1) * NBLK, :] = (target[:, META + d : META + d + 1] == parents).astype(F32).astype(BF16)
    for ux in range(HALF):
        for uy in range(HALF):
            for uz in range(HALF):
                places = [
                    (9 * (a[0] + 1) + 3 * (b[0] + 1) + c[0] + 1, a[1], b[1], c[1])
                    for a in axis_places(ux)
                    for b in axis_places(uy)
                    for c in axis_places(uz)
                ]
                u = (ux * HALF + uy) * HALF + uz
                source = rows_ref[u * total : (u + 1) * total, :].astype(BF16)
                picker = jnp.concatenate(
                    [sel_ref[d * NBLK : (d + 1) * NBLK, :] for d, _, _, _ in places], axis=0
                )
                got = dot(picker, source).astype(BF16)
                for i, (_, x, y, z) in enumerate(places):
                    nb_ref[x, y, z] = got[i * NBLK : (i + 1) * NBLK]
    span = HALF + 2
    size = span * HALF * HALF * NBLK
    acc = conv_rows(
        w_ref,
        lambda a2, a3: nb_ref[:, a2 : a2 + HALF, a3 : a3 + HALF].reshape(size, nb_ref.shape[4]),
        2,
    )
    step = HALF * HALF * NBLK
    n = HALF * step
    res = acc[0:q, 0:n] + acc[q : 2 * q, step : step + n] + acc[2 * q : 3 * q, 2 * step : 2 * step + n]
    res = jnp.maximum(res + bias_column(bias_ref[...]), 0.0).astype(BF16)
    size = picker_ref.shape[1] // 9
    pickers = [picker_ref[0, i * size : (i + 1) * size, :] for i in range(9)]
    found = []
    for ux in range(HALF):
        for uy in range(HALF):
            col = (ux * HALF + uy) * 128
            mine = [pickers[3 * (a[0] + 1) + b[0] + 1] for x, y, a, b in LINES if (x, y) == (ux, uy)]
            found.append(dot_t(res[:, col : col + 128], jnp.concatenate(mine, axis=0)))
    found = jnp.concatenate(found, axis=1).astype(BF16)
    if pl.num_programs(0) == 1:
        out_ref[...] = found
    else:
        before = out_ref[...]
        out_ref[...] = jnp.where(pl.program_id(0) == 0, jnp.zeros_like(before), before) + found


def conv_rows(w_ref, rows_of, together):
    taps = [(a2, a3) for a2 in range(3) for a3 in range(3)]
    acc = None
    for i in range(0, 9, together):
        some = taps[i : i + together]
        lhs = jnp.concatenate(
            [
                jnp.concatenate([w_ref[9 * a1 + 3 * a2 + a3] for a1 in range(3)], axis=0)
                for a2, a3 in some
            ],
            axis=1,
        )
        rhs = jnp.concatenate([rows_of(a2, a3) for a2, a3 in some], axis=1)
        term = dot_t(lhs, rhs)
        acc = term if acc is None else acc + term
    return acc


def coarse(me, pickers, slots, recv, codes, weight, bias):
    chans = len(slots)
    owners, q, lanes = slots[0].shape
    fine = lanes // CUBE
    total = owners * fine
    blocks = total // NBLK
    c_in = weight.shape[2]
    whole = lambda a: pl.BlockSpec(a.shape, lambda i: (0,) * a.ndim)
    return pl.pallas_call(
        lambda *refs: coarse_kernel(chans, codes, *refs),
        out_shape=jax.ShapeDtypeStruct((q, len(LINES) * 8 * fine), BF16),
        grid=(blocks,),
        in_specs=[pl.BlockSpec(memory_space=SM), pl.BlockSpec((1,) + pickers.shape[1:], lambda i: (i, 0, 0))]
        + [whole(a) for a in slots]
        + [
            pl.BlockSpec((owners, codes, recv.shape[2]), lambda i: (0, recv.shape[1] // codes - 1, 0)),
            whole(weight),
            whole(bias),
        ],
        out_specs=pl.BlockSpec((q, len(LINES) * 8 * fine), lambda i: (0, 0)),
        scratch_shapes=[
            pltpu.VMEM((chans, owners, q, lanes), BF16),
            pltpu.VMEM((CUBE * total, c_in), F32),
            pltpu.VMEM((27 * NBLK, total), BF16),
            pltpu.VMEM((HALF + 2, HALF + 2, HALF + 2, NBLK, c_in), BF16),
            pltpu.VMEM((total, 128), F32),
            pltpu.VMEM((owners * codes, 256), BF16),
        ],
        compiler_params=params(),
        cost_estimate=cost(2 * 27 * c_in * q * CUBE * total, 2 * 1024 * 1024),
        name="coarse",
    )(me, pickers, *slots, recv, weight, bias)


def frame_axis(f):
    if f == 0:
        return -1, EDGE - 1
    if f == FRAME - 1:
        return 1, 0
    return 0, f - 1


def frame_kernel(chans, me_ref, *refs):
    packs, halos, refs = refs[:chans], refs[chans : 2 * chans], refs[2 * chans :]
    ff_ref, up_ref, both, inner, outer, plane = refs
    fine, q, vox = halos[0].shape
    me = me_ref[0]
    for s in range(chans):
        at = pl.ds(pl.multiple_of((me ^ s) * q, q), q)
        for b in range(fine):
            both[0, b, at, :] = packs[s][b * q : (b + 1) * q, :]
            both[1, b, at, :] = halos[s][b]
        for o in range(8):
            row = (fine + o % 2) * q
            up_ref[o, at, :] = packs[s][row : row + q, o // 2 * 128 : o // 2 * 128 + 128]
    for b in range(fine):
        inner[b] = both[0, b].astype(F32).T
        outer[b] = both[1, b].astype(F32).T
    for b in range(fine):
        for s in range(2):
            dz = 2 * s - 1
            row = 2 * b + s
            for fx in range(FRAME):
                dx, vx = frame_axis(fx)
                start = STARTS[HEADING_INDEX[(dx, 0, dz)]] + (0 if dx else vx * EDGE)
                plane[pl.ds((fx * FRAME + 1) * 8 + row, EDGE, stride=8), :] = outer[b, start : start + EDGE, :]
            for fy in (0, FRAME - 1):
                dy = frame_axis(fy)[0]
                start = STARTS[HEADING_INDEX[(0, dy, dz)]]
                plane[pl.ds((FRAME + fy) * 8 + row, EDGE, stride=8 * FRAME), :] = outer[b, start : start + EDGE, :]
                for fx in (0, FRAME - 1):
                    start = STARTS[HEADING_INDEX[(frame_axis(fx)[0], dy, dz)]]
                    plane[pl.ds((fx * FRAME + fy) * 8 + row, 1), :] = outer[b, start : start + 1, :]
    for fx in range(FRAME):
        for fy in range(FRAME):
            dx, vx = frame_axis(fx)
            dy, vy = frame_axis(fy)
            at = ((1 - fx % 2) * 2 + 1 - fy % 2) * 25 + (fx // 2) * 5 + fy // 2
            tiles = []
            for b in range(fine):
                if dx == 0 and dy == 0:
                    start = (vx * EDGE + vy) * EDGE
                    tiles.append(inner[b, start : start + EDGE, :])
                else:
                    start = STARTS[HEADING_INDEX[(dx, dy, 0)]]
                    if dx == 0:
                        tiles.append(outer[b, pl.ds(start + vx, EDGE, stride=EDGE), :])
                    else:
                        start += 0 if dy else vy * EDGE
                        tiles.append(outer[b, start : start + EDGE, :])
            tiles.append(plane[(fx * FRAME + fy) * 8 : (fx * FRAME + fy) * 8 + 8, :])
            tiles.append(jnp.zeros((8, plane.shape[1]), F32))
            ff_ref[at] = jnp.concatenate(tiles, axis=0).astype(BF16)


def frames(me, packs, halos):
    chans = len(packs)
    fine, q, vox = halos[0].shape
    rows = 8 * fine + 16
    c_all = chans * q
    return pl.pallas_call(
        lambda *refs: frame_kernel(chans, *refs),
        out_shape=[
            jax.ShapeDtypeStruct((FRAME * FRAME, rows, c_all), BF16),
            jax.ShapeDtypeStruct((8, c_all, c_all), BF16),
        ],
        in_specs=[pl.BlockSpec(memory_space=SM)] + [pl.BlockSpec(memory_space=VM)] * (2 * chans),
        out_specs=[pl.BlockSpec(memory_space=VM)] * 2,
        scratch_shapes=[
            pltpu.VMEM((2, fine, c_all, vox), BF16),
            pltpu.VMEM((fine, vox, c_all), F32),
            pltpu.VMEM((fine, vox, c_all), F32),
            pltpu.VMEM((FRAME * FRAME * 8, c_all), F32),
        ],
        compiler_params=params(),
        name="frames",
    )(me, *packs, *halos)


def fine_kernel(chans, me_ref, *refs):
    slots, refs = refs[:chans], refs[chans:]
    ff_ref, sel_ref, up_ref, w_ref, bias_ref, pair_ref, out_ref, co_ref, cr, g3 = refs
    q = slots[0].shape[0]
    c_all = chans * q
    for s in range(chans):
        co_ref[me_ref[0] ^ s] = slots[s][...]
    fine = out_ref.shape[0]
    rows = ff_ref.shape[1]
    lines = 128 // (8 * fine)
    for i in range(0, len(LINES), lines):
        col = i * 8 * fine
        source = jnp.concatenate([co_ref[c, :, col : col + 128] for c in range(chans)], axis=0)
        got = dot_t(sel_ref[...], source).astype(BF16)
        for j, (_, _, x, y) in enumerate(LINES[i : i + lines]):
            cr[x[1], y[1]] = got[j * rows : (j + 1) * rows]
    r = lax.broadcasted_iota(jnp.int32, (rows, c_all), 0)
    odd = (r % 2 == 1) ^ (r >= 8 * fine)
    sub = lax.broadcasted_iota(jnp.int32, (5, 8, c_all), 1)
    for px in range(2):
        for py in range(2):
            lift = jnp.concatenate([up_ref[4 * px + 2 * py], up_ref[4 * px + 2 * py + 1]], axis=0)
            for i in range(5):
                x = i + 1 - px
                src = cr[x, 1 - py : 6 - py].reshape(5 * rows, c_all)
                both = dot_t(src, lift).reshape(5, rows, 2 * c_all)
                up = jnp.where(odd[None], both[:, :, c_all:], both[:, :, :c_all])
                at = (px * 2 + py) * 25 + i * 5
                merged = (ff_ref[at : at + 5].astype(F32) + up).astype(BF16).astype(F32)
                fx = 2 * i + 1 - px
                plane = merged[:, 8 * fine : 8 * fine + 8, :]
                for pair in range(fine // 2):
                    made = [[], [], []]
                    for h in range(2):
                        b = 2 * pair + h
                        mid = merged[:, 8 * b : 8 * b + 8, :]
                        made[0].append(
                            jnp.where(
                                sub == 0,
                                pltpu.roll(plane, (8 - 2 * b) % 8, 1),
                                pltpu.roll(mid, 1, 1),
                            )
                        )
                        made[1].append(mid)
                        made[2].append(
                            jnp.where(
                                sub == 7,
                                pltpu.roll(plane, 7 - (2 * b + 1), 1),
                                pltpu.roll(mid, 7, 1),
                            )
                        )
                    for a3 in range(3):
                        tile = jnp.concatenate(made[a3], axis=1).astype(BF16)
                        for j in range(5):
                            g3[a3, pair, fx, 2 * j + 1 - py] = tile[j]
    step = EDGE * 2 * EDGE
    n = EDGE * step
    bias = bias_column(bias_ref[...])
    for pair in range(fine // 2):
        acc = conv_rows(
            w_ref,
            lambda a2, a3: g3[a3, pair, :, a2 : a2 + EDGE].reshape(FRAME * step, c_all),
            9,
        )
        res = acc[0:q, 0:n] + acc[q : 2 * q, step : step + n] + acc[2 * q : 3 * q, 2 * step : 2 * step + n]
        res = jnp.maximum(res + bias, 0.0).astype(BF16)
        for h in range(n // 256):
            turned = dot(res[:, 256 * h : 256 * h + 256], pair_ref[...]).astype(BF16)
            for b in range(2):
                out_ref[2 * pair + b, :, 128 * h : 128 * h + 128] = turned[:, 128 * b : 128 * b + 128]


def refine(me, slots, ff, up_weight, weight, bias):
    chans = len(slots)
    q, wide = slots[0].shape
    rows = ff.shape[1]
    fine = (rows - 16) // 8
    c_all = chans * q
    return pl.pallas_call(
        lambda *refs: fine_kernel(chans, *refs),
        out_shape=jax.ShapeDtypeStruct((fine, q, EDGE**3), BF16),
        in_specs=[pl.BlockSpec(memory_space=SM)] + [pl.BlockSpec(memory_space=VM)] * (chans + 6),
        out_specs=pl.BlockSpec(memory_space=VM),
        scratch_shapes=[
            pltpu.VMEM((chans, q, wide), BF16),
            pltpu.VMEM((HALF + 2, HALF + 2, rows, c_all), BF16),
            pltpu.VMEM((3, fine // 2, FRAME, FRAME, 2 * EDGE, c_all), BF16),
        ],
        compiler_params=params(),
        cost_estimate=cost(2 * 27 * c_all * q * fine * EDGE**3, 4 * 1024 * 1024),
        name="refine",
    )(me, *slots, ff, jnp.asarray(line_spreader(fine, rows), BF16), up_weight, weight, bias, jnp.asarray(pair_selector(), BF16))


def octant_table():
    columns = np.zeros((8, 27), np.int32)
    octants = np.zeros((8, 27), np.int32)
    for o in range(8):
        bits = (o >> 2 & 1, o >> 1 & 1, o & 1)
        for d in range(27):
            go = (d // 9 - 1, d // 3 % 3 - 1, d % 3 - 1)
            cross, land = [], []
            for bit, g in zip(bits, go):
                t = bit + g
                cross.append(-1 if t < 0 else 1 if t > 1 else 0)
                land.append(t % 2)
            columns[o, d] = HEADING_INDEX[tuple(cross)]
            octants[o, d] = land[0] * 4 + land[1] * 2 + land[2]
    return columns, octants


def per_device(
    features,
    fine_links,
    coarse_links,
    parents,
    down_weight,
    coarse_weight,
    up_weight,
    fine_weight,
    coarse_bias,
    fine_bias,
):
    owners = lax.axis_size("brick")
    chans = lax.axis_size("chan")
    owner = lax.axis_index("brick").astype(jnp.int32)
    me = lax.axis_index("chan").astype(jnp.int32)
    fine, q, vox = features.shape
    parts, chunks, packed = project(me[None], features, down_weight, up_weight, chans)
    done = {}

    def projected(now):
        now, done["parts"] = lax.optimization_barrier((now, parts))
        return now

    def reduced(now):
        blocks = done["parts"]
        arrived = [blocks[0]] + [partner(blocks[s], "chan", s, chans) for s in range(1, chans)]
        now, arrived[1] = lax.optimization_barrier((now, arrived[1]))
        done["arrived"] = arrived
        return now

    asked = gathered(fine_links[None], owners, [lambda now: now, projected, reduced])
    arrived = done["arrived"]
    codes = 8 * coarse_links.shape[0]
    sending, places = assemble(arrived, owner[None], coarse_links, parents, asked, fine_links, chunks, owners)
    recv = lax.all_to_all(sending, "brick", split_axis=0, concat_axis=0, tiled=True)
    packs, _ = relayed(packed, chans)
    recv, packs = lax.optimization_barrier((recv, packs))
    slots, (around, pickers) = relayed(
        recv[:, :q],
        chans,
        lambda: halo(owner[None], fine_links, places, recv, q, fine, q, vox),
    )
    halos = exchanged(around, chans)
    co = coarse(me[None], pickers, slots, recv, codes, coarse_weight, coarse_bias[None])
    cos, (ff, up_all) = relayed(co, chans, lambda: frames(me[None], packs, halos))
    return refine(me[None], cos, ff, up_all, fine_weight, fine_bias[None])


def solution(mesh):
    in_specs = (
        P("brick", "chan", None),
        P("brick", None),
        P("brick", None),
        P("brick"),
        P(None, None, "chan"),
        P(None, "chan", None),
        P(None, "chan", None),
        P(None, "chan", None),
        P("chan"),
        P("chan"),
    )
    return jax.shard_map(
        per_device,
        mesh=mesh,
        in_specs=in_specs,
        out_specs=P("brick", "chan", None),
        check_vma=False,
    )
```
